32 devices in a mesh: dom: 16 (over z, y, x), feat: 2 (over core).
Axes of the slice: x: 2, y: 2, z: 4, core: 2. Of those that a mesh axis runs over, the one named last changes fastest.
Arguments:
- features: bfloat16 [32768, 100], P('dom', 'feat'), may hold values from -6 to 6
- local_mask: int32 [32768, 2048], P('dom'), may hold values 0 or 1
- halo_mask: int32 [32768, 128], P('dom'), may hold values 0 or 1
- send_rows: int32 [16, 16, 8], P('dom'), may hold values from 0 to 2047
- labels: int32 [32768], P('dom'), may hold values from 0 to 46
- label_mask: int32 [32768], P('dom'), may hold values from 0 to 1
- master: float32 [2, 103680], P('feat', 'dom')
- first_moment: float32 [2, 103680], P('feat', 'dom'), may hold values from -0.00390625 to 0.00390625
- second_moment: float32 [2, 103680], P('feat', 'dom'), may hold values from 6.866455e-09 to 2.746582e-08
Outputs:
- loss_sum: float32 [], replicated
- label_count: float32 [], replicated
- new_master: float32 [2, 103680], P('feat', 'dom')
- new_first: float32 [2, 103680], P('feat', 'dom')
- new_second: float32 [2, 103680], P('feat', 'dom')
The draws below stay inside these ranges and needn't reach their ends.
All inputs are finite; a program needn't handle non-finite values. No bound on the sum of `local_mask` or of `halo_mask` on one device may be relied on, other than what follows from the above.
Results may differ from the reference program's by a relative error of at most 0.0005.
The reference program's roundings to bfloat16 on the way count: a program that leaves them out, or rounds other values in their place, can miss the bound.
Values may be sent and summed in bfloat16 or wider, within the bound.
A program may use at most 128 MiB of HBM per device.

```python
import math
import jax
import jax.numpy as jnp
from jax import lax

FIN = 100
HID = 256
CLS = 47
NODE_DEV = 2048
HB = 8
STEP = 10
NODES = 32768
HALO = 128
SLICE = 103680
N_DOM = 16
N_FEAT = 2


def draw_label_mask(key, part):
    key = jax.random.fold_in(key, 3)
    groups = NODES // NODE_DEV
    partition = jnp.arange(NODES, dtype=jnp.int32) // NODE_DEV
    thresholds = 200 + 400 * partition // max(groups - 1, 1)
    rolled = jax.random.randint(key, (NODES,), 0, 1000)
    return (rolled < thresholds).astype(jnp.int32)


def draw_master(key, part):
    key = jax.random.fold_in(key, 7)
    inner_width = FIN // N_FEAT
    hidden_width = HID // N_FEAT
    edge_one = 2 * inner_width * HID
    edge_two = edge_one + 2 * hidden_width * HID
    edge_three = edge_two + 2 * hidden_width * CLS
    drawn = jax.random.normal(key, (N_FEAT, SLICE), jnp.float32)
    column = jnp.arange(SLICE)
    factor = jnp.where(column < edge_one, (2.0 * FIN) ** (-0.5), jnp.where(column < edge_two, (2.0 * HID) ** (-0.5), jnp.where(column < edge_three, 3.0 * (2.0 * HID) ** (-0.5), 0.1)))
    is_gain = (column >= edge_three) & ((column - edge_three) // hidden_width % 2 == 0)
    offset = jnp.where(is_gain, 1.0, 0.0)
    return (drawn * factor[None, :] + offset[None, :]).astype(jnp.float32)


def place_ends(values, own_key, least, high):
    longest = values.shape.index(max(values.shape))
    spots = []
    for shift in (0, 1):
        where = [jax.random.randint(jax.random.fold_in(own_key, axis), (), 0, length) for axis, length in enumerate(values.shape)]
        where[longest] = (where[longest] + shift) % values.shape[longest]
        spots.append(tuple(where))
    return values.at[spots[0]].set(least).at[spots[1]].set(high)


def block_scale(key, shape, cuts, smallest, largest):
    loudness, own = 1.0, jax.random.fold_in(key, 6)
    for position, shards_of in cuts:
        steps = jnp.exp(jax.random.uniform(jax.random.fold_in(own, position), (shards_of,), jnp.float32, smallest / len(cuts), largest / len(cuts)))
        loudness = loudness * jnp.repeat(steps, shape[position] // shards_of).reshape([-1 if axis == position else 1 for axis in range(len(shape))])
    return loudness


def bell_draw(rng, extent, deviation, reach, split=(), kind=jnp.bfloat16):
    result = deviation * jax.random.normal(rng, extent, jnp.float32)
    if split:
        result = result * block_scale(rng, extent, split, -0.22, 0.18)
    return jnp.clip(result, -reach, reach).astype(kind)


def setup_inputs(seed: int = 0) -> dict:
    seeds = jax.random.split(jax.random.key(seed), 10)
    return {
        "features": bell_draw(seeds[0], (NODES, FIN), 1.0, 6.0, ((0, 16), (1, 2))),
        "local_mask": place_ends((jax.random.randint(seeds[1], (NODES, NODE_DEV), 0, 32) < 1).astype(jnp.int32), jax.random.fold_in(seeds[1], 1), 0, 1),
        "halo_mask": place_ends((jax.random.randint(seeds[2], (NODES, HALO), 0, 64) < 1).astype(jnp.int32), jax.random.fold_in(seeds[2], 1), 0, 1),
        "send_rows": place_ends(jax.random.randint(seeds[3], (N_DOM, N_DOM, HB), 0, NODE_DEV), jax.random.fold_in(seeds[3], 1), 0, NODE_DEV - 1).astype(jnp.int32),
        "labels": place_ends(jax.random.randint(seeds[4], (NODES,), 0, CLS), jax.random.fold_in(seeds[4], 1), 0, CLS - 1).astype(jnp.int32),
        "label_mask": draw_label_mask(jax.random.fold_in(seeds[9], 71), 0),
        "master": draw_master(jax.random.fold_in(seeds[9], 71), 0),
        "first_moment": bell_draw(seeds[7], (N_FEAT, SLICE), (0.052 * NODES ** -0.5), 0.00390625, ((0, 2), (1, 16)), jnp.float32),
        "second_moment": jnp.clip(jnp.exp(math.log(2.7465819840699623e-08) - 1.3862944 * jax.random.uniform(seeds[8], (N_FEAT, SLICE), jnp.float32) ** block_scale(seeds[8], (N_FEAT, SLICE), ((0, 2), (1, 16)), -0.2, 0.2)), 6.866454960174906e-09, 2.7465819840699623e-08),
    }


EPSILON = 1e-05
LEARN_RATE = 0.02
DECAY_ONE = 0.9
DECAY_TWO = 0.999
ADAM_EPS = 1e-08
WEIGHT_DECAY = 0.01

@jax.custom_vjp
def low(v):
    return lax.optimization_barrier(v.astype(jnp.bfloat16)).astype(jnp.float32)

@jax.custom_vjp
def low_back(v):
    return v

def low_keep(v):
    return (low(v), None)

def low_pass(kept, grad):
    return (grad,)

def back_keep(v):
    return (v, None)

def back_low(kept, grad):
    return (low(grad),)
low.defvjp(low_keep, low_pass)
low_back.defvjp(back_keep, back_low)

def matmul(matrix_a, matrix_b):
    return jnp.dot(matrix_a, matrix_b, precision=lax.Precision.HIGHEST, preferred_element_type=jnp.float32)

def batched(matrix_a, matrix_b):
    return jnp.einsum('pij,pjf->pif', matrix_a, matrix_b, precision=lax.Precision.HIGHEST, preferred_element_type=jnp.float32)

def unpack(flat_params):
    inner_width = FIN // N_FEAT
    hidden_width = HID // N_FEAT
    edge_one = 2 * inner_width * HID
    edge_two = edge_one + 2 * hidden_width * HID
    edge_three = edge_two + 2 * hidden_width * CLS
    layer_one = flat_params[:, :edge_one].reshape(N_FEAT, 2, inner_width, HID)
    layer_two = flat_params[:, edge_one:edge_two].reshape(N_FEAT, 2, hidden_width, HID)
    head_part = flat_params[:, edge_two:edge_three].reshape(N_FEAT, 2, hidden_width, CLS)
    norm_part = flat_params[:, edge_three:].reshape(N_FEAT, 4, hidden_width)
    matrices = [(layer_one[:, 0].reshape(FIN, HID), layer_one[:, 1].reshape(FIN, HID)), (layer_two[:, 0].reshape(HID, HID), layer_two[:, 1].reshape(HID, HID)), (head_part[:, 0].reshape(HID, CLS), head_part[:, 1].reshape(HID, CLS))]
    norm_params = norm_part.transpose(1, 0, 2).reshape(4, HID)
    return (matrices, norm_params)

def gather_halo(states, send_index):
    blocks = states.reshape(N_DOM, NODE_DEV, -1)
    picked = jax.vmap(lambda source_block, source_index: source_block[source_index])(blocks, send_index)
    return picked.transpose(1, 0, 2, 3).reshape(N_DOM, HALO, -1)

def aggregate(states, local_adj, halo_adj, inverse, send_index):
    halo_feats = low_back(gather_halo(states, send_index))
    blocks = states.reshape(N_DOM, NODE_DEV, -1)
    summed = batched(local_adj, blocks) + batched(halo_adj, halo_feats)
    summed = low_back(summed.reshape(NODES, -1))
    return low(summed * inverse[:, None])

def forward(flat_params, inputs, local_adj, halo_adj, inverse, send_index, labels, weight_mask, label_count):
    matrices, norm_params = unpack(low(flat_params))
    states = inputs
    for number in range(3):
        self_weight, neigh_weight = matrices[number]
        aggregated = aggregate(states, local_adj, halo_adj, inverse, send_index)
        mixed = low_back(matmul(states, self_weight) + matmul(aggregated, neigh_weight))
        if number < 2:
            centre = mixed - lax.optimization_barrier(jnp.mean(mixed, axis=1, keepdims=True))
            variance = lax.optimization_barrier(jnp.mean(centre * centre, axis=1, keepdims=True))
            normed = centre * lax.rsqrt(variance + EPSILON)
            shifted = normed * norm_params[2 * number] + norm_params[2 * number + 1]
            states = low(jax.nn.gelu(shifted))
    log_total = jax.nn.logsumexp(mixed, axis=1)
    picked = jnp.take_along_axis(mixed, labels[:, None], axis=1)[:, 0]
    loss_sum = jnp.sum((log_total - picked) * weight_mask)
    return (loss_sum / label_count, loss_sum)

def reference(features, local_mask, halo_mask, send_rows, labels, label_mask, master, first_moment, second_moment):
    local_adj = local_mask.astype(jnp.float32).reshape(N_DOM, NODE_DEV, NODE_DEV)
    halo_adj = halo_mask.astype(jnp.float32).reshape(N_DOM, NODE_DEV, HALO)
    degree = lax.optimization_barrier(jnp.sum(local_mask, axis=1)) + lax.optimization_barrier(jnp.sum(halo_mask, axis=1))
    inverse = 1.0 / jnp.maximum(degree, 1).astype(jnp.float32)
    weight_mask = label_mask.astype(jnp.float32)
    label_count = jnp.sum(weight_mask)
    inputs = features.astype(jnp.float32)

    def objective(flat_params):
        return forward(flat_params, inputs, local_adj, halo_adj, inverse, send_rows, labels, weight_mask, label_count)
    mean_loss, pullback, loss_sum = jax.vjp(objective, master, has_aux=True)
    gradient = pullback(jnp.ones_like(mean_loss))[0]
    new_first = DECAY_ONE * first_moment + (1.0 - DECAY_ONE) * gradient
    new_second = DECAY_TWO * second_moment + (1.0 - DECAY_TWO) * gradient * gradient
    first_hat = new_first / (1.0 - DECAY_ONE ** STEP)
    second_hat = new_second / (1.0 - DECAY_TWO ** STEP)
    new_master = master - LEARN_RATE * (first_hat / (jnp.sqrt(second_hat) + ADAM_EPS) + WEIGHT_DECAY * master)
    return (loss_sum, label_count, new_master, new_first, new_second)
```

```python
import functools

import jax
import jax.numpy as jnp
from jax import lax
from jax.experimental import pallas as pl
from jax.experimental.pallas import tpu as pltpu
from jax.sharding import PartitionSpec as P

HID = 256
CLS = 47
STEP = 10
EPSILON = 1e-05
LEARN_RATE = 0.02
DECAY_ONE = 0.9
DECAY_TWO = 0.999
ADAM_EPS = 1e-08
WEIGHT_DECAY = 0.01

MESH = pl.DeviceIdType.MESH
BF = jnp.bfloat16
F32 = jnp.float32
LANES = 128
CLS_PAD = 64
FEAT_PAD = 64
HALF_HID = HID // 2
ROW_ONE = 2 * FEAT_PAD
ROW_TWO = ROW_ONE + 2 * HALF_HID
HEAD_ROWS = 2 * HALF_HID * CLS // HID
ROW_NORM = ROW_TWO + 48
ROWS_PAD = ROW_NORM + 16
GELU_A = 0.7978845608028654
GELU_B = 0.044715


def dot(a, b, ca=1, cb=0, precision=None):
    return lax.dot_general(
        a, b, (((ca,), (cb,)), ((), ())), precision=precision, preferred_element_type=F32
    )


def iota(shape, axis):
    return lax.broadcasted_iota(jnp.int32, shape, axis)


def gelu(x):
    t = jnp.tanh(GELU_A * (x + GELU_B * (x * x * x)))
    return 0.5 * x * (1.0 + t)


def gelu_grad(x):
    xx = x * x
    t = jnp.tanh(GELU_A * (x + GELU_B * (xx * x)))
    return 0.5 * (1.0 + t) + 0.5 * x * (1.0 - t * t) * (GELU_A + (3.0 * GELU_A * GELU_B) * xx)


def roll_rows(x, amount, right):
    for bit in range(8):
        step = 1 << bit
        moved = pltpu.roll(x, step if right else HID - step, 1)
        x = jnp.where((amount & step) != 0, moved, x)
    return x


def loop(n, body):
    def step(i, carry):
        body(i)
        return carry

    lax.fori_loop(0, n, step, 0)


def kernel(
    cfg,
    x_in, lm_in, hm_in, send_in, label_in, lmask_in, master_in,
    grad_out, scalar_out,
    a_stage, b_stage, h_stage, x_stage, x_pad,
    a_rows, b_x, hmt, sel, xs, hs, gs_all, agg_ref, agg_zero,
    mixed, normed, scale_inv, inv_ref, halo_tx, halo_rx,
    flat_t, par_tx, par_rx, wmat, wmat_t, norm_col, head_ws, head_wn, head_ws_t, head_wn_t,
    g_low, grad_a, grad_b, grad_flat, pair_rx, win_tx, win_rx, dw_head, acc_gain, acc_bias, loss_ref,
    local_sem, pair_send, pair_recv, halo_send, halo_recv, par_send, par_recv, win_send, win_recv,
):
    n_dom, nodes, half, halo, shard, fin = (
        cfg["n_dom"], cfg["nodes"], cfg["half"], cfg["halo"], cfg["shard"], cfg["fin"]
    )
    win, par_rows, rows_all = cfg["win"], cfg["par_rows"], cfg["rows_all"]
    me, f = lax.axis_index("dom"), lax.axis_index("feat")
    other = 1 - f
    own = pl.multiple_of(f * half, half)
    far = pl.multiple_of(other * half, half)
    own_cols, far_cols = pl.ds(own, half), pl.ds(far, half)

    chunk = 128
    n_chunk = half // chunk
    x_copy = pltpu.make_async_copy(x_in, x_stage, local_sem.at[0])
    x_copy.start()
    h_rows = cfg["h_rows"]

    def h_copy(i):
        return pltpu.make_async_copy(
            hm_in.at[pl.ds(i * h_rows, h_rows), :], h_stage, local_sem.at[1]
        )

    h_copy(0).start()

    def a_copy(i):
        return pltpu.make_async_copy(
            lm_in.at[pl.ds(pl.multiple_of(own + i * chunk, chunk), chunk), :],
            a_stage.at[pl.ds(pl.multiple_of(i * chunk, chunk), chunk), :],
            local_sem.at[2 + i],
        )

    for i in range(n_chunk):
        a_copy(i).start()
    b_copy = pltpu.make_async_copy(
        lm_in.at[far_cols, own_cols], b_stage, local_sem.at[2 + n_chunk]
    )
    b_copy.start()

    barrier = pltpu.get_barrier_semaphore()

    def greet(i):
        p = lax.rem(me + i + 1, n_dom)
        pl.semaphore_signal(barrier, inc=1, device_id=(p, f), device_id_type=MESH)

    loop(n_dom - 1, greet)
    pl.semaphore_signal(barrier, inc=1, device_id=(me, other), device_id_type=MESH)

    def pair_copy(src, dst, k):
        return pltpu.make_async_remote_copy(
            src_ref=src, dst_ref=dst, send_sem=pair_send.at[k], recv_sem=pair_recv.at[k],
            device_id=(me, other), device_id_type=MESH,
        )

    off = lax.rem(shard * me, HID)
    off_row, off_lane = off // LANES, lax.rem(off, LANES)
    t_rows = 2 * win
    lane_t = iota((t_rows, LANES), 1)

    def to_window(t):
        r = pltpu.roll(t, off_lane, 1)
        t = jnp.where(lane_t < off_lane, pltpu.roll(r, 1, 0), r)
        t = jnp.where(off_row == 1, pltpu.roll(t, 1, 0), t)
        flat_t[...] = t
        return jnp.concatenate(
            [flat_t[pl.ds(0, win, stride=2), :], flat_t[pl.ds(1, win, stride=2), :]], axis=1
        )

    def from_window(w):
        flat_t[pl.ds(0, win, stride=2), :] = w[:, :LANES]
        flat_t[pl.ds(1, win, stride=2), :] = w[:, LANES:]
        t = flat_t[...]
        t = jnp.where(off_row == 1, pltpu.roll(t, t_rows - 1, 0), t)
        back = lax.rem(LANES - off_lane, LANES)
        near = pltpu.roll(t, back, 1)
        after = pltpu.roll(near, t_rows - 1, 0)
        return jnp.where(lane_t + off_lane < LANES, near, after)

    flat_t[...] = jnp.zeros_like(flat_t)
    for k in range(-(-shard // LANES)):
        width = min(LANES, shard - k * LANES)
        flat_t[k : k + 1, 0:width] = master_in[0:1, k * LANES : k * LANES + width]
    window = to_window(flat_t[...])
    if par_rows > win:
        window = jnp.concatenate([window, jnp.zeros((par_rows - win, HID), F32)], axis=0)
    par_tx[...] = window.astype(BF)
    par_rx[f, pl.ds(pl.multiple_of(me * par_rows, par_rows), par_rows), :] = par_tx[...]

    x_copy.wait()
    pad_rows = iota((FEAT_PAD, nodes), 0)
    x_pad[...] = jnp.where(pad_rows == fin, 1.0, 0.0)
    x_pad[0:fin, :] = x_stage[...].astype(F32)
    xs[pl.ds(pl.multiple_of(f * FEAT_PAD, FEAT_PAD), FEAT_PAD), :] = x_pad[...].astype(BF)

    pl.semaphore_wait(barrier, n_dom)

    slice_rows = pl.ds(pl.multiple_of(f * FEAT_PAD, FEAT_PAD), FEAT_PAD)
    x_pair = pair_copy(xs.at[slice_rows, :], xs.at[slice_rows, :], 0)
    x_pair.start()

    def par_copy(p):
        return pltpu.make_async_remote_copy(
            src_ref=par_tx,
            dst_ref=par_rx.at[f, pl.ds(pl.multiple_of(me * par_rows, par_rows), par_rows), :],
            send_sem=par_send, recv_sem=par_recv, device_id=(p, f), device_id_type=MESH,
        )

    loop(n_dom - 1, lambda i: par_copy(lax.rem(me + i + 1, n_dom)).start())

    send_rows = send_in[...].astype(F32)
    lane_d = iota(send_rows.shape, 1)
    node_lane = iota((16, nodes), 1).astype(F32)

    def build_sel(q):
        first = jnp.sum(jnp.where(lane_d == 2 * q, send_rows, 0.0), axis=1, keepdims=True)
        second = jnp.sum(jnp.where(lane_d == 2 * q + 1, send_rows, 0.0), axis=1, keepdims=True)
        rows = jnp.concatenate([first, second], axis=0)
        sel[pl.ds(pl.multiple_of(q * 16, 16), 16), :] = jnp.where(
            node_lane == rows, 1.0, 0.0
        ).astype(BF)

    loop(n_dom // 2, build_sel)

    def halo_copy(k, p):
        return pltpu.make_async_remote_copy(
            src_ref=halo_tx.at[k, p], dst_ref=halo_rx.at[k, me],
            send_sem=halo_send.at[k], recv_sem=halo_recv.at[k],
            device_id=(p, f), device_id_type=MESH,
        )

    def send_halo(k):
        loop(n_dom - 1, lambda i: halo_copy(k, lax.rem(me + i + 1, n_dom)).start())
        halo_rx[k, me] = halo_tx[k, me]

    def pack_halo(k, rows):
        v = rows.reshape(n_dom, 8, HID)
        halo_tx[k] = jnp.concatenate([v[:, :, :LANES], v[:, :, LANES:]], axis=1).astype(BF)

    def wait_halo(k):
        part = pl.ds(0, n_dom - 1)
        pltpu.make_async_copy(halo_rx.at[k, part], halo_rx.at[k, part], halo_recv.at[k]).wait()

    def wait_halo_sent(k):
        part = pl.ds(0, n_dom - 1)
        pltpu.make_async_copy(halo_tx.at[k, part], halo_tx.at[k, part], halo_send.at[k]).wait()

    def read_halo(k):
        v = halo_rx[k].astype(F32)
        rows = jnp.concatenate(
            [v[:, :8, :].reshape(halo, LANES), v[:, 8:, :].reshape(halo, LANES)], axis=1
        )
        return rows.T.astype(BF)

    x_pair.wait_recv()
    picked = dot(sel[...], xs[...], 1, 1).reshape(n_dom, 8, LANES)
    count = jnp.sum(lmask_in[...].astype(F32), axis=1, keepdims=True)
    count_high = jnp.floor(count * (1.0 / 256.0))
    count_low = count - 256.0 * count_high
    count_row = iota((8, LANES), 0)
    counts = jnp.where(count_row == 0, count_high, jnp.where(count_row == 1, count_low, 0.0))
    counts = jnp.broadcast_to(counts[None], (n_dom, 8, LANES))
    halo_tx[0] = jnp.concatenate([picked, counts], axis=1).astype(BF)
    send_halo(0)

    for i in range(nodes // h_rows):
        h_copy(i).wait()
        hmt[:, i * h_rows : (i + 1) * h_rows] = h_stage[...].astype(F32).T.astype(BF)
        if (i + 1) * h_rows < nodes:
            h_copy(i + 1).start()

    def convert_a(i):
        a_copy(i).wait()
        rows = pl.ds(pl.multiple_of(i * chunk, chunk), chunk)
        a_rows[rows, :] = a_stage[rows, :].astype(F32).astype(BF)

    loop(n_chunk, convert_a)
    b_copy.wait()
    b_x[...] = b_stage[...].astype(F32).astype(BF)

    part = pl.ds(0, (n_dom - 1) * par_rows)
    pltpu.make_async_copy(par_rx.at[f, part, :], par_rx.at[f, part, :], par_recv).wait()
    par_pair = pair_copy(par_rx.at[f], par_rx.at[f], 1)
    par_pair.start()

    agg_zero[...] = dot(xs[...], a_rows[...], 1, 1)
    wait_halo(0)
    arrived = halo_rx[0].astype(F32)
    halo_zero = arrived[:, :8, :].reshape(halo, LANES).T.astype(BF)
    count_all = jnp.sum(arrived[:, 8:, :], axis=0)
    label_count = 256.0 * count_all[0:1, 0:1] + count_all[1:2, 0:1]
    summed = agg_zero[...] + dot(halo_zero, hmt[:, own_cols])
    inverse = 1.0 / jnp.maximum(summed[fin : fin + 1, :], 1.0)
    inv_ref[...] = jnp.broadcast_to(inverse, inv_ref.shape)
    agg_ref[2, 0:LANES, :] = (summed * inverse).astype(BF)

    par_pair.wait_recv()
    k_all = n_dom * par_rows
    r_pad = iota((ROWS_PAD, k_all), 0)
    k_col = iota((ROWS_PAD, k_all), 1)
    owner, inner = k_col // par_rows, lax.rem(k_col, par_rows)
    target = lax.shift_right_logical(owner * shard, 8) + inner
    row_of = jnp.where(
        r_pad < fin, r_pad,
        jnp.where(
            (r_pad >= FEAT_PAD) & (r_pad < FEAT_PAD + fin), r_pad - (FEAT_PAD - fin),
            jnp.where(
                (r_pad >= ROW_ONE) & (r_pad < ROW_TWO + HEAD_ROWS), r_pad - (ROW_ONE - 2 * fin),
                jnp.where(
                    (r_pad >= ROW_NORM) & (r_pad < ROW_NORM + 2),
                    r_pad - ROW_NORM + (rows_all - 2), -1,
                ),
            ),
        ),
    )
    place = jnp.where(row_of == target, 1.0, 0.0).astype(BF)
    node = iota((HID, 48), 0)
    first_row = lax.shift_right_logical(node * CLS, 8)
    row_id = iota((HID, 48), 1)
    pick_a = jnp.where(row_id == first_row, 1.0, 0.0)
    pick_b = jnp.where(row_id == first_row + 1, 1.0, 0.0)
    start_lane = (iota((HID, HID), 0) * CLS) & (HID - 1)
    lane_w = iota((HID, HID), 1)
    for c in range(2):
        rows = dot(place, par_rx[c])
        rows_t = rows.T
        wmat[c] = rows.astype(BF)
        wmat_t[c] = rows_t.astype(BF)
        for k in range(2):
            col = rows_t[:, ROW_NORM + k : ROW_NORM + k + 1]
            norm_col[c * HALF_HID : (c + 1) * HALF_HID, 2 * k : 2 * k + 1] = col[:HALF_HID]
            norm_col[c * HALF_HID : (c + 1) * HALF_HID, 2 * k + 1 : 2 * k + 2] = col[HALF_HID:]
        flat = rows[ROW_TWO : ROW_TWO + 48].astype(BF)
        lo, hi = dot(pick_a.astype(BF), flat), dot(pick_b.astype(BF), flat)
        wide = jnp.where(lane_w >= start_lane, lo, hi)
        wide = roll_rows(wide, start_lane, False)
        head = jnp.where(lane_w < CLS, wide, 0.0)[:, :LANES]
        head_t = head.T[:CLS_PAD]
        half_rows = slice(c * HALF_HID, (c + 1) * HALF_HID)
        head_ws[half_rows, :] = head[:HALF_HID].astype(BF)
        head_wn[half_rows, :] = head[HALF_HID:].astype(BF)
        head_ws_t[:, half_rows] = head_t[:, :HALF_HID].astype(BF)
        head_wn_t[:, half_rows] = head_t[:, HALF_HID:].astype(BF)

    wide_cols = 128
    n_cols = half // wide_cols

    def norm_forward(layer, dest):
        def body(j):
            cols = pl.ds(pl.multiple_of(j * wide_cols, wide_cols), wide_cols)
            x = mixed[:, cols]
            centre = x - jnp.mean(x, axis=0, keepdims=True)
            rs = lax.rsqrt(jnp.mean(centre * centre, axis=0, keepdims=True) + EPSILON)
            n = centre * rs
            normed[layer, :, cols] = n
            scale_inv[layer, :, cols] = jnp.broadcast_to(rs, (8, wide_cols))
            shifted = n * norm_col[:, 2 * layer : 2 * layer + 1] + norm_col[
                :, 2 * layer + 1 : 2 * layer + 2
            ]
            out = pl.ds(pl.multiple_of(own + j * wide_cols, wide_cols), wide_cols)
            hs[dest, :, out] = gelu(shifted).astype(BF)

        loop(n_cols, body)

    x_own = xs[:, own_cols]
    agg_own = agg_ref[2, 0:LANES, :]
    states = jnp.concatenate(
        [x_own[:FEAT_PAD], agg_own[:FEAT_PAD], x_own[FEAT_PAD:], agg_own[FEAT_PAD:]], axis=0
    )
    w_zero = jnp.concatenate([wmat_t[0, :, :ROW_ONE], wmat_t[1, :, :ROW_ONE]], axis=1)
    mixed[...] = dot(w_zero, states)
    norm_forward(0, 0)

    def exchange_forward(k):
        copy = pair_copy(hs.at[k, :, own_cols], hs.at[k, :, own_cols], 2 + k)
        copy.start()
        copy.wait_recv()
        pack_halo(1 + k, dot(sel[...], hs[k], 1, 1))
        send_halo(1 + k)
        return copy

    def aggregate(k):
        mixed[...] = dot(hs[k], a_rows[...], 1, 1)
        wait_halo(1 + k)
        total = mixed[...] + dot(read_halo(1 + k), hmt[:, own_cols])
        agg_ref[k] = (total * inv_ref[0:1, :]).astype(BF)

    h_pair_one = exchange_forward(0)
    aggregate(0)
    w_self_t = jnp.concatenate(
        [wmat_t[0, :, ROW_ONE : ROW_ONE + LANES], wmat_t[1, :, ROW_ONE : ROW_ONE + LANES]], axis=1
    )
    w_neigh_t = jnp.concatenate(
        [wmat_t[0, :, ROW_ONE + LANES : ROW_TWO], wmat_t[1, :, ROW_ONE + LANES : ROW_TWO]], axis=1
    )
    mixed[...] = dot(w_self_t, hs[0, :, own_cols]) + dot(w_neigh_t, agg_ref[0])
    norm_forward(1, 1)
    h_pair_two = exchange_forward(1)
    aggregate(1)

    logits = dot(head_ws_t[...], hs[1, :, own_cols]) + dot(head_wn_t[...], agg_ref[1])
    class_id = iota((CLS_PAD, half), 0)
    logits = jnp.where(class_id < CLS, logits, -1e30)
    top = jnp.max(logits, axis=0, keepdims=True)
    log_total = top + jnp.log(jnp.sum(jnp.exp(logits - top), axis=0, keepdims=True))
    onehot = class_id == label_in[0:1, own_cols]
    weight = lmask_in[0:1, own_cols].astype(F32)
    chosen = jnp.sum(jnp.where(onehot, logits, 0.0), axis=0, keepdims=True)
    loss_part = jnp.sum((log_total - chosen) * weight, axis=1, keepdims=True)
    loss_ref[...] = jnp.broadcast_to(loss_part, loss_ref.shape)
    probs = jnp.exp(logits - log_total)
    g_logits = (probs - jnp.where(onehot, 1.0, 0.0)) * (weight / label_count)
    g_low[0, 0:CLS_PAD, :] = g_logits.astype(BF)
    g_head = g_low[0, 0:CLS_PAD, :]

    def exchange_backward(k):
        copy = pair_copy(gs_all.at[k, :, own_cols], gs_all.at[k, :, own_cols], 4 + k)
        copy.start()
        copy.wait_recv()
        pack_halo(3 + k, dot(hmt[...], gs_all[k], 1, 1))
        send_halo(3 + k)
        return copy

    def spread(k):
        mixed[...] += dot(gs_all[k, :, own_cols], a_rows[:, own_cols]) + dot(
            gs_all[k, :, far_cols], b_x[...]
        )
        wait_halo(3 + k)
        mixed[...] += dot(read_halo(3 + k), sel[:, own_cols])

    def norm_backward(layer, dest):
        acc_gain[...] = jnp.zeros_like(acc_gain)
        acc_bias[...] = jnp.zeros_like(acc_bias)

        def body(j):
            cols = pl.ds(pl.multiple_of(j * wide_cols, wide_cols), wide_cols)
            n = normed[layer, :, cols]
            gain = norm_col[:, 2 * layer : 2 * layer + 1]
            shifted = n * gain + norm_col[:, 2 * layer + 1 : 2 * layer + 2]
            g_shift = mixed[:, cols] * gelu_grad(shifted)
            acc_gain[...] += g_shift * n
            acc_bias[...] += g_shift
            gn = g_shift * gain
            mean_one = jnp.mean(gn, axis=0, keepdims=True)
            mean_two = jnp.mean(gn * n, axis=0, keepdims=True)
            g_mixed = (gn - mean_one - n * mean_two) * scale_inv[layer, 0:1, cols]
            g_low[dest, :, cols] = g_mixed.astype(BF)

        loop(n_cols, body)
        gain_row = jnp.sum(acc_gain[...].T, axis=0, keepdims=True)
        bias_row = jnp.sum(acc_bias[...].T, axis=0, keepdims=True)
        base = rows_all - 2 + layer
        for ref, c in ((grad_a, 0), (grad_b, 1)):
            piece = slice(c * HALF_HID, (c + 1) * HALF_HID)
            ref[base : base + 1, :LANES] = gain_row[:, piece]
            ref[base : base + 1, LANES:] = bias_row[:, piece]

    gs_all[0, :, own_cols] = (dot(head_wn[:, :CLS_PAD], g_head) * inv_ref[0:1, :]).astype(BF)
    g_pair_two = exchange_backward(0)
    mixed[...] = dot(head_ws[:, :CLS_PAD], g_head)
    lane_h = iota((HID, HID), 1)
    dws = dot(hs[1, :, own_cols], g_head, 1, 1)
    dwn = dot(agg_ref[1], g_head, 1, 1)
    for ref, c in ((grad_a, 0), (grad_b, 1)):
        piece = slice(c * HALF_HID, (c + 1) * HALF_HID)
        dw_head[...] = jnp.zeros_like(dw_head)
        dw_head[:HALF_HID, :CLS_PAD] = dws[piece]
        dw_head[HALF_HID:, :CLS_PAD] = dwn[piece]
        wide = roll_rows(dw_head[...], start_lane, True)
        low_part = jnp.where(lane_h >= start_lane, wide, 0.0)
        high_part = jnp.where(lane_h >= start_lane, 0.0, wide)
        flat = dot(pick_a, low_part, 0, 0, lax.Precision.HIGHEST) + dot(
            pick_b, high_part, 0, 0, lax.Precision.HIGHEST
        )
        base = 2 * fin + 2 * HALF_HID
        ref[base : base + HEAD_ROWS, :] = flat[:HEAD_ROWS]
    spread(0)
    norm_backward(1, 1)

    g_one = g_low[1]
    w_self = jnp.concatenate(
        [wmat[0, ROW_ONE : ROW_ONE + LANES], wmat[1, ROW_ONE : ROW_ONE + LANES]], axis=0
    )
    w_neigh = jnp.concatenate(
        [wmat[0, ROW_ONE + LANES : ROW_TWO], wmat[1, ROW_ONE + LANES : ROW_TWO]], axis=0
    )
    gs_all[1, :, own_cols] = (dot(w_neigh, g_one) * inv_ref[0:1, :]).astype(BF)
    g_pair_one = exchange_backward(1)
    mixed[...] = dot(w_self, g_one)
    dws = dot(hs[0, :, own_cols], g_one, 1, 1)
    dwn = dot(agg_ref[0], g_one, 1, 1)
    for ref, c in ((grad_a, 0), (grad_b, 1)):
        piece = slice(c * HALF_HID, (c + 1) * HALF_HID)
        base = 2 * fin
        ref[base : base + HALF_HID, :] = dws[piece]
        ref[base + HALF_HID : base + 2 * HALF_HID, :] = dwn[piece]
    spread(1)
    norm_backward(0, 2)

    g_zero = g_low[2]
    dws = dot(x_own, g_zero, 1, 1)
    dwn = dot(agg_own, g_zero, 1, 1)
    for ref, c in ((grad_a, 0), (grad_b, 1)):
        start = c * FEAT_PAD
        ref[0:fin, :] = dws[start : start + fin]
        ref[fin : 2 * fin, :] = dwn[start : start + fin]
        tail = ref.shape[0] - 8
        ref[tail : tail + 8, :] = jnp.broadcast_to(loss_ref[:, 0:1], (8, HID))

    @pl.when(f == 0)
    def _():
        grad_flat[0] = grad_a[...]
        grad_flat[1] = grad_b[...]

    @pl.when(f == 1)
    def _():
        grad_flat[0] = grad_b[...]
        grad_flat[1] = grad_a[...]

    grad_pair = pair_copy(grad_flat.at[1], pair_rx, 6)
    grad_pair.start()
    grad_pair.wait_recv()
    grad_a[...] = grad_flat[0] + pair_rx[...]
    tail = cfg["grad_rows"] - 8

    def window_of(d):
        start = lax.shift_right_logical(shard * d, 8)
        shift = start & 7
        base = pl.multiple_of(start - shift, 8)
        rows = pltpu.roll(grad_a[pl.ds(base, win + 8), :], win + 8 - shift, 0)[:win]
        last = iota((win, HID), 0) == win - 1
        return jnp.where(last, grad_a[tail : tail + 1, :], rows)

    def win_copy(p):
        return pltpu.make_async_remote_copy(
            src_ref=win_tx.at[p], dst_ref=win_rx.at[me],
            send_sem=win_send, recv_sem=win_recv, device_id=(p, f), device_id_type=MESH,
        )

    def send_window(i):
        p = lax.rem(me + i + 1, n_dom)
        win_tx[p] = window_of(p)
        win_copy(p).start()

    loop(n_dom - 1, send_window)
    win_rx[me] = window_of(me)
    part = pl.ds(0, n_dom - 1)
    pltpu.make_async_copy(win_rx.at[part], win_rx.at[part], win_recv).wait()
    total = jnp.sum(win_rx[...], axis=0)
    scalar_out[0:1, :] = total[win - 1 : win, :LANES]
    scalar_out[1:2, :] = jnp.broadcast_to(label_count, (1, LANES))
    total = jnp.where(iota((win, HID), 0) == win - 1, 0.0, total)
    grad_out[...] = from_window(total)

    for copy in (x_pair, par_pair, h_pair_one, h_pair_two, g_pair_two, g_pair_one, grad_pair):
        copy.wait_send()
    for k in range(5):
        wait_halo_sent(k)
    pltpu.make_async_copy(win_tx.at[part], win_tx.at[part], win_send).wait()
    part = pl.ds(0, (n_dom - 1) * par_rows)
    pltpu.make_async_copy(par_rx.at[f, part, :], par_rx.at[f, part, :], par_send).wait()


def round_up(value, step):
    return -(-value // step) * step


def per_device(n_dom, features, local_mask, halo_mask, send_rows, labels, label_mask, master, first, second):
    nodes, halo = local_mask.shape[1], halo_mask.shape[1]
    half, shard, fin = nodes // 2, master.shape[1], features.shape[1]
    rows_all = n_dom * shard // HID
    span = (shard + HID - 2) // HID + 1
    win = round_up(span + 1, 8)
    par_rows = round_up(span, 16)
    grad_rows = round_up(rows_all + win, 8) + 8
    cfg = dict(
        n_dom=n_dom, nodes=nodes, half=half, halo=halo, shard=shard, fin=fin, win=win,
        par_rows=par_rows, rows_all=rows_all, grad_rows=grad_rows,
        h_rows=min(nodes, 2**18 // halo),
    )
    hbm = pl.BlockSpec(memory_space=pl.ANY)
    vmem = pl.BlockSpec(memory_space=pltpu.VMEM)
    i32 = jnp.int32
    scratch = [
        pltpu.VMEM((half, nodes), i32),
        pltpu.VMEM((half, half), i32),
        pltpu.VMEM((cfg["h_rows"], halo), i32),
        pltpu.VMEM((fin, nodes), BF),
        pltpu.VMEM((FEAT_PAD, nodes), F32),
        pltpu.VMEM((half, nodes), BF),
        pltpu.VMEM((half, half), BF),
        pltpu.VMEM((halo, nodes), BF),
        pltpu.VMEM((halo, nodes), BF),
        pltpu.VMEM((2 * FEAT_PAD, nodes), BF),
        pltpu.VMEM((2, HID, nodes), BF),
        pltpu.VMEM((2, HID, nodes), BF),
        pltpu.VMEM((3, HID, half), BF),
        pltpu.VMEM((LANES, half), F32),
        pltpu.VMEM((HID, half), F32),
        pltpu.VMEM((2, HID, half), F32),
        pltpu.VMEM((2, 8, half), F32),
        pltpu.VMEM((8, half), F32),
        pltpu.VMEM((5, n_dom, 16, LANES), BF),
        pltpu.VMEM((5, n_dom, 16, LANES), BF),
        pltpu.VMEM((2 * win, LANES), F32),
        pltpu.VMEM((par_rows, HID), BF),
        pltpu.VMEM((2, n_dom * par_rows, HID), BF),
        pltpu.VMEM((2, ROWS_PAD, HID), BF),
        pltpu.VMEM((2, HID, ROWS_PAD), BF),
        pltpu.VMEM((HID, 8), F32),
        pltpu.VMEM((HID, LANES), BF),
        pltpu.VMEM((HID, LANES), BF),
        pltpu.VMEM((CLS_PAD, HID), BF),
        pltpu.VMEM((CLS_PAD, HID), BF),
        pltpu.VMEM((3, HID, half), BF),
        pltpu.VMEM((grad_rows, HID), F32),
        pltpu.VMEM((grad_rows, HID), F32),
        pltpu.VMEM((2, grad_rows, HID), F32),
        pltpu.VMEM((grad_rows, HID), F32),
        pltpu.VMEM((n_dom, win, HID), F32),
        pltpu.VMEM((n_dom, win, HID), F32),
        pltpu.VMEM((HID, HID), F32),
        pltpu.VMEM((HID, LANES), F32),
        pltpu.VMEM((HID, LANES), F32),
        pltpu.VMEM((8, LANES), F32),
        pltpu.SemaphoreType.DMA((3 + half // 128,)),
        pltpu.SemaphoreType.DMA((7,)),
        pltpu.SemaphoreType.DMA((7,)),
        pltpu.SemaphoreType.DMA((5,)),
        pltpu.SemaphoreType.DMA((5,)),
        pltpu.SemaphoreType.DMA,
        pltpu.SemaphoreType.DMA,
        pltpu.SemaphoreType.DMA,
        pltpu.SemaphoreType.DMA,
    ]
    grad, scalars = pl.pallas_call(
        functools.partial(kernel, cfg),
        out_shape=(
            jax.ShapeDtypeStruct((2 * win, LANES), F32),
            jax.ShapeDtypeStruct((2, LANES), F32),
        ),
        in_specs=[hbm, hbm, hbm, vmem, vmem, vmem, vmem],
        out_specs=(vmem, vmem),
        scratch_shapes=scratch,
        compiler_params=pltpu.CompilerParams(
            collective_id=0, has_side_effects=True, vmem_limit_bytes=60 * 2**20
        ),
    )(
        features.T,
        local_mask,
        halo_mask,
        send_rows[0].T,
        labels.reshape(1, nodes),
        label_mask.reshape(1, nodes),
        master,
    )
    own_grad = grad.reshape(1, -1)[:, :shard]
    new_first = DECAY_ONE * first + (1.0 - DECAY_ONE) * own_grad
    new_second = DECAY_TWO * second + (1.0 - DECAY_TWO) * own_grad * own_grad
    first_hat = new_first / (1.0 - DECAY_ONE**STEP)
    second_hat = new_second / (1.0 - DECAY_TWO**STEP)
    new_master = master - LEARN_RATE * (
        first_hat / (jnp.sqrt(second_hat) + ADAM_EPS) + WEIGHT_DECAY * master
    )
    return (scalars[0, 0], scalars[1, 0], new_master, new_first, new_second)


def solution(mesh):
    in_specs = (
        P("dom", "feat"),
        P("dom", None),
        P("dom", None),
        P("dom", None, None),
        P("dom"),
        P("dom"),
        P("feat", "dom"),
        P("feat", "dom"),
        P("feat", "dom"),
    )
    out_specs = (P(), P(), P("feat", "dom"), P("feat", "dom"), P("feat", "dom"))
    return jax.shard_map(
        functools.partial(per_device, mesh.shape["dom"]),
        mesh=mesh, in_specs=in_specs, out_specs=out_specs, check_vma=False,
    )
```

```python
import functools

import jax
import jax.numpy as jnp
from jax import lax
from jax.experimental import pallas as pl
from jax.experimental.pallas import tpu as pltpu
from jax.sharding import PartitionSpec as P

HID = 256
CLS = 47
STEP = 10
EPSILON = 1e-05
LEARN_RATE = 0.02
DECAY_ONE = 0.9
DECAY_TWO = 0.999
ADAM_EPS = 1e-08
WEIGHT_DECAY = 0.01

MESH = pl.DeviceIdType.MESH
BF = jnp.bfloat16
F32 = jnp.float32
LANES = 128
CLS_PAD = 64
FEAT_PAD = 64
HALF_HID = HID // 2
ROW_ONE = 2 * FEAT_PAD
ROW_TWO = ROW_ONE + 2 * HALF_HID
HEAD_ROWS = 2 * HALF_HID * CLS // HID
ROW_NORM = ROW_TWO + 48
GELU_A = 0.7978845608028654
GELU_B = 0.044715


def dot(a, b, ca=1, cb=0, precision=None):
    return lax.dot_general(
        a, b, (((ca,), (cb,)), ((), ())), precision=precision, preferred_element_type=F32
    )


def iota(shape, axis):
    return lax.broadcasted_iota(jnp.int32, shape, axis)


def gelu(x):
    half = 0.5 * x
    return half + half * jnp.tanh(x * (GELU_A + (GELU_A * GELU_B) * (x * x)))


def gelu_grad(x):
    xx = x * x
    t = jnp.tanh(x * (GELU_A + (GELU_A * GELU_B) * xx))
    return 0.5 + 0.5 * t + (x * (GELU_A + (3.0 * GELU_A * GELU_B) * xx)) * (0.5 - 0.5 * (t * t))


def roll_rows(x, amount, right):
    for bit in range(8):
        step = 1 << bit
        moved = pltpu.roll(x, step if right else HID - step, 1)
        x = jnp.where((amount & step) != 0, moved, x)
    return x


def loop(n, body):
    def step(i, carry):
        body(i)
        return carry

    lax.fori_loop(0, n, step, 0)


def kernel(
    cfg,
    x_in, lm_in, hm_in, send_hbm, label_hbm, lmask_hbm, master_hbm,
    grad_out, scalar_out,
    send_in, label_in, lmask_in, master_in,
    a_stage, b_stage, h_stage, x_stage,
    a_rows, b_far, hmt, sel, xs, hs, gs_all, agg_ref, agg_zero,
    edge_rows, edge_far, edge_hm, edge_x, edge_h, edge_mixed, edge_inv, part_tx, part_rx,
    mixed, normed, slope, scale_inv, inv_ref, halo_tx, halo_rx,
    flat_t, par_tx, par_rx, wmat, wmat_t, norm_col, head_ws, head_wn, head_ws_t, head_wn_t,
    g_low, grads, early_rx, late_rx, one_tx, one_rx, two_tx, two_rx, top_tx, top_one, top_two, dw_head, acc_gain, acc_bias, place,
    local_sem, pair_send, pair_recv, halo_send, halo_recv, par_send, column_recv, plane_recv,
    one_send, one_recv, two_send, two_recv, top_send, top_recv,
):
    n_dom, nodes, half, halo, shard, fin = (
        cfg["n_dom"], cfg["nodes"], cfg["half"], cfg["halo"], cfg["shard"], cfg["fin"]
    )
    win, par_rows, rows_all = cfg["win"], cfg["par_rows"], cfg["rows_all"]
    me, f = lax.axis_index("dom"), lax.axis_index("feat")
    other = 1 - f
    own = pl.multiple_of(f * half, half)
    far = pl.multiple_of(other * half, half)
    own_cols, far_cols = pl.ds(own, half), pl.ds(far, half)

    barrier = pltpu.get_barrier_semaphore()

    def greet(i):
        p = lax.rem(me + i + 1, n_dom)
        pl.semaphore_signal(barrier, inc=1, device_id=(p, f), device_id_type=MESH)

    loop(n_dom - 1, greet)
    pl.semaphore_signal(barrier, inc=1, device_id=(me, other), device_id_type=MESH)

    chunk = 128
    n_chunk = half // chunk
    x_copy = pltpu.make_async_copy(x_in, x_stage, local_sem.at[4])
    x_copy.start()
    small_copies = [
        pltpu.make_async_copy(src, dst, local_sem.at[k])
        for k, (src, dst) in enumerate(
            ((master_hbm, master_in), (send_hbm, send_in), (label_hbm, label_in),
             (lmask_hbm, lmask_in))
        )
    ]
    for copy in small_copies:
        copy.start()
    h_rows = cfg["h_rows"]

    def h_copy(i):
        return pltpu.make_async_copy(
            hm_in.at[pl.ds(i * h_rows, h_rows), :], h_stage, local_sem.at[5]
        )

    h_copy(0).start()

    slots = cfg["slots"]

    def a_copy(i):
        return pltpu.make_async_copy(
            lm_in.at[pl.ds(pl.multiple_of(own + i * chunk, chunk), chunk), :],
            a_stage.at[lax.rem(i, slots)], local_sem.at[6 + lax.rem(i, slots)],
        )

    def b_copy(i):
        return pltpu.make_async_copy(
            lm_in.at[pl.ds(pl.multiple_of(far + i * chunk, chunk), chunk), own_cols],
            b_stage.at[lax.rem(i, slots)], local_sem.at[6 + slots + lax.rem(i, slots)],
        )

    loop(slots, lambda i: a_copy(i).start())
    loop(slots, lambda i: b_copy(i).start())

    def pair_copy(src, dst, k):
        return pltpu.make_async_remote_copy(
            src_ref=src, dst_ref=dst, send_sem=pair_send.at[k], recv_sem=pair_recv.at[k],
            device_id=(me, other), device_id_type=MESH,
        )

    x_copy.wait()
    slice_rows = pl.ds(pl.multiple_of(f * FEAT_PAD, FEAT_PAD), FEAT_PAD)
    pad_rows = iota((FEAT_PAD, half), 0)
    for c in range(2):
        part = slice(c * half, (c + 1) * half)
        mixed[0:FEAT_PAD, :] = jnp.where(pad_rows == fin, 1.0, 0.0)
        mixed[0:fin, :] = x_stage[:, part].astype(F32)
        xs[slice_rows, part] = mixed[0:FEAT_PAD, :].astype(BF)

    pl.semaphore_wait(barrier, n_dom)

    x_pair = pair_copy(xs.at[slice_rows, :], xs.at[slice_rows, :], 0)
    x_pair.start()
    off = lax.rem(shard * me, HID)
    off_row, off_lane = off // LANES, lax.rem(off, LANES)
    t_rows = 2 * win
    lane_t = iota((t_rows, LANES), 1)

    def to_window(t):
        r = pltpu.roll(t, off_lane, 1)
        t = jnp.where(lane_t < off_lane, pltpu.roll(r, 1, 0), r)
        t = jnp.where(off_row == 1, pltpu.roll(t, 1, 0), t)
        flat_t[...] = t
        return jnp.concatenate(
            [flat_t[pl.ds(0, win, stride=2), :], flat_t[pl.ds(1, win, stride=2), :]], axis=1
        )

    def from_window(w):
        flat_t[pl.ds(0, win, stride=2), :] = w[:, :LANES]
        flat_t[pl.ds(1, win, stride=2), :] = w[:, LANES:]
        t = flat_t[...]
        t = jnp.where(off_row == 1, pltpu.roll(t, t_rows - 1, 0), t)
        back = lax.rem(LANES - off_lane, LANES)
        near = pltpu.roll(t, back, 1)
        after = pltpu.roll(near, t_rows - 1, 0)
        return jnp.where(lane_t + off_lane < LANES, near, after)

    small_copies[0].wait()
    flat_t[...] = jnp.zeros_like(flat_t)
    for k in range(-(-shard // LANES)):
        width = min(LANES, shard - k * LANES)
        flat_t[k : k + 1, 0:width] = master_in[0:1, k * LANES : k * LANES + width]
    window = to_window(flat_t[...])
    if par_rows > win:
        window = jnp.concatenate([window, jnp.zeros((par_rows - win, HID), F32)], axis=0)
    par_tx[...] = window.astype(BF)
    par_rx[f, pl.ds(pl.multiple_of(me * par_rows, par_rows), par_rows), :] = par_tx[...]


    group = cfg["group"]
    n_high = n_dom // group
    high, low = me // group, lax.rem(me, group)
    urgent = cfg["urgent"]
    patient = [h for h in range(n_high) if h not in urgent]

    def par_slot(h, w):
        start = pl.multiple_of((h * group + w) * par_rows, par_rows)
        return par_rx.at[f, pl.ds(start, par_rows), :]

    def par_send_to(h, w, src, slot_high, sem):
        pltpu.make_async_remote_copy(
            src_ref=src, dst_ref=par_slot(slot_high, low), send_sem=par_send, recv_sem=sem,
            device_id=(h * group + w, f), device_id_type=MESH,
        ).start()

    def par_plane(slot_high, src):
        for step in range(1, group):
            par_send_to(high, lax.rem(low + step, group), src, slot_high, plane_recv.at[slot_high])

    def send_params(which):
        is_one = functools.reduce(jnp.logical_or, [high == h for h in which])

        @pl.when(is_one)
        def _():
            for step in range(1, n_high):
                par_send_to(lax.rem(high + step, n_high), low, par_tx, high, column_recv.at[high])
            par_plane(high, par_tx)

    def forward_params(which):
        for h in which:
            @pl.when(high != h)
            def _():
                pltpu.make_async_copy(par_tx, par_tx, column_recv.at[h]).wait()
                par_plane(h, par_slot(h, low))

    def wait_params(which):
        part = pl.ds(0, (group - 1) * par_rows)
        for h in which:
            pltpu.make_async_copy(
                par_rx.at[f, part, :], par_rx.at[f, part, :], plane_recv.at[h]
            ).wait()

    def par_pairs(which, k):
        runs = []
        for h in which:
            if runs and runs[-1][1] == h:
                runs[-1][1] = h + 1
            else:
                runs.append([h, h + 1])
        copies = []
        for i, (start, end) in enumerate(runs):
            part = pl.ds(start * group * par_rows, (end - start) * group * par_rows)
            copies.append(pair_copy(par_rx.at[f, part, :], par_rx.at[f, part, :], k + i))
        return copies

    first_early = cfg["first_early"]
    send_params(urgent)
    small_copies[1].wait()
    send_rows = send_in[...].astype(F32)
    lane_d = iota(send_rows.shape, 1)
    node_lane = iota((16, nodes), 1).astype(F32)

    def build_sel(q):
        first = jnp.sum(jnp.where(lane_d == 2 * q, send_rows, 0.0), axis=1, keepdims=True)
        second = jnp.sum(jnp.where(lane_d == 2 * q + 1, send_rows, 0.0), axis=1, keepdims=True)
        rows = jnp.concatenate([first, second], axis=0)
        sel[pl.ds(pl.multiple_of(q * 16, 16), 16), :] = jnp.where(
            node_lane == rows, 1.0, 0.0
        ).astype(BF)

    if n_dom <= 16:
        for q in range(n_dom // 2):
            build_sel(q)
    else:
        loop(n_dom // 2, build_sel)

    def halo_copy(k, p):
        return pltpu.make_async_remote_copy(
            src_ref=halo_tx.at[k % 2, p], dst_ref=halo_rx.at[k, me],
            send_sem=halo_send.at[k], recv_sem=halo_recv.at[k],
            device_id=(p, f), device_id_type=MESH,
        )

    def send_halo(k):
        loop(n_dom - 1, lambda i: halo_copy(k, lax.rem(me + i + 1, n_dom)).start())
        halo_rx[k, me] = halo_tx[k % 2, me]

    def pack_halo(k, rows):
        v = rows.reshape(n_dom, 8, HID)
        if k >= 2:
            wait_halo_sent(k - 2)
        halo_tx[k % 2] = jnp.concatenate([v[:, :, :LANES], v[:, :, LANES:]], axis=1).astype(BF)

    def wait_halo(k):
        part = pl.ds(0, n_dom - 1)
        pltpu.make_async_copy(halo_rx.at[k, part], halo_rx.at[k, part], halo_recv.at[k]).wait()

    def wait_halo_sent(k):
        part = pl.ds(0, n_dom - 1)
        pltpu.make_async_copy(
            halo_tx.at[k % 2, part], halo_tx.at[k % 2, part], halo_send.at[k]
        ).wait()

    def read_halo(k):
        v = halo_rx[k].astype(F32)
        rows = jnp.concatenate(
            [v[:, :8, :].reshape(halo, LANES), v[:, 8:, :].reshape(halo, LANES)], axis=1
        )
        return rows.T.astype(BF)

    x_pair.wait_recv()
    picked = dot(sel[...], xs[...], 1, 1)
    edge_x[...] = picked.T.astype(BF)
    picked = picked.reshape(n_dom, 8, LANES)
    small_copies[2].wait()
    small_copies[3].wait()
    count = jnp.sum(lmask_in[...].astype(F32), axis=1, keepdims=True)
    count_high = jnp.floor(count * (1.0 / 256.0))
    count_low = count - 256.0 * count_high
    count_row = iota((8, LANES), 0)
    counts = jnp.where(count_row == 0, count_high, jnp.where(count_row == 1, count_low, 0.0))
    counts = jnp.broadcast_to(counts[None], (n_dom, 8, LANES))
    halo_tx[0] = jnp.concatenate([picked, counts], axis=1).astype(BF)
    send_halo(0)

    for i in range(nodes // h_rows):
        h_copy(i).wait()
        hmt[:, i * h_rows : (i + 1) * h_rows] = h_stage[...].astype(F32).T.astype(BF)
        if (i + 1) * h_rows < nodes:
            h_copy(i + 1).start()

    def convert_a(i):
        a_copy(i).wait()
        rows = pl.ds(pl.multiple_of(i * chunk, chunk), chunk)
        a_rows[rows, :] = a_stage[lax.rem(i, slots)].astype(F32).astype(BF)

        @pl.when(i + slots < n_chunk)
        def _():
            a_copy(i + slots).start()

    loop(n_chunk, convert_a)
    edge_hm[...] = dot(hmt[...], sel[...], 1, 1).astype(BF)

    def edge_chunk(q):
        rows = pl.ds(pl.multiple_of(q * LANES, LANES), LANES)
        edge_rows[rows, :] = dot(sel[rows, own_cols], a_rows[...]).astype(BF)

    loop(halo // LANES, edge_chunk)
    edge_pair = pair_copy(edge_rows, edge_far, 7)
    edge_pair.start()
    forward_params(urgent)
    send_params(patient)

    def build_place(q):
        rows = pl.ds(pl.multiple_of(q * 16, 16), 16)
        r_pad = iota((16, k_all), 0) + q * 16
        k_col = iota((16, k_all), 1)
        owner, inner = k_col // par_rows, lax.rem(k_col, par_rows)
        target = lax.shift_right_logical(owner * shard, 8) + inner
        row_of = jnp.where(
            r_pad < fin, r_pad,
            jnp.where(
                (r_pad >= FEAT_PAD) & (r_pad < FEAT_PAD + fin), r_pad - (FEAT_PAD - fin),
                jnp.where(
                    (r_pad >= ROW_ONE) & (r_pad < ROW_TWO + HEAD_ROWS),
                    r_pad - (ROW_ONE - 2 * fin), -1,
                ),
            ),
        )
        place[rows, :] = jnp.where(row_of == target, 1.0, 0.0).astype(BF)

    k_all = n_dom * par_rows
    loop(ROW_NORM // 16, build_place)
    mixed[0:LANES, :] = dot(xs[...], a_rows[...], 1, 1)
    def convert_b(i):
        b_copy(i).wait()
        rows = pl.ds(pl.multiple_of(i * chunk, chunk), chunk)
        b_far[rows, :] = b_stage[lax.rem(i, slots)].astype(F32).astype(BF)

        @pl.when(i + slots < n_chunk)
        def _():
            b_copy(i + slots).start()

    loop(n_chunk, convert_b)

    wait_params(urgent)
    par_urgent = par_pairs(urgent, 16)
    for copy in par_urgent:
        copy.start()
    wait_halo(0)
    arrived = halo_rx[0].astype(F32)
    halo_zero = arrived[:, :8, :].reshape(halo, LANES).T.astype(BF)
    count_all = jnp.sum(arrived[:, 8:, :], axis=0)
    label_count = 256.0 * count_all[0:1, 0:1] + count_all[1:2, 0:1]
    summed = mixed[0:LANES, :] + dot(halo_zero, hmt[:, own_cols])
    inverse = 1.0 / jnp.maximum(summed[fin : fin + 1, :], 1.0)
    inv_ref[...] = jnp.broadcast_to(inverse, inv_ref.shape)
    agg_zero[...] = (summed * inverse).astype(BF)
    edge_pair.wait()

    def edge_sum(q):
        rows = pl.ds(pl.multiple_of(q * LANES, LANES), LANES)
        edge_rows[rows, :] = edge_rows[rows, :] + edge_far[rows, :]

    loop(halo // LANES, edge_sum)
    summed = dot(xs[...], edge_rows[...], 1, 1) + dot(halo_zero, edge_hm[...])
    inverse = 1.0 / jnp.maximum(summed[fin : fin + 1, :], 1.0)
    edge_inv[...] = jnp.broadcast_to(inverse, edge_inv.shape)
    edge_agg = (summed * inverse).astype(BF)

    forward_params(patient)
    for copy in par_urgent:
        copy.wait_recv()
    k_first = first_early * par_rows
    norm_row = (n_dom - 1) * par_rows + rows_all - 2 - shard * (n_dom - 1) // HID
    w_zero = []
    for c in range(2):
        rows_t = dot(place[:ROW_ONE, :k_first], par_rx[c, :k_first, :]).T
        w_zero.append(rows_t.astype(BF))
        block = norm_row // 16 * 16
        norms = par_rx[c, block : block + 32, :].astype(F32) if block + 32 <= k_all else (
            par_rx[c, k_all - 32 : k_all, :].astype(F32)
        )
        block = min(block, k_all - 32)
        norms_t = jnp.concatenate([norms, jnp.zeros((LANES - 32, HID), F32)], axis=0).T
        for k in range(2):
            lane = norm_row - block + k
            col = norms_t[:, lane : lane + 1]
            norm_col[c * HALF_HID : (c + 1) * HALF_HID, 2 * k : 2 * k + 1] = col[:HALF_HID]
            norm_col[c * HALF_HID : (c + 1) * HALF_HID, 2 * k + 1 : 2 * k + 2] = col[HALF_HID:]
    w_zero = jnp.concatenate(w_zero, axis=1)

    def assemble_hidden():
        for c in range(2):
            rows = dot(place[ROW_ONE:ROW_TWO, :], par_rx[c])
            wmat[c] = rows.astype(BF)
            wmat_t[c] = rows.T.astype(BF)

    node = iota((HID, 48), 0)
    first_row = lax.shift_right_logical(node * CLS, 8)
    row_id = iota((HID, 48), 1)
    pick_a = jnp.where(row_id == first_row, 1.0, 0.0)
    pick_b = jnp.where(row_id == first_row + 1, 1.0, 0.0)
    start_lane = (iota((HID, HID), 0) * CLS) & (HID - 1)
    lane_w = iota((HID, HID), 1)

    def assemble_head():
        for c in range(2):
            flat = dot(place[ROW_TWO:ROW_NORM, :], par_rx[c]).astype(BF)
            lo, hi = dot(pick_a.astype(BF), flat), dot(pick_b.astype(BF), flat)
            wide = jnp.where(lane_w >= start_lane, lo, hi)
            wide = roll_rows(wide, start_lane, False)
            head = jnp.where(lane_w < CLS, wide, 0.0)[:, :LANES]
            head_t = head.T[:CLS_PAD]
            half_rows = slice(c * HALF_HID, (c + 1) * HALF_HID)
            head_ws[half_rows, :] = head[:HALF_HID].astype(BF)
            head_wn[half_rows, :] = head[HALF_HID:].astype(BF)
            head_ws_t[:, half_rows] = head_t[:, :HALF_HID].astype(BF)
            head_wn_t[:, half_rows] = head_t[:, HALF_HID:].astype(BF)

    wide_cols = 256
    n_cols = half // wide_cols

    def norm_apply(x, layer):
        centre = x - jnp.mean(x, axis=0, keepdims=True)
        rs = lax.rsqrt(jnp.mean(centre * centre, axis=0, keepdims=True) + EPSILON)
        n = centre * rs
        shifted = n * norm_col[:, 2 * layer : 2 * layer + 1] + norm_col[
            :, 2 * layer + 1 : 2 * layer + 2
        ]
        return n, rs, gelu(shifted).astype(BF)

    def norm_forward(layer, mix):
        for j in range(n_cols):
            cols = slice(j * wide_cols, (j + 1) * wide_cols)
            n, rs, value = norm_apply(mix(j * wide_cols), layer)
            normed[layer, :, cols] = n
            scale_inv[layer, :, cols] = jnp.broadcast_to(rs, (8, wide_cols))
            out = pl.ds(pl.multiple_of(own + j * wide_cols, wide_cols), wide_cols)
            hs[layer, :, out] = value

    def norm_slope(layer):
        def body(i):
            for j in range(2):
                cols = pl.ds(pl.multiple_of((2 * i + j) * LANES, LANES), LANES)
                shifted = normed[layer, :, cols] * norm_col[
                    :, 2 * layer : 2 * layer + 1
                ] + norm_col[:, 2 * layer + 1 : 2 * layer + 2]
                slope[layer, :, cols] = gelu_grad(shifted)

        loop(half // (2 * LANES), body)

    def norm_edge(layer):
        def body(j):
            cols = pl.ds(pl.multiple_of(j * LANES, LANES), LANES)
            edge_h[layer, :, cols] = norm_apply(edge_mixed[:, cols], layer)[2]

        loop(halo // LANES, body)
        pack_halo(1 + layer, edge_h[layer].astype(F32).T)
        send_halo(1 + layer)

    def rows_of(x, agg):
        return jnp.concatenate([x[:FEAT_PAD], agg[:FEAT_PAD], x[FEAT_PAD:], agg[FEAT_PAD:]], axis=0)

    x_own = xs[:, own_cols]
    agg_own = agg_zero[...]
    edge_mixed[...] = dot(w_zero, rows_of(edge_x[...], edge_agg))
    norm_edge(0)
    norm_forward(
        0, lambda c: dot(
            w_zero,
            rows_of(
                xs[:, pl.ds(pl.multiple_of(own + c, wide_cols), wide_cols)],
                agg_zero[:, c : c + wide_cols],
            ),
        ),
    )
    h_pair_one = pair_copy(hs.at[0, :, own_cols], hs.at[0, :, own_cols], 2)
    h_pair_one.start()
    mixed[...] = dot(hs[0, :, own_cols], a_rows[:, own_cols], 1, 1)
    wait_params(patient)
    par_rest = par_pairs(patient, 20)
    for copy in par_rest:
        copy.start()
    for copy in par_rest:
        copy.wait_recv()
    assemble_hidden()
    w_self_t = jnp.concatenate([wmat_t[0, :, :LANES], wmat_t[1, :, :LANES]], axis=1)
    w_neigh_t = jnp.concatenate([wmat_t[0, :, LANES:], wmat_t[1, :, LANES:]], axis=1)
    h_pair_one.wait_recv()
    mixed[...] += dot(hs[0, :, far_cols], a_rows[:, far_cols], 1, 1)
    edge_mixed[...] = dot(hs[0], edge_rows[...], 1, 1)
    wait_halo(1)
    halo_one = read_halo(1)
    edge_agg = ((edge_mixed[...] + dot(halo_one, edge_hm[...])) * edge_inv[0:1, :]).astype(BF)
    edge_mixed[...] = dot(w_self_t, edge_h[0]) + dot(w_neigh_t, edge_agg)
    norm_edge(1)
    agg_ref[0] = ((mixed[...] + dot(halo_one, hmt[:, own_cols])) * inv_ref[0:1, :]).astype(BF)
    norm_forward(
        1, lambda c: dot(w_self_t, hs[0, :, pl.ds(pl.multiple_of(own + c, wide_cols), wide_cols)])
        + dot(w_neigh_t, agg_ref[0, :, c : c + wide_cols]),
    )
    h_pair_two = pair_copy(hs.at[1, :, own_cols], hs.at[1, :, own_cols], 3)
    h_pair_two.start()
    mixed[...] = dot(hs[1, :, own_cols], a_rows[:, own_cols], 1, 1)
    assemble_head()
    h_pair_two.wait_recv()
    mixed[...] += dot(hs[1, :, far_cols], a_rows[:, far_cols], 1, 1)
    wait_halo(2)
    total = mixed[...] + dot(read_halo(2), hmt[:, own_cols])
    agg_ref[1] = (total * inv_ref[0:1, :]).astype(BF)

    logits = dot(head_ws_t[...], hs[1, :, own_cols]) + dot(head_wn_t[...], agg_ref[1])
    class_id = iota((CLS_PAD, half), 0)
    logits = jnp.where(class_id < CLS, logits, -1e30)
    top = jnp.max(logits, axis=0, keepdims=True)
    log_total = top + jnp.log(jnp.sum(jnp.exp(logits - top), axis=0, keepdims=True))
    onehot = class_id == label_in[0:1, own_cols]
    weight = lmask_in[0:1, own_cols].astype(F32)
    chosen = jnp.sum(jnp.where(onehot, logits, 0.0), axis=0, keepdims=True)
    loss_part = jnp.sum((log_total - chosen) * weight, axis=1, keepdims=True)
    pad_rows = grads.shape[1] - rows_all // 8 * 8
    for c in range(2):
        grads[c, rows_all // 8 * 8 :, :] = jnp.broadcast_to(loss_part, (pad_rows, HID))
    probs = jnp.exp(logits - log_total)
    g_logits = (probs - jnp.where(onehot, 1.0, 0.0)) * (weight / label_count)
    g_low[0:CLS_PAD, :] = g_logits.astype(BF)
    g_head = g_low[0:CLS_PAD, :]

    def exchange_backward(k):
        whole = pair_copy(gs_all.at[k, :, own_cols], gs_all.at[k, :, own_cols], 4 + k)
        part_tx[...] = dot(hmt[:, own_cols], gs_all[k, :, own_cols], 1, 1)
        part = pair_copy(part_tx, part_rx.at[k], 8 + k)
        part.start()
        whole.start()
        return whole, part

    def send_back(k, part):
        part.wait()
        pack_halo(3 + k, part_tx[...] + part_rx[k])
        send_halo(3 + k)

    def spread(k, whole, between=None):
        mixed[...] += dot(gs_all[k, :, own_cols], a_rows[:, own_cols])
        if between is not None:
            between()
        whole.wait_recv()
        mixed[...] += dot(gs_all[k, :, far_cols], b_far[...])
        if k == 1:
            norm_slope(0)
        wait_halo(3 + k)
        return read_halo(3 + k)

    def norm_backward(layer, back):
        acc_gain[...] = jnp.zeros_like(acc_gain)
        acc_bias[...] = jnp.zeros_like(acc_bias)

        gain = norm_col[:, 2 * layer : 2 * layer + 1]
        for j in range(n_cols):
            cols = slice(j * wide_cols, (j + 1) * wide_cols)
            n = normed[layer, :, cols]
            own_chunk = pl.ds(pl.multiple_of(own + j * wide_cols, wide_cols), wide_cols)
            g_shift = (mixed[:, cols] + dot(back, sel[:, own_chunk])) * slope[layer, :, cols]
            scaled = g_shift * n
            acc_gain[...] += scaled[:, :LANES] + scaled[:, LANES:]
            acc_bias[...] += g_shift[:, :LANES] + g_shift[:, LANES:]
            gn = g_shift * gain
            mean_one = jnp.mean(gn, axis=0, keepdims=True)
            mean_two = jnp.mean(gn * n, axis=0, keepdims=True)
            g_mixed = (gn - mean_one - n * mean_two) * scale_inv[layer, 0:1, cols]
            g_low[:, cols] = g_mixed.astype(BF)

        gain_row = jnp.sum(acc_gain[...].T, axis=0, keepdims=True)
        bias_row = jnp.sum(acc_bias[...].T, axis=0, keepdims=True)
        base = rows_all - 2 + layer
        for c in range(2):
            piece = slice(c * HALF_HID, (c + 1) * HALF_HID)
            grads[c, base : base + 1, :LANES] = gain_row[:, piece]
            grads[c, base : base + 1, LANES:] = bias_row[:, piece]

    early_start = shard * first_early // HID // 8 * 8
    early_rows = round_up(rows_all + 1, 8) - early_start

    norm_first = rows_all - 2
    top_start = rows_all // 8 * 8

    def stage_one(doms, far_ref):
        loss_row = grads[f, rows_all : rows_all + 1, :] + far_ref[rows_all : rows_all + 1, :]
        row = iota((win, HID), 0)
        for d in doms:
            start = shard * d // HID
            span = slice(start, start + win)
            rows = grads[f, span, :] + far_ref[span, :]
            if d == n_dom - 1:
                rows = jnp.where(row >= norm_first - start, 0.0, rows)
            rows = jnp.where(row == win - 1, loss_row, rows)
            to_high, to_low = d // group, d % group

            @pl.when(low == to_low)
            def _():
                one_rx[to_high, low] = rows

            @pl.when(low != to_low)
            def _():
                one_tx[d] = rows
                pltpu.make_async_remote_copy(
                    src_ref=one_tx.at[d], dst_ref=one_rx.at[to_high, low],
                    send_sem=one_send, recv_sem=one_recv.at[to_high],
                    device_id=(high * group + to_low, f), device_id_type=MESH,
                ).start()

    def top_copy(k, dst, p):
        return pltpu.make_async_remote_copy(
            src_ref=top_tx.at[k], dst_ref=dst, send_sem=top_send.at[k], recv_sem=top_recv.at[k],
            device_id=(p, f), device_id_type=MESH,
        )

    def stage_two(doms):
        for d in doms:
            to_high, to_low = d // group, d % group

            @pl.when(low == to_low)
            def _():
                part = pl.ds(0, group - 1)
                pltpu.make_async_copy(
                    one_rx.at[to_high, part], one_rx.at[to_high, part], one_recv.at[to_high]
                ).wait()
                total = jnp.sum(one_rx[to_high], axis=0)

                @pl.when(high == to_high)
                def _():
                    two_rx[high] = total

                @pl.when(high != to_high)
                def _():
                    two_tx[to_high] = total
                    pltpu.make_async_remote_copy(
                        src_ref=two_tx.at[to_high], dst_ref=two_rx.at[high],
                        send_sem=two_send, recv_sem=two_recv, device_id=(d, f),
                        device_id_type=MESH,
                    ).start()

    gs_all[0, :, own_cols] = (dot(head_wn[:, :CLS_PAD], g_head) * inv_ref[0:1, :]).astype(BF)
    g_pair_two, part_two = exchange_backward(0)
    mixed[...] = dot(head_ws[:, :CLS_PAD], g_head)
    dws = dot(hs[1, :, own_cols], g_head, 1, 1)
    dwn = dot(agg_ref[1], g_head, 1, 1)
    norm_slope(1)
    send_back(0, part_two)
    lane_h = iota((HID, HID), 1)
    for c in range(2):
        piece = slice(c * HALF_HID, (c + 1) * HALF_HID)
        dw_head[...] = jnp.zeros_like(dw_head)
        dw_head[:HALF_HID, :CLS_PAD] = dws[piece]
        dw_head[HALF_HID:, :CLS_PAD] = dwn[piece]
        wide = roll_rows(dw_head[...], start_lane, True)
        low_part = jnp.where(lane_h >= start_lane, wide, 0.0)
        high_part = jnp.where(lane_h >= start_lane, 0.0, wide)
        flat = dot(pick_a, low_part, 0, 0, lax.Precision.HIGHEST) + dot(
            pick_b, high_part, 0, 0, lax.Precision.HIGHEST
        )
        base = 2 * fin + 2 * HALF_HID
        grads[c, base : base + HEAD_ROWS, :] = flat[:HEAD_ROWS]
    back = spread(0, g_pair_two)
    norm_backward(1, back)

    g_one = g_low[...]
    w_self = jnp.concatenate(
        [wmat[0, :LANES], wmat[1, :LANES]], axis=0
    )
    w_neigh = jnp.concatenate(
        [wmat[0, LANES:], wmat[1, LANES:]], axis=0
    )
    gs_all[1, :, own_cols] = (dot(w_neigh, g_one) * inv_ref[0:1, :]).astype(BF)
    g_pair_one, part_one = exchange_backward(1)
    mixed[...] = dot(w_self, g_one)
    dws = dot(hs[0, :, own_cols], g_one, 1, 1)
    dwn = dot(agg_ref[0], g_one, 1, 1)
    for c in range(2):
        piece = slice(c * HALF_HID, (c + 1) * HALF_HID)
        base = 2 * fin
        grads[c, base : base + HALF_HID, :] = dws[piece]
        grads[c, base + HALF_HID : base + 2 * HALF_HID, :] = dwn[piece]

    def early_out():
        early_pair.wait()
        stage_one(range(first_early, n_dom), early_rx)

    early_pair = pair_copy(
        grads.at[other, pl.ds(early_start, early_rows), :],
        early_rx.at[pl.ds(early_start, early_rows), :], 6,
    )
    early_pair.start()
    send_back(1, part_one)
    back = spread(1, g_pair_one, early_out)
    norm_backward(0, back)

    g_zero = g_low[...]
    dws = dot(x_own, g_zero, 1, 1)
    dwn = dot(agg_own, g_zero, 1, 1)
    for c in range(2):
        start = c * FEAT_PAD
        grads[c, 0:fin, :] = dws[start : start + fin]
        grads[c, fin : 2 * fin, :] = dwn[start : start + fin]

    low_rows = pl.ds(0, round_up(shard * (first_early - 1) // HID + win, 8))
    top_rows = pl.ds(top_start, 8)
    late_pairs = [
        pair_copy(grads.at[other, rows, :], late_rx.at[rows, :], k)
        for rows, k in ((low_rows, 12), (top_rows, 13))
    ]
    for copy in late_pairs:
        copy.start()
    stage_two(range(first_early, n_dom))
    for copy in late_pairs:
        copy.wait_recv()
    stage_one(range(first_early), late_rx)
    norms = grads[f, top_rows, :] + late_rx[top_rows, :]
    top_tx[0] = norms

    @pl.when(low == group - 1)
    def _():
        top_one[low] = norms

    @pl.when(low != group - 1)
    def _():
        top_copy(0, top_one.at[low], high * group + group - 1).start()

    stage_two(range(first_early))

    @pl.when(low == group - 1)
    def _():
        part = pl.ds(0, group - 1)
        pltpu.make_async_copy(top_one.at[part], top_one.at[part], top_recv.at[0]).wait()
        norms = jnp.sum(top_one[...], axis=0)
        top_tx[1] = norms

        @pl.when(high == n_high - 1)
        def _():
            top_two[high] = norms

        @pl.when(high != n_high - 1)
        def _():
            top_copy(1, top_two.at[high], n_dom - 1).start()

    part = pl.ds(0, n_high - 1)
    pltpu.make_async_copy(two_rx.at[part], two_rx.at[part], two_recv).wait()

    @pl.when(me == n_dom - 1)
    def _():
        pltpu.make_async_copy(top_two.at[part], top_two.at[part], top_recv.at[1]).wait()
        norms = jnp.sum(top_two[...], axis=0)
        first = norm_first - shard * (n_dom - 1) // HID
        two_rx[0, first : first + 2, :] += norms[norm_first - top_start : norm_first - top_start + 2]

    total = jnp.sum(two_rx[...], axis=0)
    scalar_out[0:1, :] = total[win - 1 : win, :LANES]
    scalar_out[1:2, :] = jnp.broadcast_to(label_count, (1, LANES))
    total = jnp.where(iota((win, HID), 0) == win - 1, 0.0, total)
    flat_t[...] = from_window(total)
    for k in range(-(-shard // LANES)):
        width = min(LANES, shard - k * LANES)
        grad_out[0:1, k * LANES : k * LANES + width] = flat_t[k : k + 1, 0:width]

    for copy in (
        x_pair, h_pair_one, h_pair_two, g_pair_two, g_pair_one,
        *par_urgent, *par_rest, *late_pairs,
    ):
        copy.wait_send()
    for k in range(3, 5):
        wait_halo_sent(k)
    pltpu.make_async_copy(two_tx.at[part], two_tx.at[part], two_send).wait()
    @pl.when(low != group - 1)
    def _():
        pltpu.make_async_copy(top_tx.at[0], top_tx.at[0], top_send.at[0]).wait()

    @pl.when((low == group - 1) & (high != n_high - 1))
    def _():
        pltpu.make_async_copy(top_tx.at[1], top_tx.at[1], top_send.at[1]).wait()

    part = pl.ds(0, n_dom - n_high)
    pltpu.make_async_copy(one_tx.at[part], one_tx.at[part], one_send).wait()
    part = pl.ds(0, (n_dom - 1) * par_rows)
    pltpu.make_async_copy(par_rx.at[f, part, :], par_rx.at[f, part, :], par_send).wait()


def round_up(value, step):
    return -(-value // step) * step


def per_device(n_dom, features, local_mask, halo_mask, send_rows, labels, label_mask, master, first, second):
    nodes, halo = local_mask.shape[1], halo_mask.shape[1]
    half, shard, fin = nodes // 2, master.shape[1], features.shape[1]
    rows_all = n_dom * shard // HID
    span = (shard + HID - 2) // HID + 1
    win = round_up(span + 1, 8)
    par_rows = round_up(span, 16)
    grad_rows = round_up(rows_all + win, 8)
    group = 1
    while (2 * group) ** 2 <= n_dom:
        group *= 2
    head_end = 2 * fin + 2 * HALF_HID + HEAD_ROWS
    first_early = -(-2 * fin * HID // shard)
    assert shard * (n_dom - 1) <= (rows_all - 2) * HID and rows_all % 8 > 2
    urgent = sorted({d // group for d in range(first_early)} | {n_dom // group - 1})
    cfg = dict(
        group=group, first_early=first_early, urgent=urgent,
        n_dom=n_dom, nodes=nodes, half=half, halo=halo, shard=shard, fin=fin, win=win,
        par_rows=par_rows, rows_all=rows_all, grad_rows=grad_rows,
        h_rows=min(nodes, 2**18 // halo), slots=half // LANES if halo <= 256 else 2,
    )
    hbm = pl.BlockSpec(memory_space=pl.ANY)
    vmem = pl.BlockSpec(memory_space=pltpu.VMEM)
    i32 = jnp.int32
    scratch = [
        pltpu.VMEM((8, n_dom), i32),
        pltpu.VMEM((1, nodes), i32),
        pltpu.VMEM((1, nodes), i32),
        pltpu.VMEM((1, shard), F32),
        pltpu.VMEM((cfg["slots"], LANES, nodes), i32),
        pltpu.VMEM((cfg["slots"], LANES, half), i32),
        pltpu.VMEM((cfg["h_rows"], halo), i32),
        pltpu.VMEM((fin, nodes), BF),
        pltpu.VMEM((half, nodes), BF),
        pltpu.VMEM((half, half), BF),
        pltpu.VMEM((halo, nodes), BF),
        pltpu.VMEM((halo, nodes), BF),
        pltpu.VMEM((2 * FEAT_PAD, nodes), BF),
        pltpu.VMEM((2, HID, nodes), BF),
        pltpu.VMEM((2, HID, nodes), BF),
        pltpu.VMEM((2, HID, half), BF),
        pltpu.VMEM((LANES, half), BF),
        pltpu.VMEM((halo, nodes), BF),
        pltpu.VMEM((halo, nodes), BF),
        pltpu.VMEM((halo, halo), BF),
        pltpu.VMEM((LANES, halo), BF),
        pltpu.VMEM((2, HID, halo), BF),
        pltpu.VMEM((HID, halo), F32),
        pltpu.VMEM((8, halo), F32),
        pltpu.VMEM((halo, HID), F32),
        pltpu.VMEM((2, halo, HID), F32),
        pltpu.VMEM((HID, half), F32),
        pltpu.VMEM((2, HID, half), F32),
        pltpu.VMEM((2, HID, half), F32),
        pltpu.VMEM((2, 8, half), F32),
        pltpu.VMEM((8, half), F32),
        pltpu.VMEM((2, n_dom, 16, LANES), BF),
        pltpu.VMEM((5, n_dom, 16, LANES), BF),
        pltpu.VMEM((2 * win, LANES), F32),
        pltpu.VMEM((par_rows, HID), BF),
        pltpu.VMEM((2, n_dom * par_rows, HID), BF),
        pltpu.VMEM((2, HID, HID), BF),
        pltpu.VMEM((2, HID, HID), BF),
        pltpu.VMEM((HID, 8), F32),
        pltpu.VMEM((HID, LANES), BF),
        pltpu.VMEM((HID, LANES), BF),
        pltpu.VMEM((CLS_PAD, HID), BF),
        pltpu.VMEM((CLS_PAD, HID), BF),
        pltpu.VMEM((HID, half), BF),
        pltpu.VMEM((2, grad_rows, HID), F32),
        pltpu.VMEM((grad_rows, HID), F32),
        pltpu.VMEM((grad_rows, HID), F32),
        pltpu.VMEM((n_dom, win, HID), F32),
        pltpu.VMEM((n_dom // group, group, win, HID), F32),
        pltpu.VMEM((n_dom // group, win, HID), F32),
        pltpu.VMEM((n_dom // group, win, HID), F32),
        pltpu.VMEM((2, 8, HID), F32),
        pltpu.VMEM((group, 8, HID), F32),
        pltpu.VMEM((n_dom // group, 8, HID), F32),
        pltpu.VMEM((HID, HID), F32),
        pltpu.VMEM((HID, LANES), F32),
        pltpu.VMEM((HID, LANES), F32),
        pltpu.VMEM((ROW_NORM, n_dom * par_rows), BF),
        pltpu.SemaphoreType.DMA((6 + 2 * cfg["slots"],)),
        pltpu.SemaphoreType.DMA((24,)),
        pltpu.SemaphoreType.DMA((24,)),
        pltpu.SemaphoreType.DMA((5,)),
        pltpu.SemaphoreType.DMA((5,)),
        pltpu.SemaphoreType.DMA,
        pltpu.SemaphoreType.DMA((n_dom // group,)),
        pltpu.SemaphoreType.DMA((n_dom // group,)),
        pltpu.SemaphoreType.DMA,
        pltpu.SemaphoreType.DMA((n_dom // group,)),
        pltpu.SemaphoreType.DMA,
        pltpu.SemaphoreType.DMA,
        pltpu.SemaphoreType.DMA((2,)),
        pltpu.SemaphoreType.DMA((2,)),
    ]
    grad, scalars = pl.pallas_call(
        functools.partial(kernel, cfg),
        out_shape=(
            jax.ShapeDtypeStruct((1, shard), F32),
            jax.ShapeDtypeStruct((2, LANES), F32),
        ),
        in_specs=[hbm] * 7,
        out_specs=(vmem, vmem),
        scratch_shapes=scratch,
        compiler_params=pltpu.CompilerParams(
            collective_id=0, has_side_effects=True, vmem_limit_bytes=63 * 2**20
        ),
    )(
        features.T,
        local_mask,
        halo_mask,
        send_rows[0].T,
        labels.reshape(1, nodes),
        label_mask.reshape(1, nodes),
        master,
    )
    own_grad = grad
    new_first = DECAY_ONE * first + (1.0 - DECAY_ONE) * own_grad
    new_second = DECAY_TWO * second + (1.0 - DECAY_TWO) * own_grad * own_grad
    first_hat = new_first / (1.0 - DECAY_ONE**STEP)
    second_hat = new_second / (1.0 - DECAY_TWO**STEP)
    new_master = master - LEARN_RATE * (
        first_hat / (jnp.sqrt(second_hat) + ADAM_EPS) + WEIGHT_DECAY * master
    )
    return (scalars[0, 0], scalars[1, 0], new_master, new_first, new_second)


def solution(mesh):
    in_specs = (
        P("dom", "feat"),
        P("dom", None),
        P("dom", None),
        P("dom", None, None),
        P("dom"),
        P("dom"),
        P("feat", "dom"),
        P("feat", "dom"),
        P("feat", "dom"),
    )
    out_specs = (P(), P(), P("feat", "dom"), P("feat", "dom"), P("feat", "dom"))
    return jax.shard_map(
        functools.partial(per_device, mesh.shape["dom"]),
        mesh=mesh, in_specs=in_specs, out_specs=out_specs, check_vma=False,
    )
```

```python
import functools

import jax
import jax.numpy as jnp
from jax import lax
from jax.experimental import pallas as pl
from jax.experimental.pallas import tpu as pltpu
from jax.sharding import PartitionSpec as P

HID = 256
CLS = 47
STEP = 10
EPSILON = 1e-05
LEARN_RATE = 0.02
DECAY_ONE = 0.9
DECAY_TWO = 0.999
ADAM_EPS = 1e-08
WEIGHT_DECAY = 0.01

MESH = pl.DeviceIdType.MESH
BF = jnp.bfloat16
F32 = jnp.float32
LANES = 128
CLS_PAD = 64
FEAT_PAD = 64
HALF_HID = HID // 2
ROW_ONE = 2 * FEAT_PAD
ROW_TWO = ROW_ONE + 2 * HALF_HID
HEAD_ROWS = 2 * HALF_HID * CLS // HID
ROW_NORM = ROW_TWO + 48
GELU_A = 0.7978845608028654
GELU_B = 0.044715


def dot(a, b, ca=1, cb=0, precision=None):
    return lax.dot_general(
        a, b, (((ca,), (cb,)), ((), ())), precision=precision, preferred_element_type=F32
    )


def iota(shape, axis):
    return lax.broadcasted_iota(jnp.int32, shape, axis)


def gelu(x):
    half = 0.5 * x
    return half + half * jnp.tanh(x * (GELU_A + (GELU_A * GELU_B) * (x * x)))


def gelu_grad(x):
    xx = x * x
    t = jnp.tanh(x * (GELU_A + (GELU_A * GELU_B) * xx))
    return 0.5 + 0.5 * t + (x * (GELU_A + (3.0 * GELU_A * GELU_B) * xx)) * (0.5 - 0.5 * (t * t))


def roll_rows(x, amount, right):
    for bit in range(7):
        step = 1 << bit
        moved = pltpu.roll(x, step if right else LANES - step, 1)
        x = jnp.where((amount & step) != 0, moved, x)
    return x


def parts(x):
    first = x.astype(BF)
    rest = x - first.astype(F32)
    second = rest.astype(BF)
    return first, second, (rest - second.astype(F32)).astype(BF)


def loop(n, body):
    def step(i, carry):
        body(i)
        return carry

    lax.fori_loop(0, n, step, 0)


def kernel(
    cfg,
    x_in, lm_in, hm_in, send_hbm, label_hbm, lmask_hbm, master_hbm,
    grad_out, scalar_out,
    send_in, label_in, lmask_in, master_in,
    a_stage, b_stage, h_stage, x_stage,
    a_rows, b_far, hmt, sel, xs, hs, gs_all, agg_ref, agg_zero,
    edge_far, edge_hm, edge_x, edge_h, edge_inv, part_tx, part_rx,
    mixed, normed, slope, scale_inv, inv_ref, halo_tx, halo_rx,
    flat_t, par_tx, par_rx, norm_rx, wmat, wmat_t, norm_col, head_ws, head_wn, head_ws_t, head_wn_t,
    g_low, grads, early_rx, late_rx, one_tx, one_rx, two_tx, two_rx, top_tx, top_one, top_two, dw_head, acc_gain, acc_bias, place,
    local_sem, pair_send, pair_recv, halo_send, halo_recv, par_send, column_recv, plane_recv, norm_send, norm_recv,
    one_send, one_recv, two_send, two_recv, top_send, top_recv,
):
    n_dom, nodes, half, halo, shard, fin = (
        cfg["n_dom"], cfg["nodes"], cfg["half"], cfg["halo"], cfg["shard"], cfg["fin"]
    )
    win, par_rows, rows_all = cfg["win"], cfg["par_rows"], cfg["rows_all"]
    me, f = lax.axis_index("dom"), lax.axis_index("feat")
    other = 1 - f
    own = pl.multiple_of(f * half, half)
    far = pl.multiple_of(other * half, half)
    own_cols, far_cols = pl.ds(own, half), pl.ds(far, half)

    group = cfg["group"]
    n_high = n_dom // group
    high, low = me // group, lax.rem(me, group)
    barrier = pltpu.get_barrier_semaphore()

    def greet(p, core):
        pl.semaphore_signal(barrier, inc=1, device_id=(p, core), device_id_type=MESH)

    loop(n_dom - 1, lambda i: greet(lax.rem(me + i + 1, n_dom), f))
    for step in range(group):
        greet(high * group + lax.rem(low + step, group), other)

    chunk = 128
    n_chunk = half // chunk
    x_copy = pltpu.make_async_copy(x_in, x_stage, local_sem.at[4])
    x_copy.start()
    small_copies = [
        pltpu.make_async_copy(src, dst, local_sem.at[k])
        for k, (src, dst) in enumerate(
            ((master_hbm, master_in), (send_hbm, send_in), (label_hbm, label_in),
             (lmask_hbm, lmask_in))
        )
    ]
    for copy in small_copies:
        copy.start()
    h_rows = cfg["h_rows"]

    def h_copy(i):
        return pltpu.make_async_copy(
            hm_in.at[pl.ds(i * h_rows, h_rows), :], h_stage, local_sem.at[5]
        )

    h_copy(0).start()

    slots = cfg["slots"]

    def a_copy(i):
        return pltpu.make_async_copy(
            lm_in.at[pl.ds(pl.multiple_of(own + i * chunk, chunk), chunk), :],
            a_stage.at[lax.rem(i, slots)], local_sem.at[6 + lax.rem(i, slots)],
        )

    def b_copy(i):
        return pltpu.make_async_copy(
            lm_in.at[pl.ds(pl.multiple_of(far + i * chunk, chunk), chunk), own_cols],
            b_stage.at[lax.rem(i, slots)], local_sem.at[6 + slots + lax.rem(i, slots)],
        )

    loop(slots, lambda i: a_copy(i).start())
    loop(slots, lambda i: b_copy(i).start())

    def pair_copy(src, dst, k):
        return pltpu.make_async_remote_copy(
            src_ref=src, dst_ref=dst, send_sem=pair_send.at[k], recv_sem=pair_recv.at[k],
            device_id=(me, other), device_id_type=MESH,
        )

    x_copy.wait()
    slice_rows = pl.ds(pl.multiple_of(f * FEAT_PAD, FEAT_PAD), FEAT_PAD)
    pad_rows = iota((FEAT_PAD, half), 0)
    for c in range(2):
        part = slice(c * half, (c + 1) * half)
        mixed[0:FEAT_PAD, :half] = jnp.where(pad_rows == fin, 1.0, 0.0)
        mixed[0:fin, :half] = x_stage[:, part].astype(F32)
        xs[slice_rows, part] = mixed[0:FEAT_PAD, :half].astype(BF)

    small_copies[1].wait()
    send_rows = send_in[...].astype(F32)
    lane_d = iota(send_rows.shape, 1)
    node_lane = iota((16, nodes), 1).astype(F32)

    def build_sel(q):
        first = jnp.sum(jnp.where(lane_d == 2 * q, send_rows, 0.0), axis=1, keepdims=True)
        second = jnp.sum(jnp.where(lane_d == 2 * q + 1, send_rows, 0.0), axis=1, keepdims=True)
        rows = jnp.concatenate([first, second], axis=0)
        sel[pl.ds(pl.multiple_of(q * 16, 16), 16), :] = jnp.where(
            node_lane == rows, 1.0, 0.0
        ).astype(BF)

    if n_dom <= 16:
        for q in range(n_dom // 2):
            build_sel(q)
    else:
        loop(n_dom // 2, build_sel)

    def halo_copy(k, p):
        return pltpu.make_async_remote_copy(
            src_ref=halo_tx.at[k % 2, p], dst_ref=halo_rx.at[k, me],
            send_sem=halo_send.at[k], recv_sem=halo_recv.at[k],
            device_id=(p, f), device_id_type=MESH,
        )

    def send_halo(k):
        loop(n_dom - 1, lambda i: halo_copy(k, lax.rem(me + i + 1, n_dom)).start())
        halo_rx[k, me] = halo_tx[k % 2, me]

    def pack_halo(k, rows):
        v = rows.reshape(n_dom, 8, HID)
        if k >= 2:
            wait_halo_sent(k - 2)
        halo_tx[k % 2] = jnp.concatenate([v[:, :, :LANES], v[:, :, LANES:]], axis=1).astype(BF)

    def wait_halo(k):
        part = pl.ds(0, n_dom - 1)
        pltpu.make_async_copy(halo_rx.at[k, part], halo_rx.at[k, part], halo_recv.at[k]).wait()

    def wait_halo_sent(k):
        part = pl.ds(0, n_dom - 1)
        pltpu.make_async_copy(
            halo_tx.at[k % 2, part], halo_tx.at[k % 2, part], halo_send.at[k]
        ).wait()

    def read_halo(k):
        v = halo_rx[k].astype(F32)
        rows = jnp.concatenate(
            [v[:, :8, :].reshape(halo, LANES), v[:, 8:, :].reshape(halo, LANES)], axis=1
        )
        return rows.T.astype(BF)

    def build_place(q):
        rows = pl.ds(pl.multiple_of(q * 16, 16), 16)
        r_pad = iota((16, k_all), 0) + q * 16
        k_col = iota((16, k_all), 1)
        owner, inner = k_col // par_rows, lax.rem(k_col, par_rows)
        target = lax.shift_right_logical(owner * shard, 8) + inner
        row_of = jnp.where(
            r_pad < fin, r_pad,
            jnp.where(
                (r_pad >= FEAT_PAD) & (r_pad < FEAT_PAD + fin), r_pad - (FEAT_PAD - fin),
                jnp.where(
                    (r_pad >= ROW_ONE) & (r_pad < ROW_TWO + HEAD_ROWS),
                    r_pad - (ROW_ONE - 2 * fin), -1,
                ),
            ),
        )
        place[rows, :] = jnp.where(row_of == target, 1.0, 0.0).astype(BF)

    k_all = n_dom * par_rows
    loop(ROW_NORM // 16, build_place)
    for i in range(nodes // h_rows):
        h_copy(i).wait()
        hmt[:, i * h_rows : (i + 1) * h_rows] = h_stage[...].astype(F32).T.astype(BF)
        if (i + 1) * h_rows < nodes:
            h_copy(i + 1).start()

    def convert_a(i):
        a_copy(i).wait()
        rows = pl.ds(pl.multiple_of(i * chunk, chunk), chunk)
        a_rows[rows, :] = a_stage[lax.rem(i, slots)].astype(F32).astype(BF)

        @pl.when(i + slots < n_chunk)
        def _():
            a_copy(i + slots).start()

    pl.semaphore_wait(barrier, n_dom - 1 + group)

    x_pair = pair_copy(xs.at[slice_rows, :], xs.at[slice_rows, :], 0)
    x_pair.start()
    off = lax.rem(shard * me, HID)
    off_row, off_lane = off // LANES, lax.rem(off, LANES)
    t_rows = 2 * win
    lane_t = iota((t_rows, LANES), 1)

    def to_window(t):
        r = pltpu.roll(t, off_lane, 1)
        t = jnp.where(lane_t < off_lane, pltpu.roll(r, 1, 0), r)
        t = jnp.where(off_row == 1, pltpu.roll(t, 1, 0), t)
        flat_t[...] = t
        return jnp.concatenate(
            [flat_t[pl.ds(0, win, stride=2), :], flat_t[pl.ds(1, win, stride=2), :]], axis=1
        )

    def from_window(w):
        flat_t[pl.ds(0, win, stride=2), :] = w[:, :LANES]
        flat_t[pl.ds(1, win, stride=2), :] = w[:, LANES:]
        t = flat_t[...]
        t = jnp.where(off_row == 1, pltpu.roll(t, t_rows - 1, 0), t)
        back = lax.rem(LANES - off_lane, LANES)
        near = pltpu.roll(t, back, 1)
        after = pltpu.roll(near, t_rows - 1, 0)
        return jnp.where(lane_t + off_lane < LANES, near, after)

    small_copies[0].wait()
    flat_t[...] = jnp.zeros_like(flat_t)
    for k in range(-(-shard // LANES)):
        width = min(LANES, shard - k * LANES)
        flat_t[k : k + 1, 0:width] = master_in[0:1, k * LANES : k * LANES + width]
    window = to_window(flat_t[...])
    if par_rows > win:
        window = jnp.concatenate([window, jnp.zeros((par_rows - win, HID), F32)], axis=0)
    par_tx[...] = window.astype(BF)
    par_rx[f, pl.ds(pl.multiple_of(me * par_rows, par_rows), par_rows), :] = par_tx[...]


    urgent = cfg["urgent"]
    patient = [h for h in range(n_high) if h not in urgent]

    def par_slot(h, w):
        start = pl.multiple_of((h * group + w) * par_rows, par_rows)
        return par_rx.at[f, pl.ds(start, par_rows), :]

    def send_to(p, core, src, dst, send_sem, recv_sem):
        pltpu.make_async_remote_copy(
            src_ref=src, dst_ref=dst, send_sem=send_sem, recv_sem=recv_sem,
            device_id=(p, core), device_id_type=MESH,
        ).start()

    def to_plane(src, dst, send_sem, recv_sem, both):
        if both:
            send_to(me, other, src, dst, send_sem, recv_sem)
        for step in range(1, group):
            p = high * group + lax.rem(low + step, group)
            send_to(p, f, src, dst, send_sem, recv_sem)
            if both:
                send_to(p, other, src, dst, send_sem, recv_sem)

    def to_column(src, dst, send_sem, recv_sem):
        for step in range(1, n_high):
            p = lax.rem(high + step, n_high) * group + low
            send_to(p, f, src, dst, send_sem, recv_sem)

    def any_of(which):
        return functools.reduce(jnp.logical_or, [high == h for h in which])

    def own_params(which):
        @pl.when(any_of(which))
        def _():
            to_plane(
                par_tx, par_slot(high, low), par_send, plane_recv.at[high], which is urgent
            )

    def forward_params(which):
        for h in which:
            @pl.when(high != h)
            def _():
                pltpu.make_async_copy(par_tx, par_tx, column_recv.at[h]).wait()
                to_plane(
                    par_slot(h, low), par_slot(h, low), par_send, plane_recv.at[h],
                    which is urgent,
                )

    def wait_params(which):
        part = pl.ds(0, (2 * group - 1 if which is urgent else group - 1) * par_rows)
        for h in which:
            pltpu.make_async_copy(
                par_rx.at[f, part, :], par_rx.at[f, part, :], plane_recv.at[h]
            ).wait()

    norm_local = rows_all - 2 - shard * (n_dom - 1) // HID
    norm_block = norm_local // 16 * 16
    norm_own = norm_rx.at[f]
    last_low = low == group - 1

    def send_norms():
        @pl.when(me == n_dom - 1)
        def _():
            norm_rx[f] = par_tx[norm_block : norm_block + 16, :]
            to_column(norm_own, norm_own, norm_send.at[0], norm_recv.at[0])

    def forward_norms():
        @pl.when(last_low)
        def _():
            @pl.when(high != n_high - 1)
            def _():
                pltpu.make_async_copy(norm_own, norm_own, norm_recv.at[0]).wait()

            to_plane(norm_own, norm_own, norm_send.at[1], norm_recv.at[1], True)

    def wait_norms():
        @pl.when(last_low)
        def _():
            pltpu.make_async_copy(norm_own, norm_own, norm_recv.at[1]).wait()

        @pl.when(jnp.logical_not(last_low))
        def _():
            pltpu.make_async_copy(norm_rx, norm_rx, norm_recv.at[1]).wait()

    def par_pairs(which, k):
        runs = []
        for h in which:
            if runs and runs[-1][1] == h:
                runs[-1][1] = h + 1
            else:
                runs.append([h, h + 1])
        copies = []
        for i, (start, end) in enumerate(runs):
            part = pl.ds(start * group * par_rows, (end - start) * group * par_rows)
            copies.append(pair_copy(par_rx.at[f, part, :], par_rx.at[f, part, :], k + i))
        return copies

    first_early = cfg["first_early"]
    to_column(par_tx, par_slot(high, low), par_send, column_recv.at[high])
    own_params(urgent)
    send_norms()
    loop(n_chunk, convert_a)
    edge_hm[...] = dot(hmt[...], sel[...], 1, 1).astype(BF)

    def edge_chunk(q):
        rows = pl.ds(pl.multiple_of(q * LANES, LANES), LANES)
        a_rows[pl.ds(pl.multiple_of(half + q * LANES, LANES), LANES), :] = dot(
            sel[rows, own_cols], a_rows[:half, :]
        ).astype(BF)

    loop(halo // LANES, edge_chunk)
    edge_pair = pair_copy(a_rows.at[pl.ds(half, halo), :], edge_far, 7)
    edge_pair.start()
    x_pair.wait_recv()
    picked = dot(sel[...], xs[...], 1, 1)
    edge_x[...] = picked.T.astype(BF)
    picked = picked.reshape(n_dom, 8, LANES)
    small_copies[2].wait()
    small_copies[3].wait()
    count = jnp.sum(lmask_in[...].astype(F32), axis=1, keepdims=True)
    count_high = jnp.floor(count * (1.0 / 256.0))
    count_low = count - 256.0 * count_high
    count_row = iota((8, LANES), 0)
    counts = jnp.where(count_row == 0, count_high, jnp.where(count_row == 1, count_low, 0.0))
    counts = jnp.broadcast_to(counts[None], (n_dom, 8, LANES))
    halo_tx[0] = jnp.concatenate([picked, counts], axis=1).astype(BF)
    send_halo(0)

    forward_params(urgent)
    forward_norms()
    own_params(patient)
    forward_params(patient)
    mixed[0:LANES, :half] = dot(xs[...], a_rows[:half, :], 1, 1)
    def convert_b(i):
        b_copy(i).wait()
        rows = pl.ds(pl.multiple_of(i * chunk, chunk), chunk)
        b_far[rows, :] = b_stage[lax.rem(i, slots)].astype(F32).astype(BF)

        @pl.when(i + slots < n_chunk)
        def _():
            b_copy(i + slots).start()

    loop(n_chunk, convert_b)

    edge_pair.wait()

    def edge_sum(q):
        rows = pl.ds(pl.multiple_of(q * LANES, LANES), LANES)
        ext = pl.ds(pl.multiple_of(half + q * LANES, LANES), LANES)
        a_rows[ext, :] = a_rows[ext, :] + edge_far[rows, :]

    loop(halo // LANES, edge_sum)
    mixed[0:LANES, half : half + halo] = dot(xs[...], a_rows[half:, :], 1, 1)
    wait_params(urgent)
    wait_norms()
    wait_halo(0)
    arrived = halo_rx[0].astype(F32)
    halo_zero = arrived[:, :8, :].reshape(halo, LANES).T.astype(BF)
    count_all = jnp.sum(arrived[:, 8:, :], axis=0)
    label_count = 256.0 * count_all[0:1, 0:1] + count_all[1:2, 0:1]
    k_first = first_early * par_rows
    w_zero = []
    for c in range(2):
        rows_t = dot(place[:ROW_ONE, :k_first], par_rx[c, :k_first, :]).T
        w_zero.append(rows_t.astype(BF))
        norms_t = jnp.concatenate(
            [norm_rx[c].astype(F32), jnp.zeros((LANES - 16, HID), F32)], axis=0
        ).T
        for k in range(2):
            lane = norm_local - norm_block + k
            col = norms_t[:, lane : lane + 1]
            norm_col[c * HALF_HID : (c + 1) * HALF_HID, 2 * k : 2 * k + 1] = col[:HALF_HID]
            norm_col[c * HALF_HID : (c + 1) * HALF_HID, 2 * k + 1 : 2 * k + 2] = col[HALF_HID:]
    w_zero = jnp.concatenate(w_zero, axis=1)

    def assemble_hidden():
        for c in range(2):
            rows = dot(place[ROW_ONE:ROW_TWO, :], par_rx[c])
            wmat[c] = rows.astype(BF)
            wmat_t[c] = rows.T.astype(BF)

    place_row = iota((2 * 48, HID), 0)
    flat_row = jnp.where(place_row < 48, 2 * place_row, 2 * (place_row - 48) + 1)
    first_row = lax.shift_right_logical(iota((2 * 48, HID), 1) * CLS, 7)
    pick_a = jnp.where(flat_row == first_row, 1.0, 0.0).astype(BF)
    pick_b = jnp.where(flat_row == first_row + 1, 1.0, 0.0).astype(BF)
    start_lane = (iota((HID, LANES), 0) * CLS) & (LANES - 1)
    lane_w = iota((HID, LANES), 1)

    def assemble_head():
        for c in range(2):
            flat = dot(place[ROW_TWO:ROW_NORM, :], par_rx[c]).astype(BF)
            flat = jnp.concatenate([flat[:, :LANES], flat[:, LANES:]], axis=0)
            wide = jnp.where(lane_w >= start_lane, dot(pick_a, flat, 0, 0), dot(pick_b, flat, 0, 0))
            head = jnp.where(lane_w < CLS, roll_rows(wide, start_lane, False), 0.0)
            head_t = head.T[:CLS_PAD]
            half_rows = slice(c * HALF_HID, (c + 1) * HALF_HID)
            head_ws[half_rows, :] = head[:HALF_HID].astype(BF)
            head_wn[half_rows, :] = head[HALF_HID:].astype(BF)
            head_ws_t[:, half_rows] = head_t[:, :HALF_HID].astype(BF)
            head_wn_t[:, half_rows] = head_t[:, HALF_HID:].astype(BF)

    wide_cols = 256
    n_cols = half // wide_cols

    def norm_apply(x, layer):
        centre = x - jnp.mean(x, axis=0, keepdims=True)
        rs = lax.rsqrt(jnp.mean(centre * centre, axis=0, keepdims=True) + EPSILON)
        n = centre * rs
        shifted = n * norm_col[:, 2 * layer : 2 * layer + 1] + norm_col[
            :, 2 * layer + 1 : 2 * layer + 2
        ]
        return n, rs, gelu(shifted).astype(BF)

    def norm_forward(layer, mix):
        for j in range(n_cols):
            cols = slice(j * wide_cols, (j + 1) * wide_cols)
            n, rs, value = norm_apply(mix(j * wide_cols), layer)
            normed[layer, :, cols] = n
            scale_inv[layer, :, cols] = jnp.broadcast_to(rs, (8, wide_cols))
            out = pl.ds(pl.multiple_of(own + j * wide_cols, wide_cols), wide_cols)
            hs[layer, :, out] = value

    def norm_slope(layer):
        def body(i):
            for j in range(2):
                cols = pl.ds(pl.multiple_of((2 * i + j) * LANES, LANES), LANES)
                shifted = normed[layer, :, cols] * norm_col[
                    :, 2 * layer : 2 * layer + 1
                ] + norm_col[:, 2 * layer + 1 : 2 * layer + 2]
                slope[layer, :, cols] = gelu_grad(shifted)

        loop(half // (2 * LANES), body)

    def norm_edge(layer, mix):
        for j in range(halo // LANES):
            cols = slice(j * LANES, (j + 1) * LANES)
            edge_h[layer, :, cols] = norm_apply(mix(cols), layer)[2]

        pack_halo(1 + layer, edge_h[layer].astype(F32).T)
        send_halo(1 + layer)

    def rows_of(x, agg):
        return jnp.concatenate([x[:FEAT_PAD], agg[:FEAT_PAD], x[FEAT_PAD:], agg[FEAT_PAD:]], axis=0)

    def aggregate_zero(summed, inv_at, cols):
        inverse = 1.0 / jnp.maximum(summed[fin : fin + 1, :], 1.0)
        inv_at[:, cols] = jnp.broadcast_to(inverse, (8, summed.shape[1]))
        return (summed * inverse).astype(BF)

    def shifted_cols(cols):
        return slice(half + cols.start, half + cols.stop)

    def own_chunk(c):
        return pl.ds(pl.multiple_of(own + c, wide_cols), wide_cols)

    def mix_edge_zero(cols):
        agg = aggregate_zero(
            mixed[0:LANES, shifted_cols(cols)] + dot(halo_zero, edge_hm[:, cols]), edge_inv, cols
        )
        return dot(w_zero, rows_of(edge_x[:, cols], agg))

    def mix_zero(c):
        cols = slice(c, c + wide_cols)
        agg = aggregate_zero(
            mixed[0:LANES, cols] + dot(halo_zero, hmt[:, own_chunk(c)]), inv_ref, cols
        )
        agg_zero[:, cols] = agg
        return dot(w_zero, rows_of(xs[:, own_chunk(c)], agg))

    norm_edge(0, mix_edge_zero)
    wait_params(patient)
    par_rest = par_pairs(patient, 20)
    for copy in par_rest:
        copy.start()
    norm_forward(0, mix_zero)
    h_pair_one = pair_copy(hs.at[0, :, own_cols], hs.at[0, :, own_cols], 2)
    h_pair_one.start()
    mixed[:, : half + halo] = dot(hs[0, :, own_cols], a_rows[:, own_cols], 1, 1)
    for copy in par_rest:
        copy.wait_recv()
    assemble_hidden()
    w_self_t = jnp.concatenate([wmat_t[0, :, :LANES], wmat_t[1, :, :LANES]], axis=1)
    w_neigh_t = jnp.concatenate([wmat_t[0, :, LANES:], wmat_t[1, :, LANES:]], axis=1)
    h_pair_one.wait_recv()
    mixed[:, : half + halo] += dot(hs[0, :, far_cols], a_rows[:, far_cols], 1, 1)
    wait_halo(1)
    halo_one = read_halo(1)

    def mix_edge_one(cols):
        summed = mixed[:, shifted_cols(cols)] + dot(halo_one, edge_hm[:, cols])
        agg = (summed * edge_inv[0:1, cols]).astype(BF)
        return dot(w_self_t, edge_h[0, :, cols]) + dot(w_neigh_t, agg)

    def mix_one(c):
        return dot(w_self_t, hs[0, :, own_chunk(c)]) + dot(
            w_neigh_t, agg_ref[0, :, c : c + wide_cols]
        )

    norm_edge(1, mix_edge_one)
    total = mixed[:, :half] + dot(halo_one, hmt[:, own_cols])
    agg_ref[0] = (total * inv_ref[0:1, :]).astype(BF)
    norm_forward(1, mix_one)
    h_pair_two = pair_copy(hs.at[1, :, own_cols], hs.at[1, :, own_cols], 3)
    h_pair_two.start()
    mixed[:, :half] = dot(hs[1, :, own_cols], a_rows[:half, own_cols], 1, 1)
    assemble_head()
    h_pair_two.wait_recv()
    mixed[:, :half] += dot(hs[1, :, far_cols], a_rows[:half, far_cols], 1, 1)
    wait_halo(2)
    halo_two = read_halo(2)
    for c in range(0, half, wide_cols):
        cols = slice(c, c + wide_cols)
        total = mixed[:, cols] + dot(halo_two, hmt[:, own_chunk(c)])
        agg_ref[1, :, cols] = (total * inv_ref[0:1, cols]).astype(BF)

    logits = dot(head_ws_t[...], hs[1, :, own_cols]) + dot(head_wn_t[...], agg_ref[1])
    class_id = iota((CLS_PAD, half), 0)
    logits = jnp.where(class_id < CLS, logits, -1e30)
    top = jnp.max(logits, axis=0, keepdims=True)
    log_total = top + jnp.log(jnp.sum(jnp.exp(logits - top), axis=0, keepdims=True))
    onehot = class_id == label_in[0:1, own_cols]
    weight = lmask_in[0:1, own_cols].astype(F32)
    chosen = jnp.sum(jnp.where(onehot, logits, 0.0), axis=0, keepdims=True)
    loss_part = jnp.sum((log_total - chosen) * weight, axis=1, keepdims=True)
    pad_rows = grads.shape[1] - rows_all // 8 * 8
    for c in range(2):
        grads[c, rows_all // 8 * 8 :, :] = jnp.broadcast_to(loss_part, (pad_rows, HID))
    probs = jnp.exp(logits - log_total)
    g_logits = (probs - jnp.where(onehot, 1.0, 0.0)) * (weight / label_count)
    g_low[0:CLS_PAD, :] = g_logits.astype(BF)
    g_head = g_low[0:CLS_PAD, :]

    def exchange_backward(k):
        whole = pair_copy(gs_all.at[k, :, own_cols], gs_all.at[k, :, own_cols], 4 + k)
        part_tx[...] = dot(hmt[:, own_cols], gs_all[k, :, own_cols], 1, 1)
        part = pair_copy(part_tx, part_rx.at[k], 8 + k)
        part.start()
        return whole, part

    def send_back(k, part, whole):
        part.wait()
        pack_halo(3 + k, part_tx[...] + part_rx[k])
        send_halo(3 + k)
        whole.start()

    def spread(k, whole, base):
        mixed[:, :half] = dot(gs_all[k, :, own_cols], a_rows[:half, own_cols])
        if k == 1:
            norm_slope(0)
        whole.wait_recv()
        mixed[:, half : 2 * half] = dot(gs_all[k, :, far_cols], b_far[...])
        mixed[:, :half] = mixed[:, :half] + mixed[:, half : 2 * half] + base()
        wait_halo(3 + k)
        return read_halo(3 + k)

    def norm_backward(layer, back, after=None):
        acc_gain[...] = jnp.zeros_like(acc_gain)
        acc_bias[...] = jnp.zeros_like(acc_bias)

        gain = norm_col[:, 2 * layer : 2 * layer + 1]
        for j in range(n_cols):
            cols = slice(j * wide_cols, (j + 1) * wide_cols)
            n = normed[layer, :, cols]
            through = mixed[:, cols] + dot(back, sel[:, own_chunk(j * wide_cols)])
            g_shift = through * slope[layer, :, cols]
            scaled = g_shift * n
            acc_gain[...] += scaled[:, :LANES] + scaled[:, LANES:]
            acc_bias[...] += g_shift[:, :LANES] + g_shift[:, LANES:]
            gn = g_shift * gain
            mean_one = jnp.mean(gn, axis=0, keepdims=True)
            mean_two = jnp.mean(gn * n, axis=0, keepdims=True)
            g_mixed = (gn - mean_one - n * mean_two) * scale_inv[layer, 0:1, cols]
            g_chunk = g_mixed.astype(BF)
            g_low[:, cols] = g_chunk
            if after is not None:
                after(cols, own_chunk(j * wide_cols), g_chunk)

        gain_row = jnp.sum(acc_gain[...].T, axis=0, keepdims=True)
        bias_row = jnp.sum(acc_bias[...].T, axis=0, keepdims=True)
        base = rows_all - 2 + layer
        for c in range(2):
            piece = slice(c * HALF_HID, (c + 1) * HALF_HID)
            grads[c, base : base + 1, :LANES] = gain_row[:, piece]
            grads[c, base : base + 1, LANES:] = bias_row[:, piece]

    early_start = shard * first_early // HID // 8 * 8
    early_rows = round_up(rows_all + 1, 8) - early_start

    norm_first = rows_all - 2
    top_start = rows_all // 8 * 8

    def stage_one(doms, far_ref):
        loss_row = grads[f, rows_all : rows_all + 1, :] + far_ref[rows_all : rows_all + 1, :]
        row = iota((win, HID), 0)
        for d in doms:
            start = shard * d // HID
            span = slice(start, start + win)
            rows = grads[f, span, :] + far_ref[span, :]
            if d == n_dom - 1:
                rows = jnp.where(row >= norm_first - start, 0.0, rows)
            rows = jnp.where(row == win - 1, loss_row, rows)
            to_high, to_low = d // group, d % group

            @pl.when(low == to_low)
            def _():
                one_rx[to_high, low] = rows

            @pl.when(low != to_low)
            def _():
                one_tx[d] = rows
                pltpu.make_async_remote_copy(
                    src_ref=one_tx.at[d], dst_ref=one_rx.at[to_high, low],
                    send_sem=one_send, recv_sem=one_recv.at[to_high],
                    device_id=(high * group + to_low, f), device_id_type=MESH,
                ).start()

    def top_copy(k, dst, p):
        return pltpu.make_async_remote_copy(
            src_ref=top_tx.at[k], dst_ref=dst, send_sem=top_send.at[k], recv_sem=top_recv.at[k],
            device_id=(p, f), device_id_type=MESH,
        )

    def stage_two(doms):
        for d in doms:
            to_high, to_low = d // group, d % group

            @pl.when(low == to_low)
            def _():
                part = pl.ds(0, group - 1)
                pltpu.make_async_copy(
                    one_rx.at[to_high, part], one_rx.at[to_high, part], one_recv.at[to_high]
                ).wait()
                total = jnp.sum(one_rx[to_high], axis=0)

                @pl.when(high == to_high)
                def _():
                    two_rx[high] = total

                @pl.when(high != to_high)
                def _():
                    two_tx[to_high] = total
                    pltpu.make_async_remote_copy(
                        src_ref=two_tx.at[to_high], dst_ref=two_rx.at[high],
                        send_sem=two_send, recv_sem=two_recv, device_id=(d, f),
                        device_id_type=MESH,
                    ).start()

    gs_all[0, :, own_cols] = (dot(head_wn[:, :CLS_PAD], g_head) * inv_ref[0:1, :]).astype(BF)
    g_pair_two, part_two = exchange_backward(0)
    dws = dot(hs[1, :, own_cols], g_head, 1, 1)
    dwn = dot(agg_ref[1], g_head, 1, 1)
    norm_slope(1)
    send_back(0, part_two, g_pair_two)
    dw_head[...] = jnp.zeros_like(dw_head)
    for c in range(2):
        piece = slice(c * HALF_HID, (c + 1) * HALF_HID)
        dw_head[:HALF_HID, :CLS_PAD] = dws[piece]
        dw_head[HALF_HID:, :CLS_PAD] = dwn[piece]
        wide = roll_rows(dw_head[...], start_lane, True)
        low_part = jnp.where(lane_w >= start_lane, wide, 0.0)
        high_part = jnp.where(lane_w >= start_lane, 0.0, wide)
        stacked = jnp.concatenate([*parts(low_part), *parts(high_part)], axis=0)
        picks = jnp.concatenate([pick_a] * 3 + [pick_b] * 3, axis=1)
        flat = dot(picks, stacked)
        flat = jnp.concatenate([flat[:48], flat[48:]], axis=1)
        base = 2 * fin + 2 * HALF_HID
        grads[c, base : base + HEAD_ROWS, :] = flat[:HEAD_ROWS]
    back = spread(0, g_pair_two, lambda: dot(head_ws[:, :CLS_PAD], g_head))
    w_self = jnp.concatenate([wmat[0, :LANES], wmat[1, :LANES]], axis=0)
    w_neigh = jnp.concatenate([wmat[0, LANES:], wmat[1, LANES:]], axis=0)

    def through_one(cols, own_part, g):
        gs_all[1, :, own_part] = (dot(w_neigh, g) * inv_ref[0:1, cols]).astype(BF)

    norm_backward(1, back, through_one)

    g_pair_one, part_one = exchange_backward(1)
    g_one = g_low[...]
    dws = dot(hs[0, :, own_cols], g_one, 1, 1)
    dwn = dot(agg_ref[0], g_one, 1, 1)
    for c in range(2):
        piece = slice(c * HALF_HID, (c + 1) * HALF_HID)
        base = 2 * fin
        grads[c, base : base + HALF_HID, :] = dws[piece]
        grads[c, base + HALF_HID : base + 2 * HALF_HID, :] = dwn[piece]

    def early_out():
        early_pair.wait()
        stage_one(range(first_early, n_dom), early_rx)

    early_pair = pair_copy(
        grads.at[other, pl.ds(early_start, early_rows), :],
        early_rx.at[pl.ds(early_start, early_rows), :], 6,
    )
    early_pair.start()
    send_back(1, part_one, g_pair_one)
    early_out()
    back = spread(1, g_pair_one, lambda: dot(w_self, g_low[...]))
    norm_backward(0, back)

    g_zero = g_low[...]
    dws = dot(xs[:, own_cols], g_zero, 1, 1)
    dwn = dot(agg_zero[...], g_zero, 1, 1)
    for c in range(2):
        start = c * FEAT_PAD
        grads[c, 0:fin, :] = dws[start : start + fin]
        grads[c, fin : 2 * fin, :] = dwn[start : start + fin]

    low_rows = pl.ds(0, round_up(shard * (first_early - 1) // HID + win, 8))
    top_rows = pl.ds(top_start, 8)
    late_pairs = [
        pair_copy(grads.at[other, rows, :], late_rx.at[rows, :], k)
        for rows, k in ((low_rows, 12), (top_rows, 13))
    ]
    for copy in late_pairs:
        copy.start()
    for copy in late_pairs:
        copy.wait_recv()
    stage_one(range(first_early), late_rx)
    norms = grads[f, top_rows, :] + late_rx[top_rows, :]
    top_tx[0] = norms

    @pl.when(low == group - 1)
    def _():
        top_one[low] = norms

    @pl.when(low != group - 1)
    def _():
        top_copy(0, top_one.at[low], high * group + group - 1).start()

    stage_two(range(first_early, n_dom))
    stage_two(range(first_early))

    @pl.when(low == group - 1)
    def _():
        part = pl.ds(0, group - 1)
        pltpu.make_async_copy(top_one.at[part], top_one.at[part], top_recv.at[0]).wait()
        norms = jnp.sum(top_one[...], axis=0)
        top_tx[1] = norms

        @pl.when(high == n_high - 1)
        def _():
            top_two[high] = norms

        @pl.when(high != n_high - 1)
        def _():
            top_copy(1, top_two.at[high], n_dom - 1).start()

    part = pl.ds(0, n_high - 1)
    pltpu.make_async_copy(two_rx.at[part], two_rx.at[part], two_recv).wait()

    @pl.when(me == n_dom - 1)
    def _():
        pltpu.make_async_copy(top_two.at[part], top_two.at[part], top_recv.at[1]).wait()
        norms = jnp.sum(top_two[...], axis=0)
        first = norm_first - shard * (n_dom - 1) // HID
        two_rx[0, first : first + 2, :] += norms[norm_first - top_start : norm_first - top_start + 2]

    total = jnp.sum(two_rx[...], axis=0)
    scalar_out[0:1, :] = total[win - 1 : win, :LANES]
    scalar_out[1:2, :] = jnp.broadcast_to(label_count, (1, LANES))
    total = jnp.where(iota((win, HID), 0) == win - 1, 0.0, total)
    flat_t[...] = from_window(total)
    for k in range(-(-shard // LANES)):
        width = min(LANES, shard - k * LANES)
        grad_out[0:1, k * LANES : k * LANES + width] = flat_t[k : k + 1, 0:width]

    for copy in (
        x_pair, h_pair_one, h_pair_two, g_pair_two, g_pair_one,
        *par_rest, *late_pairs,
    ):
        copy.wait_send()
    for k in range(3, 5):
        wait_halo_sent(k)
    pltpu.make_async_copy(two_tx.at[part], two_tx.at[part], two_send).wait()
    @pl.when(low != group - 1)
    def _():
        pltpu.make_async_copy(top_tx.at[0], top_tx.at[0], top_send.at[0]).wait()

    @pl.when((low == group - 1) & (high != n_high - 1))
    def _():
        pltpu.make_async_copy(top_tx.at[1], top_tx.at[1], top_send.at[1]).wait()

    part = pl.ds(0, n_dom - n_high)
    pltpu.make_async_copy(one_tx.at[part], one_tx.at[part], one_send).wait()
    n_sent = n_high - 1 + len(urgent) * (2 * group - 1) + len(patient) * (group - 1)
    while n_sent > 0:
        part = pl.ds(0, min(n_sent, n_dom) * par_rows)
        pltpu.make_async_copy(par_rx.at[f, part, :], par_rx.at[f, part, :], par_send).wait()
        n_sent -= n_dom

    @pl.when(me == n_dom - 1)
    def _():
        for step in range(1, n_high):
            pltpu.make_async_copy(norm_own, norm_own, norm_send.at[0]).wait()

    @pl.when(last_low)
    def _():
        for step in range(2 * group - 1):
            pltpu.make_async_copy(norm_own, norm_own, norm_send.at[1]).wait()


def round_up(value, step):
    return -(-value // step) * step


def per_device(n_dom, features, local_mask, halo_mask, send_rows, labels, label_mask, master, first, second):
    nodes, halo = local_mask.shape[1], halo_mask.shape[1]
    half, shard, fin = nodes // 2, master.shape[1], features.shape[1]
    rows_all = n_dom * shard // HID
    span = (shard + HID - 2) // HID + 1
    win = round_up(span + 1, 8)
    par_rows = round_up(span, 16)
    grad_rows = round_up(rows_all + win, 8)
    group = 1
    while (2 * group) ** 2 <= n_dom:
        group *= 2
    head_end = 2 * fin + 2 * HALF_HID + HEAD_ROWS
    first_early = -(-2 * fin * HID // shard)
    assert shard * (n_dom - 1) <= (rows_all - 2) * HID and rows_all % 8 > 2
    urgent = sorted({d // group for d in range(first_early)})
    cfg = dict(
        group=group, first_early=first_early, urgent=urgent,
        n_dom=n_dom, nodes=nodes, half=half, halo=halo, shard=shard, fin=fin, win=win,
        par_rows=par_rows, rows_all=rows_all, grad_rows=grad_rows,
        h_rows=nodes if halo <= 256 else LANES, slots=half // LANES if halo <= 256 else 2,
    )
    hbm = pl.BlockSpec(memory_space=pl.ANY)
    vmem = pl.BlockSpec(memory_space=pltpu.VMEM)
    i32 = jnp.int32
    scratch = [
        pltpu.VMEM((8, n_dom), i32),
        pltpu.VMEM((1, nodes), i32),
        pltpu.VMEM((1, nodes), i32),
        pltpu.VMEM((1, shard), F32),
        pltpu.VMEM((cfg["slots"], LANES, nodes), i32),
        pltpu.VMEM((cfg["slots"], LANES, half), i32),
        pltpu.VMEM((cfg["h_rows"], halo), i32),
        pltpu.VMEM((fin, nodes), BF),
        pltpu.VMEM((half + halo, nodes), BF),
        pltpu.VMEM((half, half), BF),
        pltpu.VMEM((halo, nodes), BF),
        pltpu.VMEM((halo, nodes), BF),
        pltpu.VMEM((2 * FEAT_PAD, nodes), BF),
        pltpu.VMEM((2, HID, nodes), BF),
        pltpu.VMEM((2, HID, nodes), BF),
        pltpu.VMEM((2, HID, half), BF),
        pltpu.VMEM((LANES, half), BF),
        pltpu.VMEM((halo, nodes), BF),
        pltpu.VMEM((halo, halo), BF),
        pltpu.VMEM((LANES, halo), BF),
        pltpu.VMEM((2, HID, halo), BF),
        pltpu.VMEM((8, halo), F32),
        pltpu.VMEM((halo, HID), F32),
        pltpu.VMEM((2, halo, HID), F32),
        pltpu.VMEM((HID, half + max(halo, half)), F32),
        pltpu.VMEM((2, HID, half), F32),
        pltpu.VMEM((2, HID, half), F32),
        pltpu.VMEM((2, 8, half), F32),
        pltpu.VMEM((8, half), F32),
        pltpu.VMEM((2, n_dom, 16, LANES), BF),
        pltpu.VMEM((5, n_dom, 16, LANES), BF),
        pltpu.VMEM((2 * win, LANES), F32),
        pltpu.VMEM((par_rows, HID), BF),
        pltpu.VMEM((2, n_dom * par_rows, HID), BF),
        pltpu.VMEM((2, 16, HID), BF),
        pltpu.VMEM((2, HID, HID), BF),
        pltpu.VMEM((2, HID, HID), BF),
        pltpu.VMEM((HID, 8), F32),
        pltpu.VMEM((HID, LANES), BF),
        pltpu.VMEM((HID, LANES), BF),
        pltpu.VMEM((CLS_PAD, HID), BF),
        pltpu.VMEM((CLS_PAD, HID), BF),
        pltpu.VMEM((HID, half), BF),
        pltpu.VMEM((2, grad_rows, HID), F32),
        pltpu.VMEM((grad_rows, HID), F32),
        pltpu.VMEM((grad_rows, HID), F32),
        pltpu.VMEM((n_dom, win, HID), F32),
        pltpu.VMEM((n_dom // group, group, win, HID), F32),
        pltpu.VMEM((n_dom // group, win, HID), F32),
        pltpu.VMEM((n_dom // group, win, HID), F32),
        pltpu.VMEM((2, 8, HID), F32),
        pltpu.VMEM((group, 8, HID), F32),
        pltpu.VMEM((n_dom // group, 8, HID), F32),
        pltpu.VMEM((HID, LANES), F32),
        pltpu.VMEM((HID, LANES), F32),
        pltpu.VMEM((HID, LANES), F32),
        pltpu.VMEM((ROW_NORM, n_dom * par_rows), BF),
        pltpu.SemaphoreType.DMA((6 + 2 * cfg["slots"],)),
        pltpu.SemaphoreType.DMA((24,)),
        pltpu.SemaphoreType.DMA((24,)),
        pltpu.SemaphoreType.DMA((5,)),
        pltpu.SemaphoreType.DMA((5,)),
        pltpu.SemaphoreType.DMA,
        pltpu.SemaphoreType.DMA((n_dom // group,)),
        pltpu.SemaphoreType.DMA((n_dom // group,)),
        pltpu.SemaphoreType.DMA((2,)),
        pltpu.SemaphoreType.DMA((2,)),
        pltpu.SemaphoreType.DMA,
        pltpu.SemaphoreType.DMA((n_dom // group,)),
        pltpu.SemaphoreType.DMA,
        pltpu.SemaphoreType.DMA,
        pltpu.SemaphoreType.DMA((2,)),
        pltpu.SemaphoreType.DMA((2,)),
    ]
    grad, scalars = pl.pallas_call(
        functools.partial(kernel, cfg),
        out_shape=(
            jax.ShapeDtypeStruct((1, shard), F32),
            jax.ShapeDtypeStruct((2, LANES), F32),
        ),
        in_specs=[hbm] * 7,
        out_specs=(vmem, vmem),
        scratch_shapes=scratch,
        compiler_params=pltpu.CompilerParams(
            collective_id=0, has_side_effects=True, vmem_limit_bytes=63 * 2**20
        ),
    )(
        features.T,
        local_mask,
        halo_mask,
        send_rows[0].T,
        labels.reshape(1, nodes),
        label_mask.reshape(1, nodes),
        master,
    )
    def finish(grad_ref, scalar_ref, master_ref, first_ref, second_ref, *outs):
        loss_out, count_out, master_out, first_out, second_out = outs
        own_grad = grad_ref[...]
        new_first = DECAY_ONE * first_ref[...] + (1.0 - DECAY_ONE) * own_grad
        new_second = DECAY_TWO * second_ref[...] + (1.0 - DECAY_TWO) * own_grad * own_grad
        first_hat = new_first / (1.0 - DECAY_ONE**STEP)
        second_hat = new_second / (1.0 - DECAY_TWO**STEP)
        old = master_ref[...]
        master_out[...] = old - LEARN_RATE * (
            first_hat / (jnp.sqrt(second_hat) + ADAM_EPS) + WEIGHT_DECAY * old
        )
        first_out[...] = new_first
        second_out[...] = new_second
        loss_out[...] = scalar_ref[0:1, 0:1]
        count_out[...] = scalar_ref[1:2, 0:1]

    one, own_shape = jax.ShapeDtypeStruct((1, 1), F32), jax.ShapeDtypeStruct((1, shard), F32)
    loss, count, *updated = pl.pallas_call(
        finish, out_shape=(one, one, own_shape, own_shape, own_shape),
        in_specs=[vmem] * 5, out_specs=(vmem,) * 5,
    )(grad, scalars, master, first, second)
    return (loss[0, 0], count[0, 0], *updated)


def solution(mesh):
    in_specs = (
        P("dom", "feat"),
        P("dom", None),
        P("dom", None),
        P("dom", None, None),
        P("dom"),
        P("dom"),
        P("feat", "dom"),
        P("feat", "dom"),
        P("feat", "dom"),
    )
    out_specs = (P(), P(), P("feat", "dom"), P("feat", "dom"), P("feat", "dom"))
    return jax.shard_map(
        functools.partial(per_device, mesh.shape["dom"]),
        mesh=mesh, in_specs=in_specs, out_specs=out_specs, check_vma=False,
    )
```

```python
import functools

import jax
import jax.numpy as jnp
from jax import lax
from jax.experimental import pallas as pl
from jax.experimental.pallas import tpu as pltpu
from jax.sharding import PartitionSpec as P

HID = 256
CLS = 47
STEP = 10
EPSILON = 1e-05
LEARN_RATE = 0.02
DECAY_ONE = 0.9
DECAY_TWO = 0.999
ADAM_EPS = 1e-08
WEIGHT_DECAY = 0.01

MESH = pl.DeviceIdType.MESH
BF = jnp.bfloat16
F32 = jnp.float32
LANES = 128
CLS_PAD = 64
FEAT_PAD = 64
HALF_HID = HID // 2
ROW_ONE = 2 * FEAT_PAD
ROW_TWO = ROW_ONE + 2 * HALF_HID
HEAD_ROWS = 2 * HALF_HID * CLS // HID
ROW_NORM = ROW_TWO + 48
GELU_A = 0.7978845608028654
GELU_B = 0.044715


def dot(a, b, ca=1, cb=0, precision=None):
    return lax.dot_general(
        a, b, (((ca,), (cb,)), ((), ())), precision=precision, preferred_element_type=F32
    )


def iota(shape, axis):
    return lax.broadcasted_iota(jnp.int32, shape, axis)


def gelu(x):
    half = 0.5 * x
    return half + half * jnp.tanh(x * (GELU_A + (GELU_A * GELU_B) * (x * x)))


def gelu_grad(x):
    xx = x * x
    t = jnp.tanh(x * (GELU_A + (GELU_A * GELU_B) * xx))
    return 0.5 + 0.5 * t + (x * (GELU_A + (3.0 * GELU_A * GELU_B) * xx)) * (0.5 - 0.5 * (t * t))


def roll_rows(x, amount, right):
    for bit in range(7):
        step = 1 << bit
        moved = pltpu.roll(x, step if right else LANES - step, 1)
        x = jnp.where((amount & step) != 0, moved, x)
    return x


def parts(x):
    first = x.astype(BF)
    rest = x - first.astype(F32)
    second = rest.astype(BF)
    return first, second, (rest - second.astype(F32)).astype(BF)


def loop(n, body):
    def step(i, carry):
        body(i)
        return carry

    lax.fori_loop(0, n, step, 0)


def kernel(
    cfg,
    x_in, lm_in, hm_in, send_hbm, label_hbm, lmask_hbm, master_hbm,
    grad_out, scalar_out,
    send_in, label_in, lmask_in, master_in, shares,
    a_stage, b_stage, h_stage, x_stage,
    a_rows, b_far, hmt, sel, xs, hs, gs_all, agg_ref, agg_zero,
    edge_far, edge_hm, edge_x, edge_h, edge_inv, part_tx, part_rx,
    mixed, normed, slope, scale_inv, inv_ref, halo_tx, halo_rx,
    flat_t, par_tx, par_rx, norm_rx, wmat, wmat_t, norm_col, head_ws, head_wn, head_ws_t, head_wn_t,
    g_low, grads, early_rx, late_rx, one_tx, one_rx, two_tx, two_rx, top_tx, top_one, top_two, dw_head, acc_gain, acc_bias, place,
    local_sem, pair_send, pair_recv, halo_send, halo_recv, par_send, column_recv, plane_recv, norm_send, norm_recv,
    one_send, one_recv, two_send, two_recv, top_send, top_recv,
):
    n_dom, nodes, half, halo, shard, fin = (
        cfg["n_dom"], cfg["nodes"], cfg["half"], cfg["halo"], cfg["shard"], cfg["fin"]
    )
    win, par_rows, rows_all = cfg["win"], cfg["par_rows"], cfg["rows_all"]
    me, f = lax.axis_index("dom"), lax.axis_index("feat")
    other = 1 - f
    own = pl.multiple_of(f * half, half)
    far = pl.multiple_of(other * half, half)
    own_cols, far_cols = pl.ds(own, half), pl.ds(far, half)

    group = cfg["group"]
    n_high = n_dom // group
    high, low = me // group, lax.rem(me, group)
    barrier = pltpu.get_barrier_semaphore()

    def greet(p, core):
        pl.semaphore_signal(barrier, inc=1, device_id=(p, core), device_id_type=MESH)

    loop(n_dom - 1, lambda i: greet(lax.rem(me + i + 1, n_dom), f))
    for step in range(group):
        greet(high * group + lax.rem(low + step, group), other)

    chunk = 128
    n_chunk = half // chunk
    x_copy = pltpu.make_async_copy(x_in, x_stage, local_sem.at[6])
    x_copy.start()
    small_copies = [
        pltpu.make_async_copy(src, dst, local_sem.at[k])
        for k, (src, dst) in enumerate(
            ((master_hbm, master_in), (send_hbm, send_in), (label_hbm, label_in),
             (lmask_hbm, lmask_in))
        )
    ]
    for copy in small_copies:
        copy.start()
    h_rows = cfg["h_rows"]

    def h_copy(i):
        return pltpu.make_async_copy(
            hm_in.at[pl.ds(i * h_rows, h_rows), :], h_stage, local_sem.at[7]
        )

    h_copy(0).start()

    slots = cfg["slots"]

    def a_copy(i):
        return pltpu.make_async_copy(
            lm_in.at[pl.ds(pl.multiple_of(own + i * chunk, chunk), chunk), :],
            a_stage.at[lax.rem(i, slots)], local_sem.at[8 + lax.rem(i, slots)],
        )

    def b_copy(i):
        return pltpu.make_async_copy(
            lm_in.at[pl.ds(pl.multiple_of(far + i * chunk, chunk), chunk), own_cols],
            b_stage.at[lax.rem(i, slots)], local_sem.at[8 + slots + lax.rem(i, slots)],
        )

    loop(slots, lambda i: a_copy(i).start())
    loop(slots, lambda i: b_copy(i).start())

    def pair_copy(src, dst, k):
        return pltpu.make_async_remote_copy(
            src_ref=src, dst_ref=dst, send_sem=pair_send.at[k], recv_sem=pair_recv.at[k],
            device_id=(me, other), device_id_type=MESH,
        )

    x_copy.wait()
    slice_rows = pl.ds(pl.multiple_of(f * FEAT_PAD, FEAT_PAD), FEAT_PAD)
    pad_rows = iota((FEAT_PAD, half), 0)
    for c in range(2):
        part = slice(c * half, (c + 1) * half)
        mixed[0:FEAT_PAD, :half] = jnp.where(pad_rows == fin, 1.0, 0.0)
        mixed[0:fin, :half] = x_stage[:, part].astype(F32)
        xs[slice_rows, part] = mixed[0:FEAT_PAD, :half].astype(BF)

    small_copies[1].wait()
    send_rows = send_in[...].astype(F32)
    lane_d = iota(send_rows.shape, 1)
    node_lane = iota((16, nodes), 1).astype(F32)

    def build_sel(q):
        first = jnp.sum(jnp.where(lane_d == 2 * q, send_rows, 0.0), axis=1, keepdims=True)
        second = jnp.sum(jnp.where(lane_d == 2 * q + 1, send_rows, 0.0), axis=1, keepdims=True)
        rows = jnp.concatenate([first, second], axis=0)
        sel[pl.ds(pl.multiple_of(q * 16, 16), 16), :] = jnp.where(
            node_lane == rows, 1.0, 0.0
        ).astype(BF)

    if n_dom <= 16:
        for q in range(n_dom // 2):
            build_sel(q)
    else:
        loop(n_dom // 2, build_sel)

    def halo_copy(k, p):
        return pltpu.make_async_remote_copy(
            src_ref=halo_tx.at[k % 2, p], dst_ref=halo_rx.at[k, me],
            send_sem=halo_send.at[k], recv_sem=halo_recv.at[k],
            device_id=(p, f), device_id_type=MESH,
        )

    def send_halo(k):
        loop(n_dom - 1, lambda i: halo_copy(k, lax.rem(me + i + 1, n_dom)).start())
        halo_rx[k, me] = halo_tx[k % 2, me]

    def pack_halo(k, rows):
        v = rows.reshape(n_dom, 8, HID)
        if k >= 2:
            wait_halo_sent(k - 2)
        halo_tx[k % 2] = jnp.concatenate([v[:, :, :LANES], v[:, :, LANES:]], axis=1).astype(BF)

    def wait_halo(k):
        part = pl.ds(0, n_dom - 1)
        pltpu.make_async_copy(halo_rx.at[k, part], halo_rx.at[k, part], halo_recv.at[k]).wait()

    def wait_halo_sent(k):
        part = pl.ds(0, n_dom - 1)
        pltpu.make_async_copy(
            halo_tx.at[k % 2, part], halo_tx.at[k % 2, part], halo_send.at[k]
        ).wait()

    def read_halo(k):
        v = halo_rx[k].astype(F32)
        rows = jnp.concatenate(
            [v[:, :8, :].reshape(halo, LANES), v[:, 8:, :].reshape(halo, LANES)], axis=1
        )
        return rows.T.astype(BF)

    def build_place(q):
        rows = pl.ds(pl.multiple_of(q * 16, 16), 16)
        r_pad = iota((16, k_all), 0) + q * 16
        k_col = iota((16, k_all), 1)
        owner, inner = k_col // par_rows, lax.rem(k_col, par_rows)
        target = lax.shift_right_logical(owner * shard, 8) + inner
        row_of = jnp.where(
            r_pad < fin, r_pad,
            jnp.where(
                (r_pad >= FEAT_PAD) & (r_pad < FEAT_PAD + fin), r_pad - (FEAT_PAD - fin),
                jnp.where(
                    (r_pad >= ROW_ONE) & (r_pad < ROW_TWO + HEAD_ROWS),
                    r_pad - (ROW_ONE - 2 * fin), -1,
                ),
            ),
        )
        place[rows, :] = jnp.where(row_of == target, 1.0, 0.0).astype(BF)

    k_all = n_dom * par_rows
    loop(ROW_NORM // 16, build_place)
    for i in range(nodes // h_rows):
        h_copy(i).wait()
        hmt[:, i * h_rows : (i + 1) * h_rows] = h_stage[...].astype(F32).T.astype(BF)
        if (i + 1) * h_rows < nodes:
            h_copy(i + 1).start()

    def convert_a(i):
        a_copy(i).wait()
        rows = pl.ds(pl.multiple_of(i * chunk, chunk), chunk)
        a_rows[rows, :] = a_stage[lax.rem(i, slots)].astype(F32).astype(BF)

        @pl.when(i + slots < n_chunk)
        def _():
            a_copy(i + slots).start()

    pl.semaphore_wait(barrier, n_dom - 1 + group)

    x_pair = pair_copy(xs.at[slice_rows, :], xs.at[slice_rows, :], 0)
    x_pair.start()
    off = lax.rem(shard * me, HID)
    off_row, off_lane = off // LANES, lax.rem(off, LANES)
    t_rows = 2 * win
    lane_t = iota((t_rows, LANES), 1)

    def to_window(t):
        r = pltpu.roll(t, off_lane, 1)
        t = jnp.where(lane_t < off_lane, pltpu.roll(r, 1, 0), r)
        t = jnp.where(off_row == 1, pltpu.roll(t, 1, 0), t)
        flat_t[...] = t
        return jnp.concatenate(
            [flat_t[pl.ds(0, win, stride=2), :], flat_t[pl.ds(1, win, stride=2), :]], axis=1
        )

    def from_window(w):
        flat_t[pl.ds(0, win, stride=2), :] = w[:, :LANES]
        flat_t[pl.ds(1, win, stride=2), :] = w[:, LANES:]
        t = flat_t[...]
        t = jnp.where(off_row == 1, pltpu.roll(t, t_rows - 1, 0), t)
        back = lax.rem(LANES - off_lane, LANES)
        near = pltpu.roll(t, back, 1)
        after = pltpu.roll(near, t_rows - 1, 0)
        return jnp.where(lane_t + off_lane < LANES, near, after)

    small_copies[0].wait()
    shares[...] = jnp.zeros_like(shares)

    for k in range(-(-shard // LANES)):
        width = min(LANES, shard - k * LANES)
        shares[k : k + 1, 0:width] = master_in[0:1, k * LANES : k * LANES + width]
    window = to_window(shares[...])
    if par_rows > win:
        window = jnp.concatenate([window, jnp.zeros((par_rows - win, HID), F32)], axis=0)
    par_tx[...] = window.astype(BF)
    par_rx[f, pl.ds(pl.multiple_of(me * par_rows, par_rows), par_rows), :] = par_tx[...]


    urgent = cfg["urgent"]
    patient = [h for h in range(n_high) if h not in urgent]

    def par_slot(h, w):
        start = pl.multiple_of((h * group + w) * par_rows, par_rows)
        return par_rx.at[f, pl.ds(start, par_rows), :]

    def send_to(p, core, src, dst, send_sem, recv_sem):
        pltpu.make_async_remote_copy(
            src_ref=src, dst_ref=dst, send_sem=send_sem, recv_sem=recv_sem,
            device_id=(p, core), device_id_type=MESH,
        ).start()

    def to_plane(src, dst, send_sem, recv_sem, both):
        if both:
            send_to(me, other, src, dst, send_sem, recv_sem)
        for step in range(1, group):
            p = high * group + lax.rem(low + step, group)
            send_to(p, f, src, dst, send_sem, recv_sem)
            if both:
                send_to(p, other, src, dst, send_sem, recv_sem)

    def to_column(src, dst, send_sem, recv_sem):
        for step in range(1, n_high):
            p = lax.rem(high + step, n_high) * group + low
            send_to(p, f, src, dst, send_sem, recv_sem)

    def any_of(which):
        return functools.reduce(jnp.logical_or, [high == h for h in which])

    def own_params(which):
        @pl.when(any_of(which))
        def _():
            to_plane(
                par_tx, par_slot(high, low), par_send, plane_recv.at[high], which is urgent
            )

    def forward_params(which):
        for h in which:
            @pl.when(high != h)
            def _():
                pltpu.make_async_copy(par_tx, par_tx, column_recv.at[h]).wait()
                to_plane(
                    par_slot(h, low), par_slot(h, low), par_send, plane_recv.at[h],
                    which is urgent,
                )

    def wait_params(which):
        part = pl.ds(0, (2 * group - 1 if which is urgent else group - 1) * par_rows)
        for h in which:
            pltpu.make_async_copy(
                par_rx.at[f, part, :], par_rx.at[f, part, :], plane_recv.at[h]
            ).wait()

    norm_local = rows_all - 2 - shard * (n_dom - 1) // HID
    norm_block = norm_local // 16 * 16
    norm_own = norm_rx.at[f]
    last_low = low == group - 1

    def send_norms():
        @pl.when(me == n_dom - 1)
        def _():
            norm_rx[f] = par_tx[norm_block : norm_block + 16, :]
            to_column(norm_own, norm_own, norm_send.at[0], norm_recv.at[0])

    def forward_norms():
        @pl.when(last_low)
        def _():
            @pl.when(high != n_high - 1)
            def _():
                pltpu.make_async_copy(norm_own, norm_own, norm_recv.at[0]).wait()

            to_plane(norm_own, norm_own, norm_send.at[1], norm_recv.at[1], True)

    def wait_norms():
        @pl.when(last_low)
        def _():
            pltpu.make_async_copy(norm_own, norm_own, norm_recv.at[1]).wait()

        @pl.when(jnp.logical_not(last_low))
        def _():
            pltpu.make_async_copy(norm_rx, norm_rx, norm_recv.at[1]).wait()

    def par_pairs(which, k):
        runs = []
        for h in which:
            if runs and runs[-1][1] == h:
                runs[-1][1] = h + 1
            else:
                runs.append([h, h + 1])
        copies = []
        for i, (start, end) in enumerate(runs):
            part = pl.ds(start * group * par_rows, (end - start) * group * par_rows)
            copies.append(pair_copy(par_rx.at[f, part, :], par_rx.at[f, part, :], k + i))
        return copies

    first_early = cfg["first_early"]
    to_column(par_tx, par_slot(high, low), par_send, column_recv.at[high])
    own_params(urgent)
    send_norms()
    loop(n_chunk, convert_a)
    edge_hm[...] = dot(hmt[...], sel[...], 1, 1).astype(BF)

    def edge_chunk(q):
        rows = pl.ds(pl.multiple_of(q * LANES, LANES), LANES)
        a_rows[pl.ds(pl.multiple_of(half + q * LANES, LANES), LANES), :] = dot(
            sel[rows, own_cols], a_rows[:half, :]
        ).astype(BF)

    loop(halo // LANES, edge_chunk)
    edge_pair = pair_copy(a_rows.at[pl.ds(half, halo), :], edge_far, 7)
    edge_pair.start()
    x_pair.wait_recv()
    picked = dot(sel[...], xs[...], 1, 1)
    edge_x[...] = picked.T.astype(BF)
    picked = picked.reshape(n_dom, 8, LANES)
    small_copies[2].wait()
    small_copies[3].wait()
    count = jnp.sum(lmask_in[...].astype(F32), axis=1, keepdims=True)
    count_high = jnp.floor(count * (1.0 / 256.0))
    count_low = count - 256.0 * count_high
    count_row = iota((8, LANES), 0)
    counts = jnp.where(count_row == 0, count_high, jnp.where(count_row == 1, count_low, 0.0))
    counts = jnp.broadcast_to(counts[None], (n_dom, 8, LANES))
    halo_tx[0] = jnp.concatenate([picked, counts], axis=1).astype(BF)
    send_halo(0)

    forward_params(urgent)
    forward_norms()
    own_params(patient)
    forward_params(patient)
    mixed[0:LANES, :half] = dot(xs[...], a_rows[:half, :], 1, 1)
    def convert_b(i):
        b_copy(i).wait()
        rows = pl.ds(pl.multiple_of(i * chunk, chunk), chunk)
        b_far[rows, :] = b_stage[lax.rem(i, slots)].astype(F32).astype(BF)

        @pl.when(i + slots < n_chunk)
        def _():
            b_copy(i + slots).start()

    loop(n_chunk, convert_b)

    edge_pair.wait()

    def edge_sum(q):
        rows = pl.ds(pl.multiple_of(q * LANES, LANES), LANES)
        ext = pl.ds(pl.multiple_of(half + q * LANES, LANES), LANES)
        a_rows[ext, :] = a_rows[ext, :] + edge_far[rows, :]

    loop(halo // LANES, edge_sum)
    mixed[0:LANES, half : half + halo] = dot(xs[...], a_rows[half:, :], 1, 1)
    wait_params(urgent)
    wait_norms()
    wait_halo(0)
    arrived = halo_rx[0].astype(F32)
    halo_zero = arrived[:, :8, :].reshape(halo, LANES).T.astype(BF)
    count_all = jnp.sum(arrived[:, 8:, :], axis=0)
    label_count = 256.0 * count_all[0:1, 0:1] + count_all[1:2, 0:1]
    k_first = first_early * par_rows
    w_zero = []
    for c in range(2):
        rows_t = dot(place[:ROW_ONE, :k_first], par_rx[c, :k_first, :]).T
        w_zero.append(rows_t.astype(BF))
        norms_t = jnp.concatenate(
            [norm_rx[c].astype(F32), jnp.zeros((LANES - 16, HID), F32)], axis=0
        ).T
        for k in range(2):
            lane = norm_local - norm_block + k
            col = norms_t[:, lane : lane + 1]
            norm_col[c * HALF_HID : (c + 1) * HALF_HID, 2 * k : 2 * k + 1] = col[:HALF_HID]
            norm_col[c * HALF_HID : (c + 1) * HALF_HID, 2 * k + 1 : 2 * k + 2] = col[HALF_HID:]
    w_zero = jnp.concatenate(w_zero, axis=1)

    def assemble_hidden():
        for c in range(2):
            rows = dot(place[ROW_ONE:ROW_TWO, :], par_rx[c])
            wmat[c] = rows.astype(BF)
            wmat_t[c] = rows.T.astype(BF)

    place_row = iota((2 * 48, HID), 0)
    flat_row = jnp.where(place_row < 48, 2 * place_row, 2 * (place_row - 48) + 1)
    first_row = lax.shift_right_logical(iota((2 * 48, HID), 1) * CLS, 7)
    pick_a = jnp.where(flat_row == first_row, 1.0, 0.0).astype(BF)
    pick_b = jnp.where(flat_row == first_row + 1, 1.0, 0.0).astype(BF)
    start_lane = (iota((HID, LANES), 0) * CLS) & (LANES - 1)
    lane_w = iota((HID, LANES), 1)

    def assemble_head():
        for c in range(2):
            flat = dot(place[ROW_TWO:ROW_NORM, :], par_rx[c]).astype(BF)
            flat = jnp.concatenate([flat[:, :LANES], flat[:, LANES:]], axis=0)
            wide = jnp.where(lane_w >= start_lane, dot(pick_a, flat, 0, 0), dot(pick_b, flat, 0, 0))
            head = jnp.where(lane_w < CLS, roll_rows(wide, start_lane, False), 0.0)
            head_t = head.T[:CLS_PAD]
            half_rows = slice(c * HALF_HID, (c + 1) * HALF_HID)
            head_ws[half_rows, :] = head[:HALF_HID].astype(BF)
            head_wn[half_rows, :] = head[HALF_HID:].astype(BF)
            head_ws_t[:, half_rows] = head_t[:, :HALF_HID].astype(BF)
            head_wn_t[:, half_rows] = head_t[:, HALF_HID:].astype(BF)

    wide_cols = 256
    n_cols = half // wide_cols

    def norm_apply(x, layer):
        centre = x - jnp.mean(x, axis=0, keepdims=True)
        rs = lax.rsqrt(jnp.mean(centre * centre, axis=0, keepdims=True) + EPSILON)
        n = centre * rs
        shifted = n * norm_col[:, 2 * layer : 2 * layer + 1] + norm_col[
            :, 2 * layer + 1 : 2 * layer + 2
        ]
        return n, rs, gelu(shifted).astype(BF)

    def norm_forward(layer, mix):
        for j in range(n_cols):
            cols = slice(j * wide_cols, (j + 1) * wide_cols)
            n, rs, value = norm_apply(mix(j * wide_cols), layer)
            normed[layer, :, cols] = n
            scale_inv[layer, :, cols] = jnp.broadcast_to(rs, (8, wide_cols))
            out = pl.ds(pl.multiple_of(own + j * wide_cols, wide_cols), wide_cols)
            hs[layer, :, out] = value

    def norm_slope(layer):
        def body(i):
            for j in range(2):
                cols = pl.ds(pl.multiple_of((2 * i + j) * LANES, LANES), LANES)
                shifted = normed[layer, :, cols] * norm_col[
                    :, 2 * layer : 2 * layer + 1
                ] + norm_col[:, 2 * layer + 1 : 2 * layer + 2]
                slope[layer, :, cols] = gelu_grad(shifted)

        loop(half // (2 * LANES), body)

    def norm_edge(layer, mix):
        for j in range(halo // LANES):
            cols = slice(j * LANES, (j + 1) * LANES)
            edge_h[layer, :, cols] = norm_apply(mix(cols), layer)[2]

        pack_halo(1 + layer, edge_h[layer].astype(F32).T)
        send_halo(1 + layer)

    def rows_of(x, agg):
        return jnp.concatenate([x[:FEAT_PAD], agg[:FEAT_PAD], x[FEAT_PAD:], agg[FEAT_PAD:]], axis=0)

    def aggregate_zero(summed, inv_at, cols):
        inverse = 1.0 / jnp.maximum(summed[fin : fin + 1, :], 1.0)
        inv_at[:, cols] = jnp.broadcast_to(inverse, (8, summed.shape[1]))
        return (summed * inverse).astype(BF)

    def shifted_cols(cols):
        return slice(half + cols.start, half + cols.stop)

    def own_chunk(c):
        return pl.ds(pl.multiple_of(own + c, wide_cols), wide_cols)

    def mix_edge_zero(cols):
        agg = aggregate_zero(
            mixed[0:LANES, shifted_cols(cols)] + dot(halo_zero, edge_hm[:, cols]), edge_inv, cols
        )
        return dot(w_zero, rows_of(edge_x[:, cols], agg))

    def mix_zero(c):
        return dot(w_zero, rows_of(xs[:, own_chunk(c)], agg_zero[:, c : c + wide_cols]))

    norm_edge(0, mix_edge_zero)
    wait_params(patient)
    par_rest = par_pairs(patient, 20)
    for copy in par_rest:
        copy.start()
    agg_zero[...] = aggregate_zero(
        mixed[0:LANES, :half] + dot(halo_zero, hmt[:, own_cols]), inv_ref, slice(0, half)
    )
    norm_forward(0, mix_zero)
    h_pair_one = pair_copy(hs.at[0, :, own_cols], hs.at[0, :, own_cols], 2)
    h_pair_one.start()
    mixed[:, : half + halo] = dot(hs[0, :, own_cols], a_rows[:, own_cols], 1, 1)
    for copy in par_rest:
        copy.wait_recv()
    assemble_hidden()
    w_self_t = jnp.concatenate([wmat_t[0, :, :LANES], wmat_t[1, :, :LANES]], axis=1)
    w_neigh_t = jnp.concatenate([wmat_t[0, :, LANES:], wmat_t[1, :, LANES:]], axis=1)
    h_pair_one.wait_recv()
    mixed[:, : half + halo] += dot(hs[0, :, far_cols], a_rows[:, far_cols], 1, 1)
    wait_halo(1)
    halo_one = read_halo(1)

    def mix_edge_one(cols):
        summed = mixed[:, shifted_cols(cols)] + dot(halo_one, edge_hm[:, cols])
        agg = (summed * edge_inv[0:1, cols]).astype(BF)
        return dot(w_self_t, edge_h[0, :, cols]) + dot(w_neigh_t, agg)

    def mix_one(c):
        return dot(w_self_t, hs[0, :, own_chunk(c)]) + dot(
            w_neigh_t, agg_ref[0, :, c : c + wide_cols]
        )

    norm_edge(1, mix_edge_one)
    total = mixed[:, :half] + dot(halo_one, hmt[:, own_cols])
    agg_ref[0] = (total * inv_ref[0:1, :]).astype(BF)
    norm_forward(1, mix_one)
    h_pair_two = pair_copy(hs.at[1, :, own_cols], hs.at[1, :, own_cols], 3)
    h_pair_two.start()
    mixed[:, :half] = dot(hs[1, :, own_cols], a_rows[:half, own_cols], 1, 1)
    assemble_head()
    h_pair_two.wait_recv()
    mixed[:, :half] += dot(hs[1, :, far_cols], a_rows[:half, far_cols], 1, 1)
    wait_halo(2)
    halo_two = read_halo(2)
    for c in range(0, half, wide_cols):
        cols = slice(c, c + wide_cols)
        total = mixed[:, cols] + dot(halo_two, hmt[:, own_chunk(c)])
        agg_ref[1, :, cols] = (total * inv_ref[0:1, cols]).astype(BF)

    logits = dot(head_ws_t[...], hs[1, :, own_cols]) + dot(head_wn_t[...], agg_ref[1])
    class_id = iota((CLS_PAD, half), 0)
    logits = jnp.where(class_id < CLS, logits, -1e30)
    top = jnp.max(logits, axis=0, keepdims=True)
    log_total = top + jnp.log(jnp.sum(jnp.exp(logits - top), axis=0, keepdims=True))
    onehot = class_id == label_in[0:1, own_cols]
    weight = lmask_in[0:1, own_cols].astype(F32)
    chosen = jnp.sum(jnp.where(onehot, logits, 0.0), axis=0, keepdims=True)
    loss_part = jnp.sum((log_total - chosen) * weight, axis=1, keepdims=True)
    pad_rows = grads.shape[1] - rows_all // 8 * 8
    for c in range(2):
        grads[c, rows_all // 8 * 8 :, :] = jnp.broadcast_to(loss_part, (pad_rows, HID))
    probs = jnp.exp(logits - log_total)
    g_logits = (probs - jnp.where(onehot, 1.0, 0.0)) * (weight / label_count)
    g_low[0:CLS_PAD, :] = g_logits.astype(BF)
    g_head = g_low[0:CLS_PAD, :]

    def exchange_backward(k):
        whole = pair_copy(gs_all.at[k, :, own_cols], gs_all.at[k, :, own_cols], 4 + k)
        part_tx[...] = dot(hmt[:, own_cols], gs_all[k, :, own_cols], 1, 1)
        part = pair_copy(part_tx, part_rx.at[k], 8 + k)
        part.start()
        return whole, part

    def send_back(k, part, whole):
        part.wait()
        pack_halo(3 + k, part_tx[...] + part_rx[k])
        send_halo(3 + k)
        whole.start()

    def spread(k, whole, base):
        mixed[:, :half] = dot(gs_all[k, :, own_cols], a_rows[:half, own_cols])
        if k == 1:
            norm_slope(0)
        whole.wait_recv()
        mixed[:, half : 2 * half] = dot(gs_all[k, :, far_cols], b_far[...])
        mixed[:, :half] = mixed[:, :half] + mixed[:, half : 2 * half] + base()
        wait_halo(3 + k)
        return read_halo(3 + k)

    def norm_backward(layer, back):
        acc_gain[...] = jnp.zeros_like(acc_gain)
        acc_bias[...] = jnp.zeros_like(acc_bias)

        gain = norm_col[:, 2 * layer : 2 * layer + 1]
        for j in range(n_cols):
            cols = slice(j * wide_cols, (j + 1) * wide_cols)
            n = normed[layer, :, cols]
            through = mixed[:, cols] + dot(back, sel[:, own_chunk(j * wide_cols)])
            g_shift = through * slope[layer, :, cols]
            scaled = g_shift * n
            acc_gain[...] += scaled[:, :LANES] + scaled[:, LANES:]
            acc_bias[...] += g_shift[:, :LANES] + g_shift[:, LANES:]
            gn = g_shift * gain
            mean_one = jnp.mean(gn, axis=0, keepdims=True)
            mean_two = jnp.mean(gn * n, axis=0, keepdims=True)
            g_mixed = (gn - mean_one - n * mean_two) * scale_inv[layer, 0:1, cols]
            g_low[:, cols] = g_mixed.astype(BF)

        gain_row = jnp.sum(acc_gain[...].T, axis=0, keepdims=True)
        bias_row = jnp.sum(acc_bias[...].T, axis=0, keepdims=True)
        base = rows_all - 2 + layer
        for c in range(2):
            piece = slice(c * HALF_HID, (c + 1) * HALF_HID)
            grads[c, base : base + 1, :LANES] = gain_row[:, piece]
            grads[c, base : base + 1, LANES:] = bias_row[:, piece]

    early_start = shard * first_early // HID // 8 * 8
    early_rows = round_up(rows_all + 1, 8) - early_start

    norm_first = rows_all - 2
    top_start = rows_all // 8 * 8

    def lay(ref, rows):
        ref[:win, :] = rows[:, :LANES]
        ref[win:, :] = rows[:, LANES:]

    def stage_one(doms, far_ref):
        loss_row = grads[f, rows_all : rows_all + 1, :] + far_ref[rows_all : rows_all + 1, :]
        row = iota((win, HID), 0)
        for d in doms:
            start = shard * d // HID
            span = slice(start, start + win)
            rows = grads[f, span, :] + far_ref[span, :]
            if d == n_dom - 1:
                rows = jnp.where(row >= norm_first - start, 0.0, rows)
            rows = jnp.where(row == win - 1, loss_row, rows)
            to_high, to_low = d // group, d % group

            @pl.when(low == to_low)
            def _():
                lay(one_rx.at[to_high, low], rows)

            @pl.when(low != to_low)
            def _():
                lay(one_tx.at[d], rows)
                pltpu.make_async_remote_copy(
                    src_ref=one_tx.at[d], dst_ref=one_rx.at[to_high, low],
                    send_sem=one_send, recv_sem=one_recv.at[to_high],
                    device_id=(high * group + to_low, f), device_id_type=MESH,
                ).start()

    def top_copy(k, dst, p):
        return pltpu.make_async_remote_copy(
            src_ref=top_tx.at[k], dst_ref=dst, send_sem=top_send.at[k], recv_sem=top_recv.at[k],
            device_id=(p, f), device_id_type=MESH,
        )

    def stage_two(doms):
        for d in doms:
            to_high, to_low = d // group, d % group

            @pl.when(low == to_low)
            def _():
                part = pl.ds(0, group - 1)
                pltpu.make_async_copy(
                    one_rx.at[to_high, part], one_rx.at[to_high, part], one_recv.at[to_high]
                ).wait()
                total = jnp.sum(one_rx[to_high], axis=0)

                @pl.when(high == to_high)
                def _():
                    two_rx[high] = total

                @pl.when(high != to_high)
                def _():
                    two_tx[to_high] = total
                    pltpu.make_async_remote_copy(
                        src_ref=two_tx.at[to_high], dst_ref=two_rx.at[high],
                        send_sem=two_send, recv_sem=two_recv, device_id=(d, f),
                        device_id_type=MESH,
                    ).start()

    gs_all[0, :, own_cols] = (dot(head_wn[:, :CLS_PAD], g_head) * inv_ref[0:1, :]).astype(BF)
    g_pair_two, part_two = exchange_backward(0)
    dws = dot(hs[1, :, own_cols], g_head, 1, 1)
    dwn = dot(agg_ref[1], g_head, 1, 1)
    norm_slope(1)
    send_back(0, part_two, g_pair_two)
    dw_head[...] = jnp.zeros_like(dw_head)
    for c in range(2):
        piece = slice(c * HALF_HID, (c + 1) * HALF_HID)
        dw_head[:HALF_HID, :CLS_PAD] = dws[piece]
        dw_head[HALF_HID:, :CLS_PAD] = dwn[piece]
        wide = roll_rows(dw_head[...], start_lane, True)
        low_part = jnp.where(lane_w >= start_lane, wide, 0.0)
        high_part = jnp.where(lane_w >= start_lane, 0.0, wide)
        stacked = jnp.concatenate([*parts(low_part), *parts(high_part)], axis=0)
        picks = jnp.concatenate([pick_a] * 3 + [pick_b] * 3, axis=1)
        flat = dot(picks, stacked)
        flat = jnp.concatenate([flat[:48], flat[48:]], axis=1)
        base = 2 * fin + 2 * HALF_HID
        grads[c, base : base + HEAD_ROWS, :] = flat[:HEAD_ROWS]
    back = spread(0, g_pair_two, lambda: dot(head_ws[:, :CLS_PAD], g_head))
    w_self = jnp.concatenate([wmat[0, :LANES], wmat[1, :LANES]], axis=0)
    w_neigh = jnp.concatenate([wmat[0, LANES:], wmat[1, LANES:]], axis=0)

    norm_backward(1, back)
    gs_all[1, :, own_cols] = (dot(w_neigh, g_low[...]) * inv_ref[0:1, :]).astype(BF)

    g_pair_one, part_one = exchange_backward(1)
    g_one = g_low[...]
    dws = dot(hs[0, :, own_cols], g_one, 1, 1)
    dwn = dot(agg_ref[0], g_one, 1, 1)
    for c in range(2):
        piece = slice(c * HALF_HID, (c + 1) * HALF_HID)
        base = 2 * fin
        grads[c, base : base + HALF_HID, :] = dws[piece]
        grads[c, base + HALF_HID : base + 2 * HALF_HID, :] = dwn[piece]

    def early_out():
        early_pair.wait()
        stage_one(range(first_early, n_dom), early_rx)

    early_pair = pair_copy(
        grads.at[other, pl.ds(early_start, early_rows), :],
        early_rx.at[pl.ds(early_start, early_rows), :], 6,
    )
    early_pair.start()
    send_back(1, part_one, g_pair_one)
    early_out()
    back = spread(1, g_pair_one, lambda: dot(w_self, g_low[...]))
    norm_backward(0, back)
    g_zero = g_low[...]
    dws = dot(xs[:, own_cols], g_zero, 1, 1)
    dwn = dot(agg_zero[...], g_zero, 1, 1)
    for c in range(2):
        start = c * FEAT_PAD
        grads[c, 0:fin, :] = dws[start : start + fin]
        grads[c, fin : 2 * fin, :] = dwn[start : start + fin]

    low_rows = pl.ds(0, round_up(shard * (first_early - 1) // HID + win, 8))
    top_rows = pl.ds(top_start, 8)
    late_pairs = [
        pair_copy(grads.at[other, rows, :], late_rx.at[rows, :], k)
        for rows, k in ((low_rows, 12), (top_rows, 13))
    ]
    for copy in late_pairs:
        copy.start()
    for copy in late_pairs:
        copy.wait_recv()
    stage_one(range(first_early), late_rx)
    norms = grads[f, top_rows, :] + late_rx[top_rows, :]
    top_tx[0] = norms

    @pl.when(low == group - 1)
    def _():
        top_one[low] = norms

    @pl.when(low != group - 1)
    def _():
        top_copy(0, top_one.at[low], high * group + group - 1).start()

    stage_two(range(first_early, n_dom))
    stage_two(range(first_early))

    @pl.when(low == group - 1)
    def _():
        part = pl.ds(0, group - 1)
        pltpu.make_async_copy(top_one.at[part], top_one.at[part], top_recv.at[0]).wait()
        norms = jnp.sum(top_one[...], axis=0)
        top_tx[1] = norms

        @pl.when(high == n_high - 1)
        def _():
            top_two[high] = norms

        @pl.when(high != n_high - 1)
        def _():
            top_copy(1, top_two.at[high], n_dom - 1).start()

    part = pl.ds(0, n_high - 1)
    pltpu.make_async_copy(two_rx.at[part], two_rx.at[part], two_recv).wait()

    @pl.when(me == n_dom - 1)
    def _():
        pltpu.make_async_copy(top_two.at[part], top_two.at[part], top_recv.at[1]).wait()
        norms = jnp.sum(top_two[...], axis=0)
        first = norm_first - shard * (n_dom - 1) // HID
        norms = norms[norm_first - top_start : norm_first - top_start + 2]
        two_rx[0, first : first + 2, :] += norms[:, :LANES]
        two_rx[0, win + first : win + first + 2, :] += norms[:, LANES:]

    flat_t[...] = jnp.sum(two_rx[...], axis=0)
    scalar_out[0:1, :] = jnp.broadcast_to(flat_t[win - 1 : win, 0:1], (1, LANES))
    scalar_out[1:2, :] = jnp.broadcast_to(label_count, (1, LANES))
    shares[...] = from_window(jnp.concatenate([flat_t[:win, :], flat_t[win:, :]], axis=1))
    for k in range(-(-shard // LANES)):
        width = min(LANES, shard - k * LANES)
        grad_out[0:1, k * LANES : k * LANES + width] = shares[k : k + 1, 0:width]

    for copy in (
        x_pair, h_pair_one, h_pair_two, g_pair_two, g_pair_one,
        *par_rest, *late_pairs,
    ):
        copy.wait_send()
    for k in range(3, 5):
        wait_halo_sent(k)
    pltpu.make_async_copy(two_tx.at[part], two_tx.at[part], two_send).wait()
    @pl.when(low != group - 1)
    def _():
        pltpu.make_async_copy(top_tx.at[0], top_tx.at[0], top_send.at[0]).wait()

    @pl.when((low == group - 1) & (high != n_high - 1))
    def _():
        pltpu.make_async_copy(top_tx.at[1], top_tx.at[1], top_send.at[1]).wait()

    part = pl.ds(0, n_dom - n_high)
    pltpu.make_async_copy(one_tx.at[part], one_tx.at[part], one_send).wait()
    n_sent = n_high - 1 + len(urgent) * (2 * group - 1) + len(patient) * (group - 1)
    while n_sent > 0:
        part = pl.ds(0, min(n_sent, n_dom) * par_rows)
        pltpu.make_async_copy(par_rx.at[f, part, :], par_rx.at[f, part, :], par_send).wait()
        n_sent -= n_dom

    @pl.when(me == n_dom - 1)
    def _():
        for step in range(1, n_high):
            pltpu.make_async_copy(norm_own, norm_own, norm_send.at[0]).wait()

    @pl.when(last_low)
    def _():
        for step in range(2 * group - 1):
            pltpu.make_async_copy(norm_own, norm_own, norm_send.at[1]).wait()


def round_up(value, step):
    return -(-value // step) * step


def per_device(n_dom, features, local_mask, halo_mask, send_rows, labels, label_mask, master, first, second):
    nodes, halo = local_mask.shape[1], halo_mask.shape[1]
    half, shard, fin = nodes // 2, master.shape[1], features.shape[1]
    rows_all = n_dom * shard // HID
    span = (shard + HID - 2) // HID + 1
    win = round_up(span + 1, 4)
    par_rows = round_up(span, 16)
    grad_rows = round_up(rows_all + win, 8)
    group = 1
    while (2 * group) ** 2 <= n_dom:
        group *= 2
    head_end = 2 * fin + 2 * HALF_HID + HEAD_ROWS
    first_early = -(-2 * fin * HID // shard)
    assert shard * (n_dom - 1) <= (rows_all - 2) * HID and rows_all % 8 > 2
    urgent = sorted({d // group for d in range(first_early)})
    cfg = dict(
        group=group, first_early=first_early, urgent=urgent,
        n_dom=n_dom, nodes=nodes, half=half, halo=halo, shard=shard, fin=fin, win=win,
        par_rows=par_rows, rows_all=rows_all, grad_rows=grad_rows,
        h_rows=nodes if halo <= 256 else LANES, slots=half // LANES if halo <= 256 else 2,
    )
    hbm = pl.BlockSpec(memory_space=pl.ANY)
    vmem = pl.BlockSpec(memory_space=pltpu.VMEM)
    i32 = jnp.int32
    pad = LANES if halo <= 256 else 0
    scratch = [
        pltpu.VMEM((8, n_dom), i32),
        pltpu.VMEM((1, nodes), i32),
        pltpu.VMEM((1, nodes), i32),
        pltpu.VMEM((1, shard), F32),
        pltpu.VMEM((2 * win, LANES), F32),
        pltpu.VMEM((cfg["slots"], LANES, nodes), i32),
        pltpu.VMEM((cfg["slots"], LANES, half), i32),
        pltpu.VMEM((cfg["h_rows"], halo), i32),
        pltpu.VMEM((fin, nodes), BF),
        pltpu.VMEM((half + halo, nodes), BF),
        pltpu.VMEM((half, half), BF),
        pltpu.VMEM((halo, nodes), BF),
        pltpu.VMEM((halo, nodes), BF),
        pltpu.VMEM((2 * FEAT_PAD, nodes), BF),
        pltpu.VMEM((2, HID, nodes), BF),
        pltpu.VMEM((2, HID, nodes), BF),
        pltpu.VMEM((2, HID, half), BF),
        pltpu.VMEM((LANES, half), BF),
        pltpu.VMEM((halo, nodes), BF),
        pltpu.VMEM((halo, halo), BF),
        pltpu.VMEM((LANES, halo), BF),
        pltpu.VMEM((2, HID, halo), BF),
        pltpu.VMEM((8, halo), F32),
        pltpu.VMEM((halo, HID), F32),
        pltpu.VMEM((2, halo, HID), F32),
        pltpu.VMEM((HID, half + max(halo, half) + pad), F32),
        pltpu.VMEM((2, HID, half + pad), F32),
        pltpu.VMEM((2, HID, half + pad), F32),
        pltpu.VMEM((2, 8, half), F32),
        pltpu.VMEM((8, half), F32),
        pltpu.VMEM((2, n_dom, 16, LANES), BF),
        pltpu.VMEM((5, n_dom, 16, LANES), BF),
        pltpu.VMEM((2 * win, LANES), F32),
        pltpu.VMEM((par_rows, HID), BF),
        pltpu.VMEM((2, n_dom * par_rows, HID), BF),
        pltpu.VMEM((2, 16, HID), BF),
        pltpu.VMEM((2, HID, HID), BF),
        pltpu.VMEM((2, HID, HID), BF),
        pltpu.VMEM((HID, 8), F32),
        pltpu.VMEM((HID, LANES), BF),
        pltpu.VMEM((HID, LANES), BF),
        pltpu.VMEM((CLS_PAD, HID), BF),
        pltpu.VMEM((CLS_PAD, HID), BF),
        pltpu.VMEM((HID, half), BF),
        pltpu.VMEM((2, grad_rows, HID), F32),
        pltpu.VMEM((grad_rows, HID), F32),
        pltpu.VMEM((grad_rows, HID), F32),
        pltpu.VMEM((n_dom, 2 * win, LANES), F32),
        pltpu.VMEM((n_dom // group, group, 2 * win, LANES), F32),
        pltpu.VMEM((n_dom // group, 2 * win, LANES), F32),
        pltpu.VMEM((n_dom // group, 2 * win, LANES), F32),
        pltpu.VMEM((2, 8, HID), F32),
        pltpu.VMEM((group, 8, HID), F32),
        pltpu.VMEM((n_dom // group, 8, HID), F32),
        pltpu.VMEM((HID, LANES), F32),
        pltpu.VMEM((HID, LANES), F32),
        pltpu.VMEM((HID, LANES), F32),
        pltpu.VMEM((ROW_NORM, n_dom * par_rows), BF),
        pltpu.SemaphoreType.DMA((8 + 2 * cfg["slots"],)),
        pltpu.SemaphoreType.DMA((24,)),
        pltpu.SemaphoreType.DMA((24,)),
        pltpu.SemaphoreType.DMA((5,)),
        pltpu.SemaphoreType.DMA((5,)),
        pltpu.SemaphoreType.DMA,
        pltpu.SemaphoreType.DMA((n_dom // group,)),
        pltpu.SemaphoreType.DMA((n_dom // group,)),
        pltpu.SemaphoreType.DMA((2,)),
        pltpu.SemaphoreType.DMA((2,)),
        pltpu.SemaphoreType.DMA,
        pltpu.SemaphoreType.DMA((n_dom // group,)),
        pltpu.SemaphoreType.DMA,
        pltpu.SemaphoreType.DMA,
        pltpu.SemaphoreType.DMA((2,)),
        pltpu.SemaphoreType.DMA((2,)),
    ]
    grad, scalars = pl.pallas_call(
        functools.partial(kernel, cfg),
        out_shape=(
            jax.ShapeDtypeStruct((1, shard), F32),
            jax.ShapeDtypeStruct((2, LANES), F32),
        ),
        in_specs=[hbm] * 7,
        out_specs=(vmem, vmem),
        scratch_shapes=scratch,
        compiler_params=pltpu.CompilerParams(
            collective_id=0, has_side_effects=True, vmem_limit_bytes=63 * 2**20
        ),
    )(
        features.T,
        local_mask,
        halo_mask,
        send_rows[0].T,
        labels.reshape(1, nodes),
        label_mask.reshape(1, nodes),
        master,
    )
    def finish(grad_ref, scalar_ref, master_ref, first_ref, second_ref, *outs):
        loss_out, count_out, master_out, first_out, second_out = outs
        own_grad = grad_ref[...]
        new_first = DECAY_ONE * first_ref[...] + (1.0 - DECAY_ONE) * own_grad
        new_second = DECAY_TWO * second_ref[...] + (1.0 - DECAY_TWO) * own_grad * own_grad
        first_hat = new_first / (1.0 - DECAY_ONE**STEP)
        second_hat = new_second / (1.0 - DECAY_TWO**STEP)
        old = master_ref[...]
        master_out[...] = old - LEARN_RATE * (
            first_hat / (jnp.sqrt(second_hat) + ADAM_EPS) + WEIGHT_DECAY * old
        )
        first_out[...] = new_first
        second_out[...] = new_second
        loss_out[...] = scalar_ref[0:1, 0:1]
        count_out[...] = scalar_ref[1:2, 0:1]

    one, own_shape = jax.ShapeDtypeStruct((1, 1), F32), jax.ShapeDtypeStruct((1, shard), F32)
    loss, count, *updated = pl.pallas_call(
        finish, out_shape=(one, one, own_shape, own_shape, own_shape),
        in_specs=[vmem] * 5, out_specs=(vmem,) * 5,
    )(grad, scalars, master, first, second)
    return (loss[0, 0], count[0, 0], *updated)


def solution(mesh):
    in_specs = (
        P("dom", "feat"),
        P("dom", None),
        P("dom", None),
        P("dom", None, None),
        P("dom"),
        P("dom"),
        P("feat", "dom"),
        P("feat", "dom"),
        P("feat", "dom"),
    )
    out_specs = (P(), P(), P("feat", "dom"), P("feat", "dom"), P("feat", "dom"))
    return jax.shard_map(
        functools.partial(per_device, mesh.shape["dom"]),
        mesh=mesh, in_specs=in_specs, out_specs=out_specs, check_vma=False,
    )
```

```python
import functools

import jax
import jax.numpy as jnp
from jax import lax
from jax.experimental import pallas as pl
from jax.experimental.pallas import tpu as pltpu
from jax.sharding import PartitionSpec as P

HID = 256
CLS = 47
STEP = 10
EPSILON = 1e-05
LEARN_RATE = 0.02
DECAY_ONE = 0.9
DECAY_TWO = 0.999
ADAM_EPS = 1e-08
WEIGHT_DECAY = 0.01

MESH = pl.DeviceIdType.MESH
BF = jnp.bfloat16
F32 = jnp.float32
LANES = 128
CLS_PAD = 64
FEAT_PAD = 64
HALF_HID = HID // 2
ROW_ONE = 2 * FEAT_PAD
ROW_TWO = ROW_ONE + 2 * HALF_HID
HEAD_ROWS = 2 * HALF_HID * CLS // HID
ROW_NORM = ROW_TWO + 48
GELU_A = 0.7978845608028654
GELU_B = 0.044715


def dot(a, b, ca=1, cb=0, precision=None):
    return lax.dot_general(
        a, b, (((ca,), (cb,)), ((), ())), precision=precision, preferred_element_type=F32
    )


def iota(shape, axis):
    return lax.broadcasted_iota(jnp.int32, shape, axis)


def gelu(x):
    half = 0.5 * x
    return half + half * jnp.tanh(x * (GELU_A + (GELU_A * GELU_B) * (x * x)))


def gelu_grad(x):
    xx = x * x
    t = jnp.tanh(x * (GELU_A + (GELU_A * GELU_B) * xx))
    return 0.5 + 0.5 * t + (x * (GELU_A + (3.0 * GELU_A * GELU_B) * xx)) * (0.5 - 0.5 * (t * t))


def roll_rows(x, amount, right):
    for bit in range(7):
        step = 1 << bit
        moved = pltpu.roll(x, step if right else LANES - step, 1)
        x = jnp.where((amount & step) != 0, moved, x)
    return x


def parts(x):
    first = x.astype(BF)
    rest = x - first.astype(F32)
    second = rest.astype(BF)
    return first, second, (rest - second.astype(F32)).astype(BF)


def loop(n, body):
    def step(i, carry):
        body(i)
        return carry

    lax.fori_loop(0, n, step, 0)


def kernel(
    cfg,
    x_in, lm_in, hm_in, send_hbm, label_hbm, lmask_hbm, master_hbm,
    grad_out, scalar_out,
    send_in, label_in, lmask_in, master_in, shares,
    a_stage, b_stage, h_stage, x_stage,
    a_rows, b_far, hmt, sel, xs, hs, gs_all, agg_ref, agg_zero,
    edge_far, edge_hm, edge_x, edge_h, edge_inv, part_tx, part_rx,
    mixed, normed, slope, scale_inv, inv_ref, halo_tx, halo_rx,
    flat_t, par_tx, par_rx, norm_rx, wmat, wmat_t, norm_col, head_ws, head_wn, head_ws_t, head_wn_t,
    g_low, grads, early_rx, late_rx, one_tx, one_rx, two_tx, two_rx, top_tx, top_one, top_two, dw_head, acc_gain, acc_bias, place,
    local_sem, pair_send, pair_recv, halo_send, halo_recv, par_send, column_recv, plane_recv, norm_send, norm_recv,
    one_send, one_recv, two_send, two_recv, top_send, top_recv,
):
    n_dom, nodes, half, halo, shard, fin = (
        cfg["n_dom"], cfg["nodes"], cfg["half"], cfg["halo"], cfg["shard"], cfg["fin"]
    )
    win, par_rows, rows_all = cfg["win"], cfg["par_rows"], cfg["rows_all"]
    me, f = lax.axis_index("dom"), lax.axis_index("feat")
    other = 1 - f
    own = pl.multiple_of(f * half, half)
    far = pl.multiple_of(other * half, half)
    own_cols, far_cols = pl.ds(own, half), pl.ds(far, half)

    group = cfg["group"]
    n_high = n_dom // group
    high, low = me // group, lax.rem(me, group)
    barrier = pltpu.get_barrier_semaphore()

    def greet(p, core):
        pl.semaphore_signal(barrier, inc=1, device_id=(p, core), device_id_type=MESH)

    loop(n_dom - 1, lambda i: greet(lax.rem(me + i + 1, n_dom), f))
    for step in range(group):
        greet(high * group + lax.rem(low + step, group), other)

    chunk = 128
    n_chunk = half // chunk
    x_copy = pltpu.make_async_copy(x_in, x_stage, local_sem.at[6])
    x_copy.start()
    small_copies = [
        pltpu.make_async_copy(src, dst, local_sem.at[k])
        for k, (src, dst) in enumerate(
            ((master_hbm, master_in), (send_hbm, send_in), (label_hbm, label_in),
             (lmask_hbm, lmask_in))
        )
    ]
    for copy in small_copies:
        copy.start()
    h_rows = cfg["h_rows"]

    def h_copy(i):
        return pltpu.make_async_copy(
            hm_in.at[pl.ds(i * h_rows, h_rows), :], h_stage, local_sem.at[7]
        )

    h_copy(0).start()

    slots = cfg["slots"]

    def a_copy(i):
        return pltpu.make_async_copy(
            lm_in.at[pl.ds(pl.multiple_of(own + i * chunk, chunk), chunk), :],
            a_stage.at[lax.rem(i, slots)], local_sem.at[8 + lax.rem(i, slots)],
        )

    def b_copy(i):
        return pltpu.make_async_copy(
            lm_in.at[pl.ds(pl.multiple_of(far + i * chunk, chunk), chunk), own_cols],
            b_stage.at[lax.rem(i, slots)], local_sem.at[8 + slots + lax.rem(i, slots)],
        )

    loop(slots, lambda i: a_copy(i).start())
    loop(slots, lambda i: b_copy(i).start())

    def pair_copy(src, dst, k):
        return pltpu.make_async_remote_copy(
            src_ref=src, dst_ref=dst, send_sem=pair_send.at[k], recv_sem=pair_recv.at[k],
            device_id=(me, other), device_id_type=MESH,
        )

    x_copy.wait()
    slice_rows = pl.ds(pl.multiple_of(f * FEAT_PAD, FEAT_PAD), FEAT_PAD)
    pad_rows = iota((FEAT_PAD, half), 0)
    for c in range(2):
        part = slice(c * half, (c + 1) * half)
        mixed[0:FEAT_PAD, :half] = jnp.where(pad_rows == fin, 1.0, 0.0)
        mixed[0:fin, :half] = x_stage[:, part].astype(F32)
        xs[slice_rows, part] = mixed[0:FEAT_PAD, :half].astype(BF)

    small_copies[1].wait()
    send_rows = send_in[...].astype(F32)
    lane_d = iota(send_rows.shape, 1)
    node_lane = iota((16, nodes), 1).astype(F32)

    def build_sel(q):
        first = jnp.sum(jnp.where(lane_d == 2 * q, send_rows, 0.0), axis=1, keepdims=True)
        second = jnp.sum(jnp.where(lane_d == 2 * q + 1, send_rows, 0.0), axis=1, keepdims=True)
        rows = jnp.concatenate([first, second], axis=0)
        sel[pl.ds(pl.multiple_of(q * 16, 16), 16), :] = jnp.where(
            node_lane == rows, 1.0, 0.0
        ).astype(BF)

    if n_dom <= 16:
        for q in range(n_dom // 2):
            build_sel(q)
    else:
        loop(n_dom // 2, build_sel)

    def halo_copy(k, p):
        return pltpu.make_async_remote_copy(
            src_ref=halo_tx.at[k % 2, p], dst_ref=halo_rx.at[k, me],
            send_sem=halo_send.at[k], recv_sem=halo_recv.at[k],
            device_id=(p, f), device_id_type=MESH,
        )

    def send_halo(k):
        loop(n_dom - 1, lambda i: halo_copy(k, lax.rem(me + i + 1, n_dom)).start())
        halo_rx[k, me] = halo_tx[k % 2, me]

    def pack_halo(k, rows):
        v = rows.reshape(n_dom, 8, HID)
        if k >= 2:
            wait_halo_sent(k - 2)
        halo_tx[k % 2] = jnp.concatenate([v[:, :, :LANES], v[:, :, LANES:]], axis=1).astype(BF)

    def wait_halo(k):
        part = pl.ds(0, n_dom - 1)
        pltpu.make_async_copy(halo_rx.at[k, part], halo_rx.at[k, part], halo_recv.at[k]).wait()

    def wait_halo_sent(k):
        part = pl.ds(0, n_dom - 1)
        pltpu.make_async_copy(
            halo_tx.at[k % 2, part], halo_tx.at[k % 2, part], halo_send.at[k]
        ).wait()

    def read_halo(k):
        v = halo_rx[k].astype(F32)
        rows = jnp.concatenate(
            [v[:, :8, :].reshape(halo, LANES), v[:, 8:, :].reshape(halo, LANES)], axis=1
        )
        return rows.T.astype(BF)

    def build_place(q):
        rows = pl.ds(pl.multiple_of(q * 16, 16), 16)
        r_pad = iota((16, k_all), 0) + q * 16
        k_col = iota((16, k_all), 1)
        owner, inner = k_col // par_rows, lax.rem(k_col, par_rows)
        target = lax.shift_right_logical(owner * shard, 8) + inner
        row_of = jnp.where(
            r_pad < fin, r_pad,
            jnp.where(
                (r_pad >= FEAT_PAD) & (r_pad < FEAT_PAD + fin), r_pad - (FEAT_PAD - fin),
                jnp.where(
                    (r_pad >= ROW_ONE) & (r_pad < ROW_TWO + HEAD_ROWS),
                    r_pad - (ROW_ONE - 2 * fin), -1,
                ),
            ),
        )
        place[rows, :] = jnp.where(row_of == target, 1.0, 0.0).astype(BF)

    k_all = n_dom * par_rows
    loop(ROW_NORM // 16, build_place)
    for i in range(nodes // h_rows):
        h_copy(i).wait()
        hmt[:, i * h_rows : (i + 1) * h_rows] = h_stage[...].astype(F32).T.astype(BF)
        if (i + 1) * h_rows < nodes:
            h_copy(i + 1).start()

    def convert_a(i):
        a_copy(i).wait()
        rows = pl.ds(pl.multiple_of(i * chunk, chunk), chunk)
        a_rows[rows, :] = a_stage[lax.rem(i, slots)].astype(F32).astype(BF)

        @pl.when(i + slots < n_chunk)
        def _():
            a_copy(i + slots).start()

    pl.semaphore_wait(barrier, n_dom - 1 + group)

    x_pair = pair_copy(xs.at[slice_rows, :], xs.at[slice_rows, :], 0)
    x_pair.start()
    off = lax.rem(shard * me, HID)
    off_row, off_lane = off // LANES, lax.rem(off, LANES)
    t_rows = 2 * win
    lane_t = iota((t_rows, LANES), 1)

    def to_window(t):
        r = pltpu.roll(t, off_lane, 1)
        t = jnp.where(lane_t < off_lane, pltpu.roll(r, 1, 0), r)
        t = jnp.where(off_row == 1, pltpu.roll(t, 1, 0), t)
        flat_t[...] = t
        return jnp.concatenate(
            [flat_t[pl.ds(0, win, stride=2), :], flat_t[pl.ds(1, win, stride=2), :]], axis=1
        )

    def from_window(w):
        flat_t[pl.ds(0, win, stride=2), :] = w[:, :LANES]
        flat_t[pl.ds(1, win, stride=2), :] = w[:, LANES:]
        t = flat_t[...]
        t = jnp.where(off_row == 1, pltpu.roll(t, t_rows - 1, 0), t)
        back = lax.rem(LANES - off_lane, LANES)
        near = pltpu.roll(t, back, 1)
        after = pltpu.roll(near, t_rows - 1, 0)
        return jnp.where(lane_t + off_lane < LANES, near, after)

    small_copies[0].wait()
    shares[...] = jnp.zeros_like(shares)

    for k in range(-(-shard // LANES)):
        width = min(LANES, shard - k * LANES)
        shares[k : k + 1, 0:width] = master_in[0:1, k * LANES : k * LANES + width]
    window = to_window(shares[...])
    if par_rows > win:
        window = jnp.concatenate([window, jnp.zeros((par_rows - win, HID), F32)], axis=0)
    par_tx[...] = window.astype(BF)
    par_rx[f, pl.ds(pl.multiple_of(me * par_rows, par_rows), par_rows), :] = par_tx[...]


    urgent = cfg["urgent"]
    patient = [h for h in range(n_high) if h not in urgent]

    def par_slot(h, w):
        start = pl.multiple_of((h * group + w) * par_rows, par_rows)
        return par_rx.at[f, pl.ds(start, par_rows), :]

    def send_to(p, core, src, dst, send_sem, recv_sem):
        pltpu.make_async_remote_copy(
            src_ref=src, dst_ref=dst, send_sem=send_sem, recv_sem=recv_sem,
            device_id=(p, core), device_id_type=MESH,
        ).start()

    def to_plane(src, dst, send_sem, recv_sem, both):
        if both:
            send_to(me, other, src, dst, send_sem, recv_sem)
        for step in range(1, group):
            p = high * group + lax.rem(low + step, group)
            send_to(p, f, src, dst, send_sem, recv_sem)
            if both:
                send_to(p, other, src, dst, send_sem, recv_sem)

    def to_column(src, dst, send_sem, recv_sem):
        for step in range(1, n_high):
            p = lax.rem(high + step, n_high) * group + low
            send_to(p, f, src, dst, send_sem, recv_sem)

    def any_of(which):
        return functools.reduce(jnp.logical_or, [high == h for h in which])

    def own_params(which):
        @pl.when(any_of(which))
        def _():
            to_plane(
                par_tx, par_slot(high, low), par_send, plane_recv.at[high], which is urgent
            )

    def forward_params(which):
        for h in which:
            @pl.when(high != h)
            def _():
                pltpu.make_async_copy(par_tx, par_tx, column_recv.at[h]).wait()
                to_plane(
                    par_slot(h, low), par_slot(h, low), par_send, plane_recv.at[h],
                    which is urgent,
                )

    def wait_params(which):
        part = pl.ds(0, (2 * group - 1 if which is urgent else group - 1) * par_rows)
        for h in which:
            pltpu.make_async_copy(
                par_rx.at[f, part, :], par_rx.at[f, part, :], plane_recv.at[h]
            ).wait()

    norm_local = rows_all - 2 - shard * (n_dom - 1) // HID
    norm_block = norm_local // 16 * 16
    norm_own = norm_rx.at[f]
    last_low = low == group - 1

    def send_norms():
        @pl.when(me == n_dom - 1)
        def _():
            norm_rx[f] = par_tx[norm_block : norm_block + 16, :]
            to_column(norm_own, norm_own, norm_send.at[0], norm_recv.at[0])

    def forward_norms():
        @pl.when(last_low)
        def _():
            @pl.when(high != n_high - 1)
            def _():
                pltpu.make_async_copy(norm_own, norm_own, norm_recv.at[0]).wait()

            to_plane(norm_own, norm_own, norm_send.at[1], norm_recv.at[1], True)

    def wait_norms():
        @pl.when(last_low)
        def _():
            pltpu.make_async_copy(norm_own, norm_own, norm_recv.at[1]).wait()

        @pl.when(jnp.logical_not(last_low))
        def _():
            pltpu.make_async_copy(norm_rx, norm_rx, norm_recv.at[1]).wait()

    def par_pairs(which, k):
        runs = []
        for h in which:
            if runs and runs[-1][1] == h:
                runs[-1][1] = h + 1
            else:
                runs.append([h, h + 1])
        copies = []
        for i, (start, end) in enumerate(runs):
            part = pl.ds(start * group * par_rows, (end - start) * group * par_rows)
            copies.append(pair_copy(par_rx.at[f, part, :], par_rx.at[f, part, :], k + i))
        return copies

    first_early = cfg["first_early"]
    to_column(par_tx, par_slot(high, low), par_send, column_recv.at[high])
    own_params(urgent)
    send_norms()
    loop(n_chunk, convert_a)
    edge_hm[...] = dot(hmt[...], sel[...], 1, 1).astype(BF)

    def edge_chunk(q):
        rows = pl.ds(pl.multiple_of(q * LANES, LANES), LANES)
        a_rows[pl.ds(pl.multiple_of(half + q * LANES, LANES), LANES), :] = dot(
            sel[rows, own_cols], a_rows[:half, :]
        ).astype(BF)

    loop(halo // LANES, edge_chunk)
    edge_pair = pair_copy(a_rows.at[pl.ds(half, halo), :], edge_far, 7)
    edge_pair.start()
    x_pair.wait_recv()
    picked = dot(sel[...], xs[...], 1, 1)
    edge_x[...] = picked.T.astype(BF)
    picked = picked.reshape(n_dom, 8, LANES)
    small_copies[2].wait()
    small_copies[3].wait()
    count = jnp.sum(lmask_in[...].astype(F32), axis=1, keepdims=True)
    count_high = jnp.floor(count * (1.0 / 256.0))
    count_low = count - 256.0 * count_high
    count_row = iota((8, LANES), 0)
    counts = jnp.where(count_row == 0, count_high, jnp.where(count_row == 1, count_low, 0.0))
    counts = jnp.broadcast_to(counts[None], (n_dom, 8, LANES))
    halo_tx[0] = jnp.concatenate([picked, counts], axis=1).astype(BF)
    send_halo(0)

    forward_params(urgent)
    forward_norms()
    own_params(patient)
    forward_params(patient)
    mixed[0:LANES, :half] = dot(xs[...], a_rows[:half, :], 1, 1)
    def convert_b(i):
        b_copy(i).wait()
        rows = pl.ds(pl.multiple_of(i * chunk, chunk), chunk)
        b_far[rows, :] = b_stage[lax.rem(i, slots)].astype(F32).astype(BF)

        @pl.when(i + slots < n_chunk)
        def _():
            b_copy(i + slots).start()

    loop(n_chunk, convert_b)

    edge_pair.wait()

    def edge_sum(q):
        rows = pl.ds(pl.multiple_of(q * LANES, LANES), LANES)
        ext = pl.ds(pl.multiple_of(half + q * LANES, LANES), LANES)
        a_rows[ext, :] = a_rows[ext, :] + edge_far[rows, :]

    loop(halo // LANES, edge_sum)
    mixed[0:LANES, half : half + halo] = dot(xs[...], a_rows[half:, :], 1, 1)
    wait_params(urgent)
    wait_norms()
    wait_halo(0)
    arrived = halo_rx[0].astype(F32)
    halo_zero = arrived[:, :8, :].reshape(halo, LANES).T.astype(BF)
    count_all = jnp.sum(arrived[:, 8:, :], axis=0)
    label_count = 256.0 * count_all[0:1, 0:1] + count_all[1:2, 0:1]
    k_first = first_early * par_rows
    w_zero = []
    for c in range(2):
        rows_t = dot(place[:ROW_ONE, :k_first], par_rx[c, :k_first, :]).T
        w_zero.append(rows_t.astype(BF))
        norms_t = jnp.concatenate(
            [norm_rx[c].astype(F32), jnp.zeros((LANES - 16, HID), F32)], axis=0
        ).T
        for k in range(2):
            lane = norm_local - norm_block + k
            col = norms_t[:, lane : lane + 1]
            norm_col[c * HALF_HID : (c + 1) * HALF_HID, 2 * k : 2 * k + 1] = col[:HALF_HID]
            norm_col[c * HALF_HID : (c + 1) * HALF_HID, 2 * k + 1 : 2 * k + 2] = col[HALF_HID:]
    w_zero = jnp.concatenate(w_zero, axis=1)

    def assemble_hidden():
        for c in range(2):
            rows = dot(place[ROW_ONE:ROW_TWO, :], par_rx[c])
            wmat[c] = rows.astype(BF)
            wmat_t[c] = rows.T.astype(BF)

    place_row = iota((2 * 48, HID), 0)
    flat_row = jnp.where(place_row < 48, 2 * place_row, 2 * (place_row - 48) + 1)
    first_row = lax.shift_right_logical(iota((2 * 48, HID), 1) * CLS, 7)
    pick_a = jnp.where(flat_row == first_row, 1.0, 0.0).astype(BF)
    pick_b = jnp.where(flat_row == first_row + 1, 1.0, 0.0).astype(BF)
    start_lane = (iota((HID, LANES), 0) * CLS) & (LANES - 1)
    lane_w = iota((HID, LANES), 1)

    def assemble_head():
        for c in range(2):
            flat = dot(place[ROW_TWO:ROW_NORM, :], par_rx[c]).astype(BF)
            flat = jnp.concatenate([flat[:, :LANES], flat[:, LANES:]], axis=0)
            wide = jnp.where(lane_w >= start_lane, dot(pick_a, flat, 0, 0), dot(pick_b, flat, 0, 0))
            head = jnp.where(lane_w < CLS, roll_rows(wide, start_lane, False), 0.0)
            head_t = head.T[:CLS_PAD]
            half_rows = slice(c * HALF_HID, (c + 1) * HALF_HID)
            head_ws[half_rows, :] = head[:HALF_HID].astype(BF)
            head_wn[half_rows, :] = head[HALF_HID:].astype(BF)
            head_ws_t[:, half_rows] = head_t[:, :HALF_HID].astype(BF)
            head_wn_t[:, half_rows] = head_t[:, HALF_HID:].astype(BF)

    wide_cols = 256
    n_cols = half // wide_cols

    def norm_apply(x, layer):
        centre = x - jnp.mean(x, axis=0, keepdims=True)
        rs = lax.rsqrt(jnp.mean(centre * centre, axis=0, keepdims=True) + EPSILON)
        n = centre * rs
        shifted = n * norm_col[:, 2 * layer : 2 * layer + 1] + norm_col[
            :, 2 * layer + 1 : 2 * layer + 2
        ]
        return n, rs, gelu(shifted).astype(BF)

    def norm_forward(layer, mix):
        for j in range(n_cols):
            cols = slice(j * wide_cols, (j + 1) * wide_cols)
            n, rs, value = norm_apply(mix(j * wide_cols), layer)
            normed[layer, :, cols] = n
            scale_inv[layer, :, cols] = jnp.broadcast_to(rs, (8, wide_cols))
            out = pl.ds(pl.multiple_of(own + j * wide_cols, wide_cols), wide_cols)
            hs[layer, :, out] = value

    def norm_slope(layer):
        for c in range(0, half, wide_cols):
            cols = slice(c, c + wide_cols)
            shifted = normed[layer, :, cols] * norm_col[
                :, 2 * layer : 2 * layer + 1
            ] + norm_col[:, 2 * layer + 1 : 2 * layer + 2]
            slope[layer, :, cols] = gelu_grad(shifted)

    def norm_edge(layer, mix):
        for j in range(halo // LANES):
            cols = slice(j * LANES, (j + 1) * LANES)
            edge_h[layer, :, cols] = norm_apply(mix(cols), layer)[2]

        pack_halo(1 + layer, edge_h[layer].astype(F32).T)
        send_halo(1 + layer)

    def rows_of(x, agg):
        return jnp.concatenate([x[:FEAT_PAD], agg[:FEAT_PAD], x[FEAT_PAD:], agg[FEAT_PAD:]], axis=0)

    def aggregate_zero(summed, inv_at, cols):
        inverse = 1.0 / jnp.maximum(summed[fin : fin + 1, :], 1.0)
        inv_at[:, cols] = jnp.broadcast_to(inverse, (8, summed.shape[1]))
        return (summed * inverse).astype(BF)

    def shifted_cols(cols):
        return slice(half + cols.start, half + cols.stop)

    def own_chunk(c):
        return pl.ds(pl.multiple_of(own + c, wide_cols), wide_cols)

    def mix_edge_zero(cols):
        agg = aggregate_zero(
            mixed[0:LANES, shifted_cols(cols)] + dot(halo_zero, edge_hm[:, cols]), edge_inv, cols
        )
        return dot(w_zero, rows_of(edge_x[:, cols], agg))

    def mix_zero(c):
        return dot(w_zero, rows_of(xs[:, own_chunk(c)], agg_zero[:, c : c + wide_cols]))

    norm_edge(0, mix_edge_zero)
    wait_params(patient)
    par_rest = par_pairs(patient, 20)
    for copy in par_rest:
        copy.start()
    agg_zero[...] = aggregate_zero(
        mixed[0:LANES, :half] + dot(halo_zero, hmt[:, own_cols]), inv_ref, slice(0, half)
    )
    norm_forward(0, mix_zero)
    h_pair_one = pair_copy(hs.at[0, :, own_cols], hs.at[0, :, own_cols], 2)
    h_pair_one.start()
    mixed[:, : half + halo] = dot(hs[0, :, own_cols], a_rows[:, own_cols], 1, 1)
    for copy in par_rest:
        copy.wait_recv()
    assemble_hidden()
    w_self_t = jnp.concatenate([wmat_t[0, :, :LANES], wmat_t[1, :, :LANES]], axis=1)
    w_neigh_t = jnp.concatenate([wmat_t[0, :, LANES:], wmat_t[1, :, LANES:]], axis=1)
    h_pair_one.wait_recv()
    mixed[:, : half + halo] += dot(hs[0, :, far_cols], a_rows[:, far_cols], 1, 1)
    wait_halo(1)
    halo_one = read_halo(1)

    def mix_edge_one(cols):
        summed = mixed[:, shifted_cols(cols)] + dot(halo_one, edge_hm[:, cols])
        agg = (summed * edge_inv[0:1, cols]).astype(BF)
        return dot(w_self_t, edge_h[0, :, cols]) + dot(w_neigh_t, agg)

    def mix_one(c):
        return dot(w_self_t, hs[0, :, own_chunk(c)]) + dot(
            w_neigh_t, agg_ref[0, :, c : c + wide_cols]
        )

    norm_edge(1, mix_edge_one)
    total = mixed[:, :half] + dot(halo_one, hmt[:, own_cols])
    agg_ref[0] = (total * inv_ref[0:1, :]).astype(BF)
    norm_forward(1, mix_one)
    h_pair_two = pair_copy(hs.at[1, :, own_cols], hs.at[1, :, own_cols], 3)
    h_pair_two.start()
    mixed[:, :half] = dot(hs[1, :, own_cols], a_rows[:half, own_cols], 1, 1)
    assemble_head()
    h_pair_two.wait_recv()
    mixed[:, :half] += dot(hs[1, :, far_cols], a_rows[:half, far_cols], 1, 1)
    wait_halo(2)
    halo_two = read_halo(2)
    for c in range(0, half, wide_cols):
        cols = slice(c, c + wide_cols)
        total = mixed[:, cols] + dot(halo_two, hmt[:, own_chunk(c)])
        agg_ref[1, :, cols] = (total * inv_ref[0:1, cols]).astype(BF)

    logits = dot(head_ws_t[...], hs[1, :, own_cols]) + dot(head_wn_t[...], agg_ref[1])
    class_id = iota((CLS_PAD, half), 0)
    logits = jnp.where(class_id < CLS, logits, -1e30)
    top = jnp.max(logits, axis=0, keepdims=True)
    log_total = top + jnp.log(jnp.sum(jnp.exp(logits - top), axis=0, keepdims=True))
    onehot = class_id == label_in[0:1, own_cols]
    weight = lmask_in[0:1, own_cols].astype(F32)
    chosen = jnp.sum(jnp.where(onehot, logits, 0.0), axis=0, keepdims=True)
    loss_part = jnp.sum((log_total - chosen) * weight, axis=1, keepdims=True)
    pad_rows = grads.shape[1] - rows_all // 8 * 8
    for c in range(2):
        grads[c, rows_all // 8 * 8 :, :] = jnp.broadcast_to(loss_part, (pad_rows, HID))
    probs = jnp.exp(logits - log_total)
    g_logits = (probs - jnp.where(onehot, 1.0, 0.0)) * (weight / label_count)
    g_low[0:CLS_PAD, :] = g_logits.astype(BF)
    g_head = g_low[0:CLS_PAD, :]

    def exchange_backward(k):
        whole = pair_copy(gs_all.at[k, :, own_cols], gs_all.at[k, :, own_cols], 4 + k)
        part_tx[...] = dot(hmt[:, own_cols], gs_all[k, :, own_cols], 1, 1)
        part = pair_copy(part_tx, part_rx.at[k], 8 + k)
        part.start()
        return whole, part

    def send_back(k, part, whole):
        part.wait()
        pack_halo(3 + k, part_tx[...] + part_rx[k])
        send_halo(3 + k)
        whole.start()

    def spread(k, whole, base):
        mixed[:, :half] = dot(gs_all[k, :, own_cols], a_rows[:half, own_cols])
        norm_slope(1 - k)
        whole.wait_recv()
        mixed[:, half : 2 * half] = dot(gs_all[k, :, far_cols], b_far[...])
        mixed[:, :half] = mixed[:, :half] + mixed[:, half : 2 * half] + base()
        wait_halo(3 + k)
        return read_halo(3 + k)

    def norm_backward(layer, back):
        acc_gain[...] = jnp.zeros_like(acc_gain)
        acc_bias[...] = jnp.zeros_like(acc_bias)

        gain = norm_col[:, 2 * layer : 2 * layer + 1]
        for j in range(n_cols):
            cols = slice(j * wide_cols, (j + 1) * wide_cols)
            n = normed[layer, :, cols]
            through = mixed[:, cols] + dot(back, sel[:, own_chunk(j * wide_cols)])
            g_shift = through * slope[layer, :, cols]
            scaled = g_shift * n
            acc_gain[...] += scaled[:, :LANES] + scaled[:, LANES:]
            acc_bias[...] += g_shift[:, :LANES] + g_shift[:, LANES:]
            gn = g_shift * gain
            mean_one = jnp.mean(gn, axis=0, keepdims=True)
            mean_two = jnp.mean(gn * n, axis=0, keepdims=True)
            g_mixed = (gn - mean_one - n * mean_two) * scale_inv[layer, 0:1, cols]
            g_low[:, cols] = g_mixed.astype(BF)

        gain_row = jnp.sum(acc_gain[...].T, axis=0, keepdims=True)
        bias_row = jnp.sum(acc_bias[...].T, axis=0, keepdims=True)
        base = rows_all - 2 + layer
        for c in range(2):
            piece = slice(c * HALF_HID, (c + 1) * HALF_HID)
            grads[c, base : base + 1, :LANES] = gain_row[:, piece]
            grads[c, base : base + 1, LANES:] = bias_row[:, piece]

    early_start = shard * first_early // HID // 8 * 8
    early_rows = round_up(rows_all + 1, 8) - early_start

    norm_first = rows_all - 2
    top_start = rows_all // 8 * 8

    def lay(ref, rows):
        ref[:win, :] = rows[:, :LANES]
        ref[win:, :] = rows[:, LANES:]

    whole_window = [slice(0, 2 * win)]
    cut = 2 * win // 16 * 8
    two_parts = [slice(0, cut), slice(cut, 2 * win)]

    def stage_one(doms, far_ref, pieces):
        loss_row = grads[f, rows_all : rows_all + 1, :] + far_ref[rows_all : rows_all + 1, :]
        row = iota((win, HID), 0)
        for d in doms:
            start = shard * d // HID
            span = slice(start, start + win)
            rows = grads[f, span, :] + far_ref[span, :]
            if d == n_dom - 1:
                rows = jnp.where(row >= norm_first - start, 0.0, rows)
            rows = jnp.where(row == win - 1, loss_row, rows)

            @pl.when(low == d % group)
            def _():
                lay(one_rx.at[d // group, low], rows)

            @pl.when(low != d % group)
            def _():
                lay(one_tx.at[d], rows)

        for n, piece in enumerate(pieces):
            for d in doms:
                to_high, to_low = d // group, d % group

                @pl.when(low != to_low)
                def _():
                    send_to(
                        high * group + to_low, f, one_tx.at[d, piece, :],
                        one_rx.at[to_high, low, piece, :], one_send, one_recv.at[n, to_high],
                    )

    def top_copy(k, dst, p):
        return pltpu.make_async_remote_copy(
            src_ref=top_tx.at[k], dst_ref=dst, send_sem=top_send.at[k], recv_sem=top_recv.at[k],
            device_id=(p, f), device_id_type=MESH,
        )

    def stage_two(doms, pieces):
        for n, piece in enumerate(pieces):
            for d in doms:
                to_high, to_low = d // group, d % group

                @pl.when(low == to_low)
                def _():
                    got = one_rx.at[to_high, pl.ds(0, group - 1), piece, :]
                    pltpu.make_async_copy(got, got, one_recv.at[n, to_high]).wait()
                    total = jnp.sum(one_rx[to_high, :, piece, :], axis=0)

                    @pl.when(high == to_high)
                    def _():
                        two_rx[high, piece, :] = total

                    @pl.when(high != to_high)
                    def _():
                        two_tx[to_high, piece, :] = total
                        send_to(
                            d, f, two_tx.at[to_high, piece, :], two_rx.at[high, piece, :],
                            two_send, two_recv,
                        )

    gs_all[0, :, own_cols] = (dot(head_wn[:, :CLS_PAD], g_head) * inv_ref[0:1, :]).astype(BF)
    g_pair_two, part_two = exchange_backward(0)
    dws = dot(hs[1, :, own_cols], g_head, 1, 1)
    dwn = dot(agg_ref[1], g_head, 1, 1)
    send_back(0, part_two, g_pair_two)
    dw_head[...] = jnp.zeros_like(dw_head)
    for c in range(2):
        piece = slice(c * HALF_HID, (c + 1) * HALF_HID)
        dw_head[:HALF_HID, :CLS_PAD] = dws[piece]
        dw_head[HALF_HID:, :CLS_PAD] = dwn[piece]
        wide = roll_rows(dw_head[...], start_lane, True)
        low_part = jnp.where(lane_w >= start_lane, wide, 0.0)
        high_part = jnp.where(lane_w >= start_lane, 0.0, wide)
        stacked = jnp.concatenate([*parts(low_part), *parts(high_part)], axis=0)
        picks = jnp.concatenate([pick_a] * 3 + [pick_b] * 3, axis=1)
        flat = dot(picks, stacked)
        flat = jnp.concatenate([flat[:48], flat[48:]], axis=1)
        base = 2 * fin + 2 * HALF_HID
        grads[c, base : base + HEAD_ROWS, :] = flat[:HEAD_ROWS]
    back = spread(0, g_pair_two, lambda: dot(head_ws[:, :CLS_PAD], g_head))
    w_self = jnp.concatenate([wmat[0, :LANES], wmat[1, :LANES]], axis=0)
    w_neigh = jnp.concatenate([wmat[0, LANES:], wmat[1, LANES:]], axis=0)

    norm_backward(1, back)
    gs_all[1, :, own_cols] = (dot(w_neigh, g_low[...]) * inv_ref[0:1, :]).astype(BF)

    g_pair_one, part_one = exchange_backward(1)
    g_one = g_low[...]
    dws = dot(hs[0, :, own_cols], g_one, 1, 1)
    dwn = dot(agg_ref[0], g_one, 1, 1)
    for c in range(2):
        piece = slice(c * HALF_HID, (c + 1) * HALF_HID)
        base = 2 * fin
        grads[c, base : base + HALF_HID, :] = dws[piece]
        grads[c, base + HALF_HID : base + 2 * HALF_HID, :] = dwn[piece]

    def early_out():
        early_pair.wait()
        stage_one(range(first_early, n_dom), early_rx, whole_window)

    early_pair = pair_copy(
        grads.at[other, pl.ds(early_start, early_rows), :],
        early_rx.at[pl.ds(early_start, early_rows), :], 6,
    )
    early_pair.start()
    send_back(1, part_one, g_pair_one)
    early_out()
    back = spread(1, g_pair_one, lambda: dot(w_self, g_low[...]))
    norm_backward(0, back)
    g_zero = g_low[...]
    dws = dot(xs[:, own_cols], g_zero, 1, 1)
    dwn = dot(agg_zero[...], g_zero, 1, 1)
    for c in range(2):
        start = c * FEAT_PAD
        grads[c, 0:fin, :] = dws[start : start + fin]
        grads[c, fin : 2 * fin, :] = dwn[start : start + fin]

    low_rows = pl.ds(0, round_up(shard * (first_early - 1) // HID + win, 8))
    top_rows = pl.ds(top_start, 8)
    late_pairs = [
        pair_copy(grads.at[other, rows, :], late_rx.at[rows, :], k)
        for rows, k in ((low_rows, 12), (top_rows, 13))
    ]
    for copy in late_pairs:
        copy.start()
    for copy in late_pairs:
        copy.wait_recv()
    stage_one(range(first_early), late_rx, two_parts)
    norms = grads[f, top_rows, :] + late_rx[top_rows, :]
    top_tx[0] = norms

    @pl.when(low == group - 1)
    def _():
        top_one[low] = norms

    @pl.when(low != group - 1)
    def _():
        top_copy(0, top_one.at[low], high * group + group - 1).start()

    stage_two(range(first_early, n_dom), whole_window)
    stage_two(range(first_early), two_parts)

    @pl.when(low == group - 1)
    def _():
        part = pl.ds(0, group - 1)
        pltpu.make_async_copy(top_one.at[part], top_one.at[part], top_recv.at[0]).wait()
        norms = jnp.sum(top_one[...], axis=0)
        top_tx[1] = norms

        @pl.when(high == n_high - 1)
        def _():
            top_two[high] = norms

        @pl.when(high != n_high - 1)
        def _():
            top_copy(1, top_two.at[high], n_dom - 1).start()

    part = pl.ds(0, n_high - 1)
    pltpu.make_async_copy(two_rx.at[part], two_rx.at[part], two_recv).wait()

    @pl.when(me == n_dom - 1)
    def _():
        pltpu.make_async_copy(top_two.at[part], top_two.at[part], top_recv.at[1]).wait()
        norms = jnp.sum(top_two[...], axis=0)
        first = norm_first - shard * (n_dom - 1) // HID
        norms = norms[norm_first - top_start : norm_first - top_start + 2]
        two_rx[0, first : first + 2, :] += norms[:, :LANES]
        two_rx[0, win + first : win + first + 2, :] += norms[:, LANES:]

    flat_t[...] = jnp.sum(two_rx[...], axis=0)
    scalar_out[0:1, :] = jnp.broadcast_to(flat_t[win - 1 : win, 0:1], (1, LANES))
    scalar_out[1:2, :] = jnp.broadcast_to(label_count, (1, LANES))
    shares[...] = from_window(jnp.concatenate([flat_t[:win, :], flat_t[win:, :]], axis=1))
    for k in range(-(-shard // LANES)):
        width = min(LANES, shard - k * LANES)
        grad_out[0:1, k * LANES : k * LANES + width] = shares[k : k + 1, 0:width]

    for copy in (
        x_pair, h_pair_one, h_pair_two, g_pair_two, g_pair_one,
        *par_rest, *late_pairs,
    ):
        copy.wait_send()
    for k in range(3, 5):
        wait_halo_sent(k)
    pltpu.make_async_copy(two_tx.at[part], two_tx.at[part], two_send).wait()
    @pl.when(low != group - 1)
    def _():
        pltpu.make_async_copy(top_tx.at[0], top_tx.at[0], top_send.at[0]).wait()

    @pl.when((low == group - 1) & (high != n_high - 1))
    def _():
        pltpu.make_async_copy(top_tx.at[1], top_tx.at[1], top_send.at[1]).wait()

    part = pl.ds(0, n_dom - n_high)
    pltpu.make_async_copy(one_tx.at[part], one_tx.at[part], one_send).wait()
    n_sent = n_high - 1 + len(urgent) * (2 * group - 1) + len(patient) * (group - 1)
    while n_sent > 0:
        part = pl.ds(0, min(n_sent, n_dom) * par_rows)
        pltpu.make_async_copy(par_rx.at[f, part, :], par_rx.at[f, part, :], par_send).wait()
        n_sent -= n_dom

    @pl.when(me == n_dom - 1)
    def _():
        for step in range(1, n_high):
            pltpu.make_async_copy(norm_own, norm_own, norm_send.at[0]).wait()

    @pl.when(last_low)
    def _():
        for step in range(2 * group - 1):
            pltpu.make_async_copy(norm_own, norm_own, norm_send.at[1]).wait()


def round_up(value, step):
    return -(-value // step) * step


def per_device(n_dom, features, local_mask, halo_mask, send_rows, labels, label_mask, master, first, second):
    nodes, halo = local_mask.shape[1], halo_mask.shape[1]
    half, shard, fin = nodes // 2, master.shape[1], features.shape[1]
    rows_all = n_dom * shard // HID
    span = (shard + HID - 2) // HID + 1
    win = round_up(span + 1, 4)
    par_rows = round_up(span, 16)
    grad_rows = round_up(rows_all + win, 8)
    group = 1
    while (2 * group) ** 2 <= n_dom:
        group *= 2
    head_end = 2 * fin + 2 * HALF_HID + HEAD_ROWS
    first_early = -(-2 * fin * HID // shard)
    assert shard * (n_dom - 1) <= (rows_all - 2) * HID and rows_all % 8 > 2
    urgent = sorted({d // group for d in range(first_early)})
    cfg = dict(
        group=group, first_early=first_early, urgent=urgent,
        n_dom=n_dom, nodes=nodes, half=half, halo=halo, shard=shard, fin=fin, win=win,
        par_rows=par_rows, rows_all=rows_all, grad_rows=grad_rows,
        h_rows=nodes if halo <= 256 else LANES, slots=half // LANES if halo <= 256 else 2,
    )
    hbm = pl.BlockSpec(memory_space=pl.ANY)
    vmem = pl.BlockSpec(memory_space=pltpu.VMEM)
    i32 = jnp.int32
    pad = LANES if halo <= 256 else 0
    scratch = [
        pltpu.VMEM((8, n_dom), i32),
        pltpu.VMEM((1, nodes), i32),
        pltpu.VMEM((1, nodes), i32),
        pltpu.VMEM((1, shard), F32),
        pltpu.VMEM((2 * win, LANES), F32),
        pltpu.VMEM((cfg["slots"], LANES, nodes), i32),
        pltpu.VMEM((cfg["slots"], LANES, half), i32),
        pltpu.VMEM((cfg["h_rows"], halo), i32),
        pltpu.VMEM((fin, nodes), BF),
        pltpu.VMEM((half + halo, nodes), BF),
        pltpu.VMEM((half, half), BF),
        pltpu.VMEM((halo, nodes), BF),
        pltpu.VMEM((halo, nodes), BF),
        pltpu.VMEM((2 * FEAT_PAD, nodes), BF),
        pltpu.VMEM((2, HID, nodes), BF),
        pltpu.VMEM((2, HID, nodes), BF),
        pltpu.VMEM((2, HID, half), BF),
        pltpu.VMEM((LANES, half), BF),
        pltpu.VMEM((halo, nodes), BF),
        pltpu.VMEM((halo, halo), BF),
        pltpu.VMEM((LANES, halo), BF),
        pltpu.VMEM((2, HID, halo), BF),
        pltpu.VMEM((8, halo), F32),
        pltpu.VMEM((halo, HID), F32),
        pltpu.VMEM((2, halo, HID), F32),
        pltpu.VMEM((HID, half + max(halo, half) + pad), F32),
        pltpu.VMEM((2, HID, half + pad), F32),
        pltpu.VMEM((2, HID, half + pad), F32),
        pltpu.VMEM((2, 8, half), F32),
        pltpu.VMEM((8, half), F32),
        pltpu.VMEM((2, n_dom, 16, LANES), BF),
        pltpu.VMEM((5, n_dom, 16, LANES), BF),
        pltpu.VMEM((2 * win, LANES), F32),
        pltpu.VMEM((par_rows, HID), BF),
        pltpu.VMEM((2, n_dom * par_rows, HID), BF),
        pltpu.VMEM((2, 16, HID), BF),
        pltpu.VMEM((2, HID, HID), BF),
        pltpu.VMEM((2, HID, HID), BF),
        pltpu.VMEM((HID, 8), F32),
        pltpu.VMEM((HID, LANES), BF),
        pltpu.VMEM((HID, LANES), BF),
        pltpu.VMEM((CLS_PAD, HID), BF),
        pltpu.VMEM((CLS_PAD, HID), BF),
        pltpu.VMEM((HID, half), BF),
        pltpu.VMEM((2, grad_rows, HID), F32),
        pltpu.VMEM((grad_rows, HID), F32),
        pltpu.VMEM((grad_rows, HID), F32),
        pltpu.VMEM((n_dom, 2 * win, LANES), F32),
        pltpu.VMEM((n_dom // group, group, 2 * win, LANES), F32),
        pltpu.VMEM((n_dom // group, 2 * win, LANES), F32),
        pltpu.VMEM((n_dom // group, 2 * win, LANES), F32),
        pltpu.VMEM((2, 8, HID), F32),
        pltpu.VMEM((group, 8, HID), F32),
        pltpu.VMEM((n_dom // group, 8, HID), F32),
        pltpu.VMEM((HID, LANES), F32),
        pltpu.VMEM((HID, LANES), F32),
        pltpu.VMEM((HID, LANES), F32),
        pltpu.VMEM((ROW_NORM, n_dom * par_rows), BF),
        pltpu.SemaphoreType.DMA((8 + 2 * cfg["slots"],)),
        pltpu.SemaphoreType.DMA((24,)),
        pltpu.SemaphoreType.DMA((24,)),
        pltpu.SemaphoreType.DMA((5,)),
        pltpu.SemaphoreType.DMA((5,)),
        pltpu.SemaphoreType.DMA,
        pltpu.SemaphoreType.DMA((n_dom // group,)),
        pltpu.SemaphoreType.DMA((n_dom // group,)),
        pltpu.SemaphoreType.DMA((2,)),
        pltpu.SemaphoreType.DMA((2,)),
        pltpu.SemaphoreType.DMA,
        pltpu.SemaphoreType.DMA((2, n_dom // group)),
        pltpu.SemaphoreType.DMA,
        pltpu.SemaphoreType.DMA,
        pltpu.SemaphoreType.DMA((2,)),
        pltpu.SemaphoreType.DMA((2,)),
    ]
    grad, scalars = pl.pallas_call(
        functools.partial(kernel, cfg),
        out_shape=(
            jax.ShapeDtypeStruct((1, shard), F32),
            jax.ShapeDtypeStruct((2, LANES), F32),
        ),
        in_specs=[hbm] * 7,
        out_specs=(vmem, vmem),
        scratch_shapes=scratch,
        compiler_params=pltpu.CompilerParams(
            collective_id=0, has_side_effects=True, vmem_limit_bytes=63 * 2**20
        ),
    )(
        features.T,
        local_mask,
        halo_mask,
        send_rows[0].T,
        labels.reshape(1, nodes),
        label_mask.reshape(1, nodes),
        master,
    )
    def finish(grad_ref, scalar_ref, master_ref, first_ref, second_ref, *outs):
        loss_out, count_out, master_out, first_out, second_out = outs
        own_grad = grad_ref[...]
        new_first = DECAY_ONE * first_ref[...] + (1.0 - DECAY_ONE) * own_grad
        new_second = DECAY_TWO * second_ref[...] + (1.0 - DECAY_TWO) * own_grad * own_grad
        first_hat = new_first / (1.0 - DECAY_ONE**STEP)
        second_hat = new_second / (1.0 - DECAY_TWO**STEP)
        old = master_ref[...]
        master_out[...] = old - LEARN_RATE * (
            first_hat / (jnp.sqrt(second_hat) + ADAM_EPS) + WEIGHT_DECAY * old
        )
        first_out[...] = new_first
        second_out[...] = new_second
        loss_out[...] = scalar_ref[0:1, 0:1]
        count_out[...] = scalar_ref[1:2, 0:1]

    one, own_shape = jax.ShapeDtypeStruct((1, 1), F32), jax.ShapeDtypeStruct((1, shard), F32)
    loss, count, *updated = pl.pallas_call(
        finish, out_shape=(one, one, own_shape, own_shape, own_shape),
        in_specs=[vmem] * 5, out_specs=(vmem,) * 5,
    )(grad, scalars, master, first, second)
    return (loss[0, 0], count[0, 0], *updated)


def solution(mesh):
    in_specs = (
        P("dom", "feat"),
        P("dom", None),
        P("dom", None),
        P("dom", None, None),
        P("dom"),
        P("dom"),
        P("feat", "dom"),
        P("feat", "dom"),
        P("feat", "dom"),
    )
    out_specs = (P(), P(), P("feat", "dom"), P("feat", "dom"), P("feat", "dom"))
    return jax.shard_map(
        functools.partial(per_device, mesh.shape["dom"]),
        mesh=mesh, in_specs=in_specs, out_specs=out_specs, check_vma=False,
    )
```

```python
import functools

import jax
import jax.numpy as jnp
from jax import lax
from jax.experimental import pallas as pl
from jax.experimental.pallas import tpu as pltpu
from jax.sharding import PartitionSpec as P

HID = 256
CLS = 47
STEP = 10
EPSILON = 1e-05
LEARN_RATE = 0.02
DECAY_ONE = 0.9
DECAY_TWO = 0.999
ADAM_EPS = 1e-08
WEIGHT_DECAY = 0.01

MESH = pl.DeviceIdType.MESH
BF = jnp.bfloat16
F32 = jnp.float32
LANES = 128
CLS_PAD = 64
FEAT_PAD = 64
HALF_HID = HID // 2
ROW_ONE = 2 * FEAT_PAD
ROW_TWO = ROW_ONE + 2 * HALF_HID
HEAD_ROWS = 2 * HALF_HID * CLS // HID
ROW_NORM = ROW_TWO + 48
GELU_A = 0.7978845608028654
GELU_B = 0.044715


def dot(a, b, ca=1, cb=0, precision=None):
    return lax.dot_general(
        a, b, (((ca,), (cb,)), ((), ())), precision=precision, preferred_element_type=F32
    )


def iota(shape, axis):
    return lax.broadcasted_iota(jnp.int32, shape, axis)


def gelu(x):
    half = 0.5 * x
    return half + half * jnp.tanh(x * (GELU_A + (GELU_A * GELU_B) * (x * x)))


def gelu_grad(x):
    xx = x * x
    t = jnp.tanh(x * (GELU_A + (GELU_A * GELU_B) * xx))
    return 0.5 + 0.5 * t + (x * (GELU_A + (3.0 * GELU_A * GELU_B) * xx)) * (0.5 - 0.5 * (t * t))


def roll_rows(x, amount, right):
    for bit in range(7):
        step = 1 << bit
        moved = pltpu.roll(x, step if right else LANES - step, 1)
        x = jnp.where((amount & step) != 0, moved, x)
    return x


def parts(x):
    first = x.astype(BF)
    rest = x - first.astype(F32)
    second = rest.astype(BF)
    return first, second, (rest - second.astype(F32)).astype(BF)


def loop(n, body):
    def step(i, carry):
        body(i)
        return carry

    lax.fori_loop(0, n, step, 0)


def kernel(
    cfg,
    x_in, lm_in, hm_in, send_hbm, label_hbm, lmask_hbm, master_hbm,
    grad_out, scalar_out,
    send_in, label_in, lmask_in, master_in, shares,
    a_stage, b_stage, h_stage, x_stage,
    a_rows, b_far, hmt, sel, xs, hs, gs_all, agg_ref, agg_zero,
    edge_far, edge_hm, edge_x, edge_h, edge_inv, part_tx, part_rx,
    mixed, normed, slope, scale_inv, inv_ref, halo_tx, halo_rx,
    flat_t, par_tx, par_rx, norm_rx, wmat, wmat_t, norm_col, head_ws, head_wn, head_ws_t, head_wn_t,
    g_low, grads, early_rx, late_rx, one_tx, one_rx, two_tx, two_rx, top_tx, top_one, top_two, dw_head, acc_gain, acc_bias, place,
    local_sem, pair_send, pair_recv, halo_send, halo_recv, par_send, column_recv, plane_recv, norm_send, norm_recv,
    one_send, one_recv, two_send, two_recv, top_send, top_recv,
):
    n_dom, nodes, half, halo, shard, fin = (
        cfg["n_dom"], cfg["nodes"], cfg["half"], cfg["halo"], cfg["shard"], cfg["fin"]
    )
    win, par_rows, rows_all = cfg["win"], cfg["par_rows"], cfg["rows_all"]
    me, f = lax.axis_index("dom"), lax.axis_index("feat")
    other = 1 - f
    own = pl.multiple_of(f * half, half)
    far = pl.multiple_of(other * half, half)
    own_cols, far_cols = pl.ds(own, half), pl.ds(far, half)

    group = cfg["group"]
    n_high = n_dom // group
    high, low = me // group, lax.rem(me, group)
    barrier = pltpu.get_barrier_semaphore()

    def greet(p, core):
        pl.semaphore_signal(barrier, inc=1, device_id=(p, core), device_id_type=MESH)

    loop(n_dom - 1, lambda i: greet(lax.rem(me + i + 1, n_dom), f))
    for step in range(group):
        greet(high * group + lax.rem(low + step, group), other)

    chunk = 128
    n_chunk = half // chunk
    x_copy = pltpu.make_async_copy(x_in, x_stage, local_sem.at[6])
    x_copy.start()
    small_copies = [
        pltpu.make_async_copy(src, dst, local_sem.at[k])
        for k, (src, dst) in enumerate(
            ((master_hbm, master_in), (send_hbm, send_in), (label_hbm, label_in),
             (lmask_hbm, lmask_in))
        )
    ]
    for copy in small_copies:
        copy.start()
    h_rows = cfg["h_rows"]

    def h_copy(i):
        return pltpu.make_async_copy(
            hm_in.at[pl.ds(i * h_rows, h_rows), :], h_stage, local_sem.at[7]
        )

    h_copy(0).start()

    slots = cfg["slots"]

    def a_copy(i):
        return pltpu.make_async_copy(
            lm_in.at[pl.ds(pl.multiple_of(own + i * chunk, chunk), chunk), :],
            a_stage.at[lax.rem(i, slots)], local_sem.at[8 + lax.rem(i, slots)],
        )

    def b_copy(i):
        return pltpu.make_async_copy(
            lm_in.at[pl.ds(pl.multiple_of(far + i * chunk, chunk), chunk), own_cols],
            b_stage.at[lax.rem(i, slots)], local_sem.at[8 + slots + lax.rem(i, slots)],
        )

    loop(slots, lambda i: a_copy(i).start())
    loop(slots, lambda i: b_copy(i).start())

    def pair_copy(src, dst, k):
        return pltpu.make_async_remote_copy(
            src_ref=src, dst_ref=dst, send_sem=pair_send.at[k], recv_sem=pair_recv.at[k],
            device_id=(me, other), device_id_type=MESH,
        )

    x_copy.wait()
    slice_rows = pl.ds(pl.multiple_of(f * FEAT_PAD, FEAT_PAD), FEAT_PAD)
    pad_rows = iota((FEAT_PAD, half), 0)
    for c in range(2):
        part = slice(c * half, (c + 1) * half)
        mixed[0:FEAT_PAD, :half] = jnp.where(pad_rows == fin, 1.0, 0.0)
        mixed[0:fin, :half] = x_stage[:, part].astype(F32)
        xs[slice_rows, part] = mixed[0:FEAT_PAD, :half].astype(BF)

    small_copies[1].wait()
    send_rows = send_in[...].astype(F32)
    lane_d = iota(send_rows.shape, 1)
    node_lane = iota((16, nodes), 1).astype(F32)

    def build_sel(q):
        first = jnp.sum(jnp.where(lane_d == 2 * q, send_rows, 0.0), axis=1, keepdims=True)
        second = jnp.sum(jnp.where(lane_d == 2 * q + 1, send_rows, 0.0), axis=1, keepdims=True)
        rows = jnp.concatenate([first, second], axis=0)
        sel[pl.ds(pl.multiple_of(q * 16, 16), 16), :] = jnp.where(
            node_lane == rows, 1.0, 0.0
        ).astype(BF)

    if n_dom <= 16:
        for q in range(n_dom // 2):
            build_sel(q)
    else:
        loop(n_dom // 2, build_sel)

    def halo_copy(k, p):
        return pltpu.make_async_remote_copy(
            src_ref=halo_tx.at[k % 2, p], dst_ref=halo_rx.at[k, me],
            send_sem=halo_send.at[k], recv_sem=halo_recv.at[k],
            device_id=(p, f), device_id_type=MESH,
        )

    def send_halo(k):
        loop(n_dom - 1, lambda i: halo_copy(k, lax.rem(me + i + 1, n_dom)).start())
        halo_rx[k, me] = halo_tx[k % 2, me]

    def pack_halo(k, rows):
        v = rows.reshape(n_dom, 8, HID)
        if k >= 2:
            wait_halo_sent(k - 2)
        halo_tx[k % 2] = jnp.concatenate([v[:, :, :LANES], v[:, :, LANES:]], axis=1).astype(BF)

    def wait_halo(k):
        part = pl.ds(0, n_dom - 1)
        pltpu.make_async_copy(halo_rx.at[k, part], halo_rx.at[k, part], halo_recv.at[k]).wait()

    def wait_halo_sent(k):
        part = pl.ds(0, n_dom - 1)
        pltpu.make_async_copy(
            halo_tx.at[k % 2, part], halo_tx.at[k % 2, part], halo_send.at[k]
        ).wait()

    def read_halo(k):
        v = halo_rx[k].astype(F32)
        rows = jnp.concatenate(
            [v[:, :8, :].reshape(halo, LANES), v[:, 8:, :].reshape(halo, LANES)], axis=1
        )
        return rows.T.astype(BF)

    def build_place(q):
        rows = pl.ds(pl.multiple_of(q * 16, 16), 16)
        r_pad = iota((16, k_all), 0) + q * 16
        k_col = iota((16, k_all), 1)
        owner, inner = k_col // par_rows, lax.rem(k_col, par_rows)
        target = lax.shift_right_logical(owner * shard, 8) + inner
        row_of = jnp.where(
            r_pad < fin, r_pad,
            jnp.where(
                (r_pad >= FEAT_PAD) & (r_pad < FEAT_PAD + fin), r_pad - (FEAT_PAD - fin),
                jnp.where(
                    (r_pad >= ROW_ONE) & (r_pad < ROW_TWO + HEAD_ROWS),
                    r_pad - (ROW_ONE - 2 * fin), -1,
                ),
            ),
        )
        place[rows, :] = jnp.where(row_of == target, 1.0, 0.0).astype(BF)

    k_all = n_dom * par_rows
    loop(ROW_NORM // 16, build_place)
    for i in range(nodes // h_rows):
        h_copy(i).wait()
        hmt[:, i * h_rows : (i + 1) * h_rows] = h_stage[...].astype(F32).T.astype(BF)
        if (i + 1) * h_rows < nodes:
            h_copy(i + 1).start()

    def convert_a(i):
        a_copy(i).wait()
        rows = pl.ds(pl.multiple_of(i * chunk, chunk), chunk)
        a_rows[rows, :] = a_stage[lax.rem(i, slots)].astype(F32).astype(BF)

        @pl.when(i + slots < n_chunk)
        def _():
            a_copy(i + slots).start()

    pl.semaphore_wait(barrier, n_dom - 1 + group)

    x_pair = pair_copy(xs.at[slice_rows, :], xs.at[slice_rows, :], 0)
    x_pair.start()
    off = lax.rem(shard * me, HID)
    off_row, off_lane = off // LANES, lax.rem(off, LANES)
    t_rows = 2 * win
    lane_t = iota((t_rows, LANES), 1)

    def to_window(t):
        r = pltpu.roll(t, off_lane, 1)
        t = jnp.where(lane_t < off_lane, pltpu.roll(r, 1, 0), r)
        t = jnp.where(off_row == 1, pltpu.roll(t, 1, 0), t)
        flat_t[...] = t
        return jnp.concatenate(
            [flat_t[pl.ds(0, win, stride=2), :], flat_t[pl.ds(1, win, stride=2), :]], axis=1
        )

    def from_window(w):
        flat_t[pl.ds(0, win, stride=2), :] = w[:, :LANES]
        flat_t[pl.ds(1, win, stride=2), :] = w[:, LANES:]
        t = flat_t[...]
        t = jnp.where(off_row == 1, pltpu.roll(t, t_rows - 1, 0), t)
        back = lax.rem(LANES - off_lane, LANES)
        near = pltpu.roll(t, back, 1)
        after = pltpu.roll(near, t_rows - 1, 0)
        return jnp.where(lane_t + off_lane < LANES, near, after)

    small_copies[0].wait()
    shares[...] = jnp.zeros_like(shares)

    for k in range(-(-shard // LANES)):
        width = min(LANES, shard - k * LANES)
        shares[k : k + 1, 0:width] = master_in[0:1, k * LANES : k * LANES + width]
    window = to_window(shares[...])
    if par_rows > win:
        window = jnp.concatenate([window, jnp.zeros((par_rows - win, HID), F32)], axis=0)
    par_tx[...] = window.astype(BF)
    par_rx[f, pl.ds(pl.multiple_of(me * par_rows, par_rows), par_rows), :] = par_tx[...]


    urgent = cfg["urgent"]
    patient = [h for h in range(n_high) if h not in urgent]

    def par_slot(h, w):
        start = pl.multiple_of((h * group + w) * par_rows, par_rows)
        return par_rx.at[f, pl.ds(start, par_rows), :]

    def send_to(p, core, src, dst, send_sem, recv_sem):
        pltpu.make_async_remote_copy(
            src_ref=src, dst_ref=dst, send_sem=send_sem, recv_sem=recv_sem,
            device_id=(p, core), device_id_type=MESH,
        ).start()

    def to_plane(src, dst, send_sem, recv_sem, both):
        if both:
            send_to(me, other, src, dst, send_sem, recv_sem)
        for step in range(1, group):
            p = high * group + lax.rem(low + step, group)
            send_to(p, f, src, dst, send_sem, recv_sem)
            if both:
                send_to(p, other, src, dst, send_sem, recv_sem)

    def to_column(src, dst, send_sem, recv_sem):
        for step in range(1, n_high):
            p = lax.rem(high + step, n_high) * group + low
            send_to(p, f, src, dst, send_sem, recv_sem)

    def any_of(which):
        return functools.reduce(jnp.logical_or, [high == h for h in which])

    def own_params(which):
        @pl.when(any_of(which))
        def _():
            to_plane(
                par_tx, par_slot(high, low), par_send, plane_recv.at[high], which is urgent
            )

    def forward_params(which):
        for h in which:
            @pl.when(high != h)
            def _():
                pltpu.make_async_copy(par_tx, par_tx, column_recv.at[h]).wait()
                to_plane(
                    par_slot(h, low), par_slot(h, low), par_send, plane_recv.at[h],
                    which is urgent,
                )

    def wait_params(which):
        part = pl.ds(0, (2 * group - 1 if which is urgent else group - 1) * par_rows)
        for h in which:
            pltpu.make_async_copy(
                par_rx.at[f, part, :], par_rx.at[f, part, :], plane_recv.at[h]
            ).wait()

    norm_local = rows_all - 2 - shard * (n_dom - 1) // HID
    norm_block = norm_local // 16 * 16
    norm_own = norm_rx.at[f]
    last_low = low == group - 1

    def send_norms():
        @pl.when(me == n_dom - 1)
        def _():
            norm_rx[f] = par_tx[norm_block : norm_block + 16, :]
            to_column(norm_own, norm_own, norm_send.at[0], norm_recv.at[0])

    def forward_norms():
        @pl.when(last_low)
        def _():
            @pl.when(high != n_high - 1)
            def _():
                pltpu.make_async_copy(norm_own, norm_own, norm_recv.at[0]).wait()

            to_plane(norm_own, norm_own, norm_send.at[1], norm_recv.at[1], True)

    def wait_norms():
        @pl.when(last_low)
        def _():
            pltpu.make_async_copy(norm_own, norm_own, norm_recv.at[1]).wait()

        @pl.when(jnp.logical_not(last_low))
        def _():
            pltpu.make_async_copy(norm_rx, norm_rx, norm_recv.at[1]).wait()

    def par_pairs(which, k):
        runs = []
        for h in which:
            if runs and runs[-1][1] == h:
                runs[-1][1] = h + 1
            else:
                runs.append([h, h + 1])
        copies = []
        for i, (start, end) in enumerate(runs):
            part = pl.ds(start * group * par_rows, (end - start) * group * par_rows)
            copies.append(pair_copy(par_rx.at[f, part, :], par_rx.at[f, part, :], k + i))
        return copies

    first_early = cfg["first_early"]
    to_column(par_tx, par_slot(high, low), par_send, column_recv.at[high])
    own_params(urgent)
    send_norms()
    loop(n_chunk, convert_a)
    edge_hm[...] = dot(hmt[...], sel[...], 1, 1).astype(BF)

    def edge_chunk(q):
        rows = pl.ds(pl.multiple_of(q * LANES, LANES), LANES)
        a_rows[pl.ds(pl.multiple_of(half + q * LANES, LANES), LANES), :] = dot(
            sel[rows, own_cols], a_rows[:half, :]
        ).astype(BF)

    loop(halo // LANES, edge_chunk)
    edge_pair = pair_copy(a_rows.at[pl.ds(half, halo), :], edge_far, 7)
    edge_pair.start()
    x_pair.wait_recv()
    picked = dot(sel[...], xs[...], 1, 1)
    edge_x[...] = picked.T.astype(BF)
    picked = picked.reshape(n_dom, 8, LANES)
    small_copies[2].wait()
    small_copies[3].wait()
    count = jnp.sum(lmask_in[...].astype(F32), axis=1, keepdims=True)
    count_high = jnp.floor(count * (1.0 / 256.0))
    count_low = count - 256.0 * count_high
    count_row = iota((8, LANES), 0)
    counts = jnp.where(count_row == 0, count_high, jnp.where(count_row == 1, count_low, 0.0))
    counts = jnp.broadcast_to(counts[None], (n_dom, 8, LANES))
    halo_tx[0] = jnp.concatenate([picked, counts], axis=1).astype(BF)
    send_halo(0)

    forward_params(urgent)
    forward_norms()
    own_params(patient)
    forward_params(patient)
    mixed[0:LANES, :half] = dot(xs[...], a_rows[:half, :], 1, 1)
    def convert_b(i):
        b_copy(i).wait()
        rows = pl.ds(pl.multiple_of(i * chunk, chunk), chunk)
        b_far[rows, :] = b_stage[lax.rem(i, slots)].astype(F32).astype(BF)

        @pl.when(i + slots < n_chunk)
        def _():
            b_copy(i + slots).start()

    loop(n_chunk, convert_b)

    edge_pair.wait()

    def edge_sum(q):
        rows = pl.ds(pl.multiple_of(q * LANES, LANES), LANES)
        ext = pl.ds(pl.multiple_of(half + q * LANES, LANES), LANES)
        a_rows[ext, :] = a_rows[ext, :] + edge_far[rows, :]

    loop(halo // LANES, edge_sum)
    mixed[0:LANES, half : half + halo] = dot(xs[...], a_rows[half:, :], 1, 1)
    wait_params(urgent)
    wait_norms()
    wait_halo(0)
    arrived = halo_rx[0].astype(F32)
    halo_zero = arrived[:, :8, :].reshape(halo, LANES).T.astype(BF)
    count_all = jnp.sum(arrived[:, 8:, :], axis=0)
    label_count = 256.0 * count_all[0:1, 0:1] + count_all[1:2, 0:1]
    k_first = first_early * par_rows
    w_zero = []
    for c in range(2):
        rows_t = dot(place[:ROW_ONE, :k_first], par_rx[c, :k_first, :]).T
        w_zero.append(rows_t.astype(BF))
        norms_t = jnp.concatenate(
            [norm_rx[c].astype(F32), jnp.zeros((LANES - 16, HID), F32)], axis=0
        ).T
        for k in range(2):
            lane = norm_local - norm_block + k
            col = norms_t[:, lane : lane + 1]
            norm_col[c * HALF_HID : (c + 1) * HALF_HID, 2 * k : 2 * k + 1] = col[:HALF_HID]
            norm_col[c * HALF_HID : (c + 1) * HALF_HID, 2 * k + 1 : 2 * k + 2] = col[HALF_HID:]
    w_zero = jnp.concatenate(w_zero, axis=1)

    def assemble_hidden():
        for c in range(2):
            rows = dot(place[ROW_ONE:ROW_TWO, :], par_rx[c])
            wmat[c] = rows.astype(BF)
            wmat_t[c] = rows.T.astype(BF)

    place_row = iota((2 * 48, HID), 0)
    flat_row = jnp.where(place_row < 48, 2 * place_row, 2 * (place_row - 48) + 1)
    first_row = lax.shift_right_logical(iota((2 * 48, HID), 1) * CLS, 7)
    pick_a = jnp.where(flat_row == first_row, 1.0, 0.0).astype(BF)
    pick_b = jnp.where(flat_row == first_row + 1, 1.0, 0.0).astype(BF)
    start_lane = (iota((HID, LANES), 0) * CLS) & (LANES - 1)
    lane_w = iota((HID, LANES), 1)

    def assemble_head():
        for c in range(2):
            flat = dot(place[ROW_TWO:ROW_NORM, :], par_rx[c]).astype(BF)
            flat = jnp.concatenate([flat[:, :LANES], flat[:, LANES:]], axis=0)
            wide = jnp.where(lane_w >= start_lane, dot(pick_a, flat, 0, 0), dot(pick_b, flat, 0, 0))
            head = jnp.where(lane_w < CLS, roll_rows(wide, start_lane, False), 0.0)
            head_t = head.T[:CLS_PAD]
            half_rows = slice(c * HALF_HID, (c + 1) * HALF_HID)
            head_ws[half_rows, :] = head[:HALF_HID].astype(BF)
            head_wn[half_rows, :] = head[HALF_HID:].astype(BF)
            head_ws_t[:, half_rows] = head_t[:, :HALF_HID].astype(BF)
            head_wn_t[:, half_rows] = head_t[:, HALF_HID:].astype(BF)

    wide_cols = 256
    n_cols = half // wide_cols

    def norm_apply(x, layer):
        centre = x - jnp.mean(x, axis=0, keepdims=True)
        rs = lax.rsqrt(jnp.mean(centre * centre, axis=0, keepdims=True) + EPSILON)
        n = centre * rs
        shifted = n * norm_col[:, 2 * layer : 2 * layer + 1] + norm_col[
            :, 2 * layer + 1 : 2 * layer + 2
        ]
        return n, rs, gelu(shifted).astype(BF)

    def h_part(layer, n):
        cols = pl.ds(pl.multiple_of(own + n * (half // 2), half // 2), half // 2)
        return pair_copy(hs.at[layer, :, cols], hs.at[layer, :, cols], 2 + layer + 12 * n)

    h_pairs = [[h_part(layer, n) for n in range(2)] for layer in range(2)]

    def norm_forward(layer, mix):
        for j in range(n_cols):
            cols = slice(j * wide_cols, (j + 1) * wide_cols)
            n, rs, value = norm_apply(mix(j * wide_cols), layer)
            normed[layer, :, cols] = n
            scale_inv[layer, :, cols] = jnp.broadcast_to(rs, (8, wide_cols))
            out = pl.ds(pl.multiple_of(own + j * wide_cols, wide_cols), wide_cols)
            hs[layer, :, out] = value
            if (j + 1) % (n_cols // 2) == 0:
                h_pairs[layer][j // (n_cols // 2)].start()

    def norm_slope(layer):
        for c in range(0, half, wide_cols):
            cols = slice(c, c + wide_cols)
            shifted = normed[layer, :, cols] * norm_col[
                :, 2 * layer : 2 * layer + 1
            ] + norm_col[:, 2 * layer + 1 : 2 * layer + 2]
            slope[layer, :, cols] = gelu_grad(shifted)

    def norm_edge(layer, mix):
        for j in range(halo // LANES):
            cols = slice(j * LANES, (j + 1) * LANES)
            edge_h[layer, :, cols] = norm_apply(mix(cols), layer)[2]

        pack_halo(1 + layer, edge_h[layer].astype(F32).T)
        send_halo(1 + layer)

    def rows_of(x, agg):
        return jnp.concatenate([x[:FEAT_PAD], agg[:FEAT_PAD], x[FEAT_PAD:], agg[FEAT_PAD:]], axis=0)

    def aggregate_zero(summed, inv_at, cols):
        inverse = 1.0 / jnp.maximum(summed[fin : fin + 1, :], 1.0)
        inv_at[:, cols] = jnp.broadcast_to(inverse, (8, summed.shape[1]))
        return (summed * inverse).astype(BF)

    def shifted_cols(cols):
        return slice(half + cols.start, half + cols.stop)

    def own_chunk(c):
        return pl.ds(pl.multiple_of(own + c, wide_cols), wide_cols)

    def mix_edge_zero(cols):
        agg = aggregate_zero(
            mixed[0:LANES, shifted_cols(cols)] + dot(halo_zero, edge_hm[:, cols]), edge_inv, cols
        )
        return dot(w_zero, rows_of(edge_x[:, cols], agg))

    def mix_zero(c):
        return dot(w_zero, rows_of(xs[:, own_chunk(c)], agg_zero[:, c : c + wide_cols]))

    norm_edge(0, mix_edge_zero)
    wait_params(patient)
    par_rest = par_pairs(patient, 20)
    for copy in par_rest:
        copy.start()
    agg_zero[...] = aggregate_zero(
        mixed[0:LANES, :half] + dot(halo_zero, hmt[:, own_cols]), inv_ref, slice(0, half)
    )
    norm_forward(0, mix_zero)
    mixed[:, :half] = dot(hs[0, :, own_cols], a_rows[:half, own_cols], 1, 1)
    for copy in par_rest:
        copy.wait_recv()
    assemble_hidden()
    w_self_t = jnp.concatenate([wmat_t[0, :, :LANES], wmat_t[1, :, :LANES]], axis=1)
    w_neigh_t = jnp.concatenate([wmat_t[0, :, LANES:], wmat_t[1, :, LANES:]], axis=1)
    for copy in h_pairs[0]:
        copy.wait_recv()
    mixed[:, half : half + halo] = dot(hs[0], a_rows[half:, :], 1, 1)
    wait_halo(1)
    halo_one = read_halo(1)

    def mix_edge_one(cols):
        summed = mixed[:, shifted_cols(cols)] + dot(halo_one, edge_hm[:, cols])
        agg = (summed * edge_inv[0:1, cols]).astype(BF)
        return dot(w_self_t, edge_h[0, :, cols]) + dot(w_neigh_t, agg)

    def mix_one(c):
        return dot(w_self_t, hs[0, :, own_chunk(c)]) + dot(
            w_neigh_t, agg_ref[0, :, c : c + wide_cols]
        )

    norm_edge(1, mix_edge_one)
    mixed[:, :half] += dot(hs[0, :, far_cols], a_rows[:half, far_cols], 1, 1)
    total = mixed[:, :half] + dot(halo_one, hmt[:, own_cols])
    agg_ref[0] = (total * inv_ref[0:1, :]).astype(BF)
    norm_forward(1, mix_one)
    mixed[:, :half] = dot(hs[1, :, own_cols], a_rows[:half, own_cols], 1, 1)
    assemble_head()
    for copy in h_pairs[1]:
        copy.wait_recv()
    mixed[:, :half] += dot(hs[1, :, far_cols], a_rows[:half, far_cols], 1, 1)
    wait_halo(2)
    halo_two = read_halo(2)
    for c in range(0, half, wide_cols):
        cols = slice(c, c + wide_cols)
        total = mixed[:, cols] + dot(halo_two, hmt[:, own_chunk(c)])
        agg_ref[1, :, cols] = (total * inv_ref[0:1, cols]).astype(BF)

    logits = dot(head_ws_t[...], hs[1, :, own_cols]) + dot(head_wn_t[...], agg_ref[1])
    class_id = iota((CLS_PAD, half), 0)
    logits = jnp.where(class_id < CLS, logits, -1e30)
    top = jnp.max(logits, axis=0, keepdims=True)
    log_total = top + jnp.log(jnp.sum(jnp.exp(logits - top), axis=0, keepdims=True))
    onehot = class_id == label_in[0:1, own_cols]
    weight = lmask_in[0:1, own_cols].astype(F32)
    chosen = jnp.sum(jnp.where(onehot, logits, 0.0), axis=0, keepdims=True)
    loss_part = jnp.sum((log_total - chosen) * weight, axis=1, keepdims=True)
    pad_rows = grads.shape[1] - rows_all // 8 * 8
    for c in range(2):
        grads[c, rows_all // 8 * 8 :, :] = jnp.broadcast_to(loss_part, (pad_rows, HID))
    probs = jnp.exp(logits - log_total)
    g_logits = (probs - jnp.where(onehot, 1.0, 0.0)) * (weight / label_count)
    g_low[0:CLS_PAD, :] = g_logits.astype(BF)
    g_head = g_low[0:CLS_PAD, :]

    def exchange_backward(k):
        whole = pair_copy(gs_all.at[k, :, own_cols], gs_all.at[k, :, own_cols], 4 + k)
        part_tx[...] = dot(hmt[:, own_cols], gs_all[k, :, own_cols], 1, 1)
        part = pair_copy(part_tx, part_rx.at[k], 8 + k)
        part.start()
        return whole, part

    def send_back(k, part, whole):
        part.wait()
        pack_halo(3 + k, part_tx[...] + part_rx[k])
        send_halo(3 + k)
        whole.start()

    def spread(k, whole, base):
        mixed[:, :half] = dot(gs_all[k, :, own_cols], a_rows[:half, own_cols])
        norm_slope(1 - k)
        whole.wait_recv()
        mixed[:, half : 2 * half] = dot(gs_all[k, :, far_cols], b_far[...])
        mixed[:, :half] = mixed[:, :half] + mixed[:, half : 2 * half] + base()
        wait_halo(3 + k)
        return read_halo(3 + k)

    def norm_backward(layer, back):
        acc_gain[...] = jnp.zeros_like(acc_gain)
        acc_bias[...] = jnp.zeros_like(acc_bias)

        gain = norm_col[:, 2 * layer : 2 * layer + 1]
        for j in range(n_cols):
            cols = slice(j * wide_cols, (j + 1) * wide_cols)
            n = normed[layer, :, cols]
            through = mixed[:, cols] + dot(back, sel[:, own_chunk(j * wide_cols)])
            g_shift = through * slope[layer, :, cols]
            scaled = g_shift * n
            acc_gain[...] += scaled[:, :LANES] + scaled[:, LANES:]
            acc_bias[...] += g_shift[:, :LANES] + g_shift[:, LANES:]
            gn = g_shift * gain
            mean_one = jnp.mean(gn, axis=0, keepdims=True)
            mean_two = jnp.mean(gn * n, axis=0, keepdims=True)
            g_mixed = (gn - mean_one - n * mean_two) * scale_inv[layer, 0:1, cols]
            g_low[:, cols] = g_mixed.astype(BF)

        gain_row = jnp.sum(acc_gain[...].T, axis=0, keepdims=True)
        bias_row = jnp.sum(acc_bias[...].T, axis=0, keepdims=True)
        base = rows_all - 2 + layer
        for c in range(2):
            piece = slice(c * HALF_HID, (c + 1) * HALF_HID)
            grads[c, base : base + 1, :LANES] = gain_row[:, piece]
            grads[c, base : base + 1, LANES:] = bias_row[:, piece]

    early_start = shard * first_early // HID // 8 * 8
    early_rows = round_up(rows_all + 1, 8) - early_start

    norm_first = rows_all - 2
    top_start = rows_all // 8 * 8

    def lay(ref, rows):
        ref[:win, :] = rows[:, :LANES]
        ref[win:, :] = rows[:, LANES:]

    whole_window = [slice(0, 2 * win)]
    cut = 2 * win // 16 * 8
    two_parts = [slice(0, cut), slice(cut, 2 * win)]

    def stage_one(doms, far_ref, pieces):
        loss_row = grads[f, rows_all : rows_all + 1, :] + far_ref[rows_all : rows_all + 1, :]
        row = iota((win, HID), 0)
        for d in doms:
            start = shard * d // HID
            span = slice(start, start + win)
            rows = grads[f, span, :] + far_ref[span, :]
            if d == n_dom - 1:
                rows = jnp.where(row >= norm_first - start, 0.0, rows)
            rows = jnp.where(row == win - 1, loss_row, rows)

            @pl.when(low == d % group)
            def _():
                lay(one_rx.at[d // group, low], rows)

            @pl.when(low != d % group)
            def _():
                lay(one_tx.at[d], rows)

        for n, piece in enumerate(pieces):
            for d in doms:
                to_high, to_low = d // group, d % group

                @pl.when(low != to_low)
                def _():
                    send_to(
                        high * group + to_low, f, one_tx.at[d, piece, :],
                        one_rx.at[to_high, low, piece, :], one_send, one_recv.at[n, to_high],
                    )

    def top_copy(k, dst, p):
        return pltpu.make_async_remote_copy(
            src_ref=top_tx.at[k], dst_ref=dst, send_sem=top_send.at[k], recv_sem=top_recv.at[k],
            device_id=(p, f), device_id_type=MESH,
        )

    def stage_two(doms, pieces):
        for n, piece in enumerate(pieces):
            for d in doms:
                to_high, to_low = d // group, d % group

                @pl.when(low == to_low)
                def _():
                    got = one_rx.at[to_high, pl.ds(0, group - 1), piece, :]
                    pltpu.make_async_copy(got, got, one_recv.at[n, to_high]).wait()
                    total = jnp.sum(one_rx[to_high, :, piece, :], axis=0)

                    @pl.when(high == to_high)
                    def _():
                        two_rx[high, piece, :] = total

                    @pl.when(high != to_high)
                    def _():
                        two_tx[to_high, piece, :] = total
                        send_to(
                            d, f, two_tx.at[to_high, piece, :], two_rx.at[high, piece, :],
                            two_send, two_recv,
                        )

    gs_all[0, :, own_cols] = (dot(head_wn[:, :CLS_PAD], g_head) * inv_ref[0:1, :]).astype(BF)
    g_pair_two, part_two = exchange_backward(0)
    dws = dot(hs[1, :, own_cols], g_head, 1, 1)
    dwn = dot(agg_ref[1], g_head, 1, 1)
    send_back(0, part_two, g_pair_two)
    dw_head[...] = jnp.zeros_like(dw_head)
    for c in range(2):
        piece = slice(c * HALF_HID, (c + 1) * HALF_HID)
        dw_head[:HALF_HID, :CLS_PAD] = dws[piece]
        dw_head[HALF_HID:, :CLS_PAD] = dwn[piece]
        wide = roll_rows(dw_head[...], start_lane, True)
        low_part = jnp.where(lane_w >= start_lane, wide, 0.0)
        high_part = jnp.where(lane_w >= start_lane, 0.0, wide)
        stacked = jnp.concatenate([*parts(low_part), *parts(high_part)], axis=0)
        picks = jnp.concatenate([pick_a] * 3 + [pick_b] * 3, axis=1)
        flat = dot(picks, stacked)
        flat = jnp.concatenate([flat[:48], flat[48:]], axis=1)
        base = 2 * fin + 2 * HALF_HID
        grads[c, base : base + HEAD_ROWS, :] = flat[:HEAD_ROWS]
    back = spread(0, g_pair_two, lambda: dot(head_ws[:, :CLS_PAD], g_head))
    w_self = jnp.concatenate([wmat[0, :LANES], wmat[1, :LANES]], axis=0)
    w_neigh = jnp.concatenate([wmat[0, LANES:], wmat[1, LANES:]], axis=0)

    norm_backward(1, back)
    gs_all[1, :, own_cols] = (dot(w_neigh, g_low[...]) * inv_ref[0:1, :]).astype(BF)

    g_pair_one, part_one = exchange_backward(1)
    g_one = g_low[...]
    dws = dot(hs[0, :, own_cols], g_one, 1, 1)
    dwn = dot(agg_ref[0], g_one, 1, 1)
    for c in range(2):
        piece = slice(c * HALF_HID, (c + 1) * HALF_HID)
        base = 2 * fin
        grads[c, base : base + HALF_HID, :] = dws[piece]
        grads[c, base + HALF_HID : base + 2 * HALF_HID, :] = dwn[piece]

    def early_out():
        early_pair.wait()
        stage_one(range(first_early, n_dom), early_rx, whole_window)

    early_pair = pair_copy(
        grads.at[other, pl.ds(early_start, early_rows), :],
        early_rx.at[pl.ds(early_start, early_rows), :], 6,
    )
    early_pair.start()
    send_back(1, part_one, g_pair_one)
    early_out()
    back = spread(1, g_pair_one, lambda: dot(w_self, g_low[...]))
    norm_backward(0, back)
    g_zero = g_low[...]
    dws = dot(xs[:, own_cols], g_zero, 1, 1)
    dwn = dot(agg_zero[...], g_zero, 1, 1)
    for c in range(2):
        start = c * FEAT_PAD
        grads[c, 0:fin, :] = dws[start : start + fin]
        grads[c, fin : 2 * fin, :] = dwn[start : start + fin]

    low_rows = pl.ds(0, round_up(shard * (first_early - 1) // HID + win, 8))
    top_rows = pl.ds(top_start, 8)
    late_pairs = [
        pair_copy(grads.at[other, rows, :], late_rx.at[rows, :], k)
        for rows, k in ((low_rows, 12), (top_rows, 13))
    ]
    for copy in late_pairs:
        copy.start()
    for copy in late_pairs:
        copy.wait_recv()
    stage_one(range(first_early), late_rx, two_parts)
    norms = grads[f, top_rows, :] + late_rx[top_rows, :]
    top_tx[0] = norms

    @pl.when(low == group - 1)
    def _():
        top_one[low] = norms

    @pl.when(low != group - 1)
    def _():
        top_copy(0, top_one.at[low], high * group + group - 1).start()

    stage_two(range(first_early, n_dom), whole_window)
    stage_two(range(first_early), two_parts)

    @pl.when(low == group - 1)
    def _():
        part = pl.ds(0, group - 1)
        pltpu.make_async_copy(top_one.at[part], top_one.at[part], top_recv.at[0]).wait()
        norms = jnp.sum(top_one[...], axis=0)
        top_tx[1] = norms

        @pl.when(high == n_high - 1)
        def _():
            top_two[high] = norms

        @pl.when(high != n_high - 1)
        def _():
            top_copy(1, top_two.at[high], n_dom - 1).start()

    part = pl.ds(0, n_high - 1)
    pltpu.make_async_copy(two_rx.at[part], two_rx.at[part], two_recv).wait()

    @pl.when(me == n_dom - 1)
    def _():
        pltpu.make_async_copy(top_two.at[part], top_two.at[part], top_recv.at[1]).wait()
        norms = jnp.sum(top_two[...], axis=0)
        first = norm_first - shard * (n_dom - 1) // HID
        norms = norms[norm_first - top_start : norm_first - top_start + 2]
        two_rx[0, first : first + 2, :] += norms[:, :LANES]
        two_rx[0, win + first : win + first + 2, :] += norms[:, LANES:]

    flat_t[...] = jnp.sum(two_rx[...], axis=0)
    scalar_out[0:1, :] = jnp.broadcast_to(flat_t[win - 1 : win, 0:1], (1, LANES))
    scalar_out[1:2, :] = jnp.broadcast_to(label_count, (1, LANES))
    shares[...] = from_window(jnp.concatenate([flat_t[:win, :], flat_t[win:, :]], axis=1))
    for k in range(-(-shard // LANES)):
        width = min(LANES, shard - k * LANES)
        grad_out[0:1, k * LANES : k * LANES + width] = shares[k : k + 1, 0:width]

    for copy in (
        x_pair, *h_pairs[0], *h_pairs[1], g_pair_two, g_pair_one,
        *par_rest, *late_pairs,
    ):
        copy.wait_send()
    for k in range(3, 5):
        wait_halo_sent(k)
    pltpu.make_async_copy(two_tx.at[part], two_tx.at[part], two_send).wait()
    @pl.when(low != group - 1)
    def _():
        pltpu.make_async_copy(top_tx.at[0], top_tx.at[0], top_send.at[0]).wait()

    @pl.when((low == group - 1) & (high != n_high - 1))
    def _():
        pltpu.make_async_copy(top_tx.at[1], top_tx.at[1], top_send.at[1]).wait()

    part = pl.ds(0, n_dom - n_high)
    pltpu.make_async_copy(one_tx.at[part], one_tx.at[part], one_send).wait()
    n_sent = n_high - 1 + len(urgent) * (2 * group - 1) + len(patient) * (group - 1)
    while n_sent > 0:
        part = pl.ds(0, min(n_sent, n_dom) * par_rows)
        pltpu.make_async_copy(par_rx.at[f, part, :], par_rx.at[f, part, :], par_send).wait()
        n_sent -= n_dom

    @pl.when(me == n_dom - 1)
    def _():
        for step in range(1, n_high):
            pltpu.make_async_copy(norm_own, norm_own, norm_send.at[0]).wait()

    @pl.when(last_low)
    def _():
        for step in range(2 * group - 1):
            pltpu.make_async_copy(norm_own, norm_own, norm_send.at[1]).wait()


def round_up(value, step):
    return -(-value // step) * step


def per_device(n_dom, features, local_mask, halo_mask, send_rows, labels, label_mask, master, first, second):
    nodes, halo = local_mask.shape[1], halo_mask.shape[1]
    half, shard, fin = nodes // 2, master.shape[1], features.shape[1]
    rows_all = n_dom * shard // HID
    span = (shard + HID - 2) // HID + 1
    win = round_up(span + 1, 4)
    par_rows = round_up(span, 16)
    grad_rows = round_up(rows_all + win, 8)
    group = 1
    while (2 * group) ** 2 <= n_dom:
        group *= 2
    head_end = 2 * fin + 2 * HALF_HID + HEAD_ROWS
    first_early = -(-2 * fin * HID // shard)
    assert shard * (n_dom - 1) <= (rows_all - 2) * HID and rows_all % 8 > 2
    urgent = sorted({d // group for d in range(first_early)})
    cfg = dict(
        group=group, first_early=first_early, urgent=urgent,
        n_dom=n_dom, nodes=nodes, half=half, halo=halo, shard=shard, fin=fin, win=win,
        par_rows=par_rows, rows_all=rows_all, grad_rows=grad_rows,
        h_rows=nodes if halo <= 256 else LANES, slots=half // LANES if halo <= 256 else 2,
    )
    hbm = pl.BlockSpec(memory_space=pl.ANY)
    vmem = pl.BlockSpec(memory_space=pltpu.VMEM)
    i32 = jnp.int32
    pad = LANES if halo <= 256 else 0
    scratch = [
        pltpu.VMEM((8, n_dom), i32),
        pltpu.VMEM((1, nodes), i32),
        pltpu.VMEM((1, nodes), i32),
        pltpu.VMEM((1, shard), F32),
        pltpu.VMEM((2 * win, LANES), F32),
        pltpu.VMEM((cfg["slots"], LANES, nodes), i32),
        pltpu.VMEM((cfg["slots"], LANES, half), i32),
        pltpu.VMEM((cfg["h_rows"], halo), i32),
        pltpu.VMEM((fin, nodes), BF),
        pltpu.VMEM((half + halo, nodes), BF),
        pltpu.VMEM((half, half), BF),
        pltpu.VMEM((halo, nodes), BF),
        pltpu.VMEM((halo, nodes), BF),
        pltpu.VMEM((2 * FEAT_PAD, nodes), BF),
        pltpu.VMEM((2, HID, nodes), BF),
        pltpu.VMEM((2, HID, nodes), BF),
        pltpu.VMEM((2, HID, half), BF),
        pltpu.VMEM((LANES, half), BF),
        pltpu.VMEM((halo, nodes), BF),
        pltpu.VMEM((halo, halo), BF),
        pltpu.VMEM((LANES, halo), BF),
        pltpu.VMEM((2, HID, halo), BF),
        pltpu.VMEM((8, halo), F32),
        pltpu.VMEM((halo, HID), F32),
        pltpu.VMEM((2, halo, HID), F32),
        pltpu.VMEM((HID, half + max(halo, half) + pad), F32),
        pltpu.VMEM((2, HID, half + pad), F32),
        pltpu.VMEM((2, HID, half + pad), F32),
        pltpu.VMEM((2, 8, half), F32),
        pltpu.VMEM((8, half), F32),
        pltpu.VMEM((2, n_dom, 16, LANES), BF),
        pltpu.VMEM((5, n_dom, 16, LANES), BF),
        pltpu.VMEM((2 * win, LANES), F32),
        pltpu.VMEM((par_rows, HID), BF),
        pltpu.VMEM((2, n_dom * par_rows, HID), BF),
        pltpu.VMEM((2, 16, HID), BF),
        pltpu.VMEM((2, HID, HID), BF),
        pltpu.VMEM((2, HID, HID), BF),
        pltpu.VMEM((HID, 8), F32),
        pltpu.VMEM((HID, LANES), BF),
        pltpu.VMEM((HID, LANES), BF),
        pltpu.VMEM((CLS_PAD, HID), BF),
        pltpu.VMEM((CLS_PAD, HID), BF),
        pltpu.VMEM((HID, half), BF),
        pltpu.VMEM((2, grad_rows, HID), F32),
        pltpu.VMEM((grad_rows, HID), F32),
        pltpu.VMEM((grad_rows, HID), F32),
        pltpu.VMEM((n_dom, 2 * win, LANES), F32),
        pltpu.VMEM((n_dom // group, group, 2 * win, LANES), F32),
        pltpu.VMEM((n_dom // group, 2 * win, LANES), F32),
        pltpu.VMEM((n_dom // group, 2 * win, LANES), F32),
        pltpu.VMEM((2, 8, HID), F32),
        pltpu.VMEM((group, 8, HID), F32),
        pltpu.VMEM((n_dom // group, 8, HID), F32),
        pltpu.VMEM((HID, LANES), F32),
        pltpu.VMEM((HID, LANES), F32),
        pltpu.VMEM((HID, LANES), F32),
        pltpu.VMEM((ROW_NORM, n_dom * par_rows), BF),
        pltpu.SemaphoreType.DMA((8 + 2 * cfg["slots"],)),
        pltpu.SemaphoreType.DMA((24,)),
        pltpu.SemaphoreType.DMA((24,)),
        pltpu.SemaphoreType.DMA((5,)),
        pltpu.SemaphoreType.DMA((5,)),
        pltpu.SemaphoreType.DMA,
        pltpu.SemaphoreType.DMA((n_dom // group,)),
        pltpu.SemaphoreType.DMA((n_dom // group,)),
        pltpu.SemaphoreType.DMA((2,)),
        pltpu.SemaphoreType.DMA((2,)),
        pltpu.SemaphoreType.DMA,
        pltpu.SemaphoreType.DMA((2, n_dom // group)),
        pltpu.SemaphoreType.DMA,
        pltpu.SemaphoreType.DMA,
        pltpu.SemaphoreType.DMA((2,)),
        pltpu.SemaphoreType.DMA((2,)),
    ]
    grad, scalars = pl.pallas_call(
        functools.partial(kernel, cfg),
        out_shape=(
            jax.ShapeDtypeStruct((1, shard), F32),
            jax.ShapeDtypeStruct((2, LANES), F32),
        ),
        in_specs=[hbm] * 7,
        out_specs=(vmem, vmem),
        scratch_shapes=scratch,
        compiler_params=pltpu.CompilerParams(
            collective_id=0, has_side_effects=True, vmem_limit_bytes=63 * 2**20
        ),
    )(
        features.T,
        local_mask,
        halo_mask,
        send_rows[0].T,
        labels.reshape(1, nodes),
        label_mask.reshape(1, nodes),
        master,
    )
    def finish(grad_ref, scalar_ref, master_ref, first_ref, second_ref, *outs):
        loss_out, count_out, master_out, first_out, second_out = outs
        own_grad = grad_ref[...]
        new_first = DECAY_ONE * first_ref[...] + (1.0 - DECAY_ONE) * own_grad
        new_second = DECAY_TWO * second_ref[...] + (1.0 - DECAY_TWO) * own_grad * own_grad
        first_hat = new_first / (1.0 - DECAY_ONE**STEP)
        second_hat = new_second / (1.0 - DECAY_TWO**STEP)
        old = master_ref[...]
        master_out[...] = old - LEARN_RATE * (
            first_hat / (jnp.sqrt(second_hat) + ADAM_EPS) + WEIGHT_DECAY * old
        )
        first_out[...] = new_first
        second_out[...] = new_second
        loss_out[...] = scalar_ref[0:1, 0:1]
        count_out[...] = scalar_ref[1:2, 0:1]

    one, own_shape = jax.ShapeDtypeStruct((1, 1), F32), jax.ShapeDtypeStruct((1, shard), F32)
    loss, count, *updated = pl.pallas_call(
        finish, out_shape=(one, one, own_shape, own_shape, own_shape),
        in_specs=[vmem] * 5, out_specs=(vmem,) * 5,
    )(grad, scalars, master, first, second)
    return (loss[0, 0], count[0, 0], *updated)


def solution(mesh):
    in_specs = (
        P("dom", "feat"),
        P("dom", None),
        P("dom", None),
        P("dom", None, None),
        P("dom"),
        P("dom"),
        P("feat", "dom"),
        P("feat", "dom"),
        P("feat", "dom"),
    )
    out_specs = (P(), P(), P("feat", "dom"), P("feat", "dom"), P("feat", "dom"))
    return jax.shard_map(
        functools.partial(per_device, mesh.shape["dom"]),
        mesh=mesh, in_specs=in_specs, out_specs=out_specs, check_vma=False,
    )
```
